32 devices in a mesh: fsdp: 8 (over y, x, core), tensor: 4 (over z).
Axes of the slice: x: 2, y: 2, z: 4, core: 2. Of those that a mesh axis runs over, the one named last changes fastest.
Arguments:
- layer_input: bfloat16 [16384, 2048], P(('fsdp', 'tensor')), may hold values from -6 to 6
- query_weight: bfloat16 [2048, 2048], P('fsdp', 'tensor'), as said below
- key_weight: bfloat16 [2048, 2048], P('fsdp', 'tensor'), as said below
- value_weight: bfloat16 [2048, 2048], P('fsdp', 'tensor'), may hold values from -0.125 to 0.125
- out_weight: bfloat16 [2048, 2048], P('tensor', 'fsdp'), may hold values from -0.125 to 0.125
- gate_weight: bfloat16 [2048, 8192], P('fsdp', 'tensor'), may hold values from -0.125 to 0.125
- up_weight: bfloat16 [2048, 8192], P('fsdp', 'tensor'), may hold values from -0.125 to 0.125
- down_weight: bfloat16 [8192, 2048], P('tensor', 'fsdp'), may hold values from -0.0625 to 0.0625
- query_gain: float32 [2048], replicated, may hold values from 0.25 to 1.75
- key_gain: float32 [2048], replicated, may hold values from 0.25 to 1.75
- attn_gain: float32 [2048], replicated, may hold values from 0.25 to 1.75
- ffn_gain: float32 [2048], replicated, may hold values from 0.25 to 1.75
- out_cotangent: bfloat16 [16384, 2048], P(('fsdp', 'tensor')), may hold values from -6 to 6
Outputs:
- layer_output: bfloat16 [16384, 2048], P(('fsdp', 'tensor'))
- input_grad: float32 [16384, 2048], P(('fsdp', 'tensor'))
- query_weight_grad: float32 [2048, 2048], P('fsdp', 'tensor')
- key_weight_grad: float32 [2048, 2048], P('fsdp', 'tensor')
- value_weight_grad: float32 [2048, 2048], P('fsdp', 'tensor')
- out_weight_grad: float32 [2048, 2048], P('tensor', 'fsdp')
- gate_weight_grad: float32 [2048, 8192], P('fsdp', 'tensor')
- up_weight_grad: float32 [2048, 8192], P('fsdp', 'tensor')
- down_weight_grad: float32 [8192, 2048], P('tensor', 'fsdp')
- query_gain_grad: float32 [2048], replicated
- key_gain_grad: float32 [2048], replicated
- attn_gain_grad: float32 [2048], replicated
- ffn_gain_grad: float32 [2048], replicated
The draws below stay inside these ranges and needn't reach their ends.
Inputs may be any that keep to these rules, and one draw needn't show every extreme that they name: `query_weight`: entries have magnitude under 17 / sqrt(2048). `key_weight`: entries have magnitude under 17 / sqrt(2048).
All inputs are finite; a program needn't handle non-finite values.
Results may differ from the reference program's by a relative error of at most 0.02.
Values may be sent and summed in bfloat16 or wider, within the bound.
A program may use at most 384 MiB of HBM per device.

```python
import math
import jax
import jax.numpy as jnp
from jax import lax

D = 2048
HEADS = 16
HEAD_DIM = 128
FF = 8192
SEQ_LEN = 1024
TOKENS = 16384


def column_weight(key, fan_rows, fan_cols, spread):
    normals = jax.random.truncated_normal(key, -6.0, 6.0, (fan_rows, fan_cols), jnp.float32)
    jitter = jax.random.uniform(jax.random.fold_in(key, 7), (1, fan_cols), jnp.float32, 0.8, 1.2)
    position = jnp.arange(fan_cols, dtype=jnp.float32)[None, :] / (fan_cols - 1)
    factor = spread ** (position - 0.5)
    return normals * jitter * factor / math.sqrt(fan_rows)


def draw_query_weight(key, part):
    key = jax.random.fold_in(key, 1)
    return column_weight(key, D, D, 3.0).astype(jnp.bfloat16)


def draw_key_weight(key, part):
    key = jax.random.fold_in(key, 2)
    return column_weight(key, D, D, 3.0).astype(jnp.bfloat16)


def level_of(rng, shape, shards, low, top_value):
    factor_of, own = 1.0, jax.random.fold_in(rng, 6)
    for dim, blocks in shards:
        steps = jnp.exp(jax.random.uniform(jax.random.fold_in(own, dim), (blocks,), jnp.float32, low / len(shards), top_value / len(shards)))
        factor_of = factor_of * jnp.repeat(steps, shape[dim] // blocks).reshape([-1 if axis == dim else 1 for axis in range(len(shape))])
    return factor_of


def gaussian(key, extent, deviation, most, shards=(), kind=jnp.bfloat16):
    result = deviation * jax.random.normal(key, extent, jnp.float32)
    if shards:
        result = result * level_of(key, extent, shards, -0.22, 0.18)
    return jnp.clip(result, -most, most).astype(kind)


def setup_inputs(seed: int = 0) -> dict:
    key_of = jax.random.split(jax.random.key(seed), 14)
    return {
        "layer_input": gaussian(key_of[0], (TOKENS, D), 1.0, 6.0, ((0, 32),)),
        "query_weight": draw_query_weight(jax.random.fold_in(key_of[13], 71), 0),
        "key_weight": draw_key_weight(jax.random.fold_in(key_of[13], 71), 0),
        "value_weight": gaussian(key_of[3], (D, D), D ** -0.5, 0.125, ((0, 8), (1, 4))),
        "out_weight": gaussian(key_of[4], (D, D), D ** -0.5, 0.125, ((0, 4), (1, 8))),
        "gate_weight": gaussian(key_of[5], (D, FF), D ** -0.5, 0.125, ((0, 8), (1, 4))),
        "up_weight": gaussian(key_of[6], (D, FF), D ** -0.5, 0.125, ((0, 8), (1, 4))),
        "down_weight": gaussian(key_of[7], (FF, D), FF ** -0.5, 0.0625, ((0, 4), (1, 8))),
        "query_gain": jnp.clip(1.0 + 0.15 * jax.random.normal(key_of[8], (D,), jnp.float32), 0.25, 1.75),
        "key_gain": jnp.clip(1.0 + 0.15 * jax.random.normal(key_of[9], (D,), jnp.float32), 0.25, 1.75),
        "attn_gain": jnp.clip(1.0 + 0.15 * jax.random.normal(key_of[10], (D,), jnp.float32), 0.25, 1.75),
        "ffn_gain": jnp.clip(1.0 + 0.15 * jax.random.normal(key_of[11], (D,), jnp.float32), 0.25, 1.75),
        "out_cotangent": gaussian(key_of[12], (TOKENS, D), 1.0, 6.0, ((0, 32),)),
    }


@jax.custom_vjp
def low(v):
    return lax.optimization_barrier(v.astype(jnp.bfloat16)).astype(jnp.float32)

@jax.custom_vjp
def low_back(v):
    return v

def low_keep(v):
    return (low(v), None)

def low_pass(kept, grad):
    return (grad,)

def back_keep(v):
    return (v, None)

def back_low(kept, grad):
    return (low(grad),)
low.defvjp(low_keep, low_pass)
low_back.defvjp(back_keep, back_low)
EPSILON = 1e-06
THETA = 500000.0

def matmul(left, right):
    return jnp.dot(left, right, precision=lax.Precision.HIGHEST, preferred_element_type=jnp.float32)

def rms_scale(values):
    return lax.rsqrt(lax.optimization_barrier(jnp.mean(values * values, axis=-1, keepdims=True)) + EPSILON)

def rotary_tables(count):
    position = (jnp.arange(count) % SEQ_LEN).astype(jnp.float32)
    inverse = THETA ** (-jnp.arange(0, HEAD_DIM, 2).astype(jnp.float32) / HEAD_DIM)
    angles = position[:, None] * inverse[None, :]
    angles = jnp.concatenate([angles, angles], axis=-1)
    return (jnp.cos(angles), jnp.sin(angles))

def rotate(values, cos_table, sin_table):
    half_dim = HEAD_DIM // 2
    turned = jnp.concatenate([-values[..., half_dim:], values[..., :half_dim]], axis=-1)
    return values * cos_table[:, None, :] + turned * sin_table[:, None, :]

def attend_sequence(packed):
    query_seq, key_seq, value_seq = packed
    scores = jnp.einsum('qhd,khd->hqk', query_seq, key_seq, precision=lax.Precision.HIGHEST)
    scores = low_back(scores) * (1.0 / math.sqrt(HEAD_DIM))
    causal = jnp.arange(SEQ_LEN)[:, None] >= jnp.arange(SEQ_LEN)[None, :]
    scores = jnp.where(causal[None], scores, -1e+30)
    top_score = lax.optimization_barrier(jnp.max(scores, axis=-1, keepdims=True))
    exps = jnp.exp(scores - top_score)
    weights = low(exps / lax.optimization_barrier(jnp.sum(exps, axis=-1, keepdims=True)))
    return jnp.einsum('hqk,khd->qhd', weights, value_seq, precision=lax.Precision.HIGHEST)

def by_sequence(values, count):
    return values.reshape(count // SEQ_LEN, SEQ_LEN, HEADS, HEAD_DIM)

def layer(inputs, query_w, key_w, value_w, out_w, gate_w, up_w, down_w, query_g, key_g, attn_g, ffn_g):
    count = inputs.shape[0]
    query_pre = low_back(matmul(inputs, query_w))
    key_pre = low_back(matmul(inputs, key_w))
    query_hat = query_pre * rms_scale(query_pre)
    key_hat = key_pre * rms_scale(key_pre)
    cos_table, sin_table = rotary_tables(count)
    query_rot = low(rotate((query_hat * query_g).reshape(count, HEADS, HEAD_DIM), cos_table, sin_table))
    key_rot = low(rotate((key_hat * key_g).reshape(count, HEADS, HEAD_DIM), cos_table, sin_table))
    value_low = low(low_back(matmul(inputs, value_w)))
    attended = lax.map(jax.checkpoint(attend_sequence), (by_sequence(query_rot, count), by_sequence(key_rot, count), by_sequence(value_low, count)))
    attended = low(low_back(attended.reshape(count, D)))
    branch = low_back(matmul(attended, out_w))
    middle = inputs + branch * rms_scale(branch) * attn_g
    mixed = low(middle)
    gate = low_back(matmul(mixed, gate_w))
    upper = low_back(matmul(mixed, up_w))
    hidden = low(jax.nn.silu(gate) * upper)
    second = low_back(matmul(hidden, down_w))
    return middle + second * rms_scale(second) * ffn_g

def reference(layer_input, query_weight, key_weight, value_weight, out_weight, gate_weight, up_weight, down_weight, query_gain, key_gain, attn_gain, ffn_gain, out_cotangent):
    floats = [arr.astype(jnp.float32) for arr in (layer_input, query_weight, key_weight, value_weight, out_weight, gate_weight, up_weight, down_weight, query_gain, key_gain, attn_gain, ffn_gain)]
    output, pullback = jax.vjp(layer, *floats)
    grads = pullback(out_cotangent.astype(jnp.float32))
    return (output.astype(jnp.bfloat16), grads[0], grads[1], grads[2], grads[3], grads[4], grads[5], grads[6], grads[7], grads[8], grads[9], grads[10], grads[11])
```

```python
import functools
import math

import jax
import jax.numpy as jnp
from jax import lax
from jax.experimental import pallas as pl
from jax.experimental.pallas import tpu as pltpu
from jax.sharding import PartitionSpec as P

HEAD_DIM = 128
SEQ_LEN = 1024
EPSILON = 1e-06
THETA = 500000.0
BLOCK = 256
LOW = jnp.bfloat16
F32 = jnp.float32


def nn(a, b):
    return lax.dot_general(a, b, (((1,), (0,)), ((), ())), preferred_element_type=F32)


def nt(a, b):
    return lax.dot_general(a, b, (((1,), (1,)), ((), ())), preferred_element_type=F32)


def tn(a, b):
    return lax.dot_general(a, b, (((0,), (0,)), ((), ())), preferred_element_type=F32)


def block_start(place, block, rows, parts):
    part = block * BLOCK // rows
    return pl.multiple_of(
        lax.rem(place + parts - part, parts) * rows + block * BLOCK % rows, BLOCK
    )


def masked(scores):
    row = lax.broadcasted_iota(jnp.int32, scores.shape, 0)
    col = lax.broadcasted_iota(jnp.int32, scores.shape, 1)
    return jnp.where(row + (scores.shape[1] - scores.shape[0]) >= col, scores, -1e30)


def attend_kernel(
    rows,
    parts,
    scale,
    place_ref,
    query_ref,
    key_ref,
    value_ref,
    query_inv_ref,
    key_inv_ref,
    query_gain_ref,
    key_gain_ref,
    cos_ref,
    sin_ref,
    out_ref,
    query_rot_ref,
    key_rot_ref,
    lse_ref,
    key_seq,
    value_seq,
):
    place = place_ref[0]
    half = HEAD_DIM // 2
    for block in range(SEQ_LEN // BLOCK):
        here = pl.ds(block_start(place, block, rows, parts), BLOCK)
        there = pl.ds(block * BLOCK, BLOCK)
        cos, sin = cos_ref[here], sin_ref[here]
        key = key_ref[here] * key_inv_ref[here] * key_gain_ref[...]
        key = (key * cos + pltpu.roll(key, half, 1) * sin).astype(LOW)
        key_rot_ref[here] = key
        key_seq[there] = key
        value_seq[there] = value_ref[here]
        query = query_ref[here] * query_inv_ref[here] * query_gain_ref[...]
        query = (query * cos + pltpu.roll(query, half, 1) * sin).astype(LOW)
        query_rot_ref[here] = query
        span = (block + 1) * BLOCK
        scores = masked(nt(query, key_seq[:span]) * scale)
        top = jnp.max(scores, axis=1, keepdims=True)
        exps = jnp.exp(scores - top)
        total = jnp.sum(exps, axis=1, keepdims=True)
        weights = (exps * (1.0 / total)).astype(LOW)
        out_ref[here] = nn(weights, value_seq[:span]).astype(LOW)
        lse_ref[here] = top + jnp.log(total)


def attend_back_kernel(
    rows,
    parts,
    scale,
    place_ref,
    query_rot_ref,
    key_rot_ref,
    value_ref,
    grad_ref,
    lse_ref,
    query_ref,
    key_ref,
    query_inv_ref,
    key_inv_ref,
    query_gain_ref,
    key_gain_ref,
    cos_ref,
    sin_ref,
    query_out_ref,
    key_out_ref,
    value_out_ref,
    query_gain_out_ref,
    key_gain_out_ref,
    query_inner_ref,
    key_inner_ref,
    key_seq,
    value_seq,
    key_acc,
    value_acc,
):
    place = place_ref[0]
    half = HEAD_DIM // 2
    count = SEQ_LEN // BLOCK

    @pl.when(pl.program_id(0) == 0)
    def _():
        query_inner_ref[...] = jnp.zeros_like(query_inner_ref)
        key_inner_ref[...] = jnp.zeros_like(key_inner_ref)

    def finish(grad, here, values_ref, inv_ref, gain_ref, out_ref, inner_ref):
        back = grad * cos_ref[here] - pltpu.roll(grad, half, 1) * sin_ref[here]
        hat = values_ref[here] * inv_ref[here]
        gained = back * gain_ref[...]
        out_ref[here] = gained
        inner_ref[here] += jnp.sum(gained * hat, axis=1, keepdims=True)
        return jnp.sum(back * hat, axis=0, keepdims=True)

    query_gain_sum = jnp.zeros((1, HEAD_DIM), F32)
    for block in range(count):
        here = pl.ds(block_start(place, block, rows, parts), BLOCK)
        there = pl.ds(block * BLOCK, BLOCK)
        key_seq[there] = key_rot_ref[here]
        value_seq[there] = value_ref[here]
        query, grad = query_rot_ref[here], grad_ref[here]
        span = (block + 1) * BLOCK
        scores = masked(nt(query, key_seq[:span]) * scale)
        probs = jnp.exp(scores - lse_ref[here])
        weights = probs.astype(LOW)
        grad_probs = nt(grad, value_seq[:span])
        delta = jnp.sum(probs * grad_probs, axis=1, keepdims=True)
        grad_scores = (probs * (grad_probs - delta) * scale).astype(LOW)
        value_part = tn(weights, grad)
        key_part = tn(grad_scores, query)
        past = block * BLOCK
        if block:
            key_acc[:past] += key_part[:past]
            value_acc[:past] += value_part[:past]
        key_acc[past:span] = key_part[past:]
        value_acc[past:span] = value_part[past:]
        query_gain_sum += finish(
            nn(grad_scores, key_seq[:span]),
            here,
            query_ref,
            query_inv_ref,
            query_gain_ref,
            query_out_ref,
            query_inner_ref,
        )
    query_gain_out_ref[...] = query_gain_sum
    key_gain_sum = jnp.zeros((1, HEAD_DIM), F32)
    for block in range(count):
        here = pl.ds(block_start(place, block, rows, parts), BLOCK)
        there = pl.ds(block * BLOCK, BLOCK)
        value_out_ref[here] = value_acc[there].astype(LOW)
        key_gain_sum += finish(
            key_acc[there],
            here,
            key_ref,
            key_inv_ref,
            key_gain_ref,
            key_out_ref,
            key_inner_ref,
        )
    key_gain_out_ref[...] = key_gain_sum


def attention_specs(width):
    head = pl.BlockSpec((SEQ_LEN, HEAD_DIM), lambda i, place: (0, i))
    whole = pl.BlockSpec((SEQ_LEN, HEAD_DIM), lambda i, place: (0, 0))
    column = pl.BlockSpec((SEQ_LEN, 1), lambda i, place: (0, 0))
    gain = pl.BlockSpec((1, HEAD_DIM), lambda i, place: (0, i))
    lse = pl.BlockSpec((None, SEQ_LEN, 1), lambda i, place: (i, 0, 0))
    return head, whole, column, gain, lse


def attend(rows, parts, place, query, key, value, invs, gains, tables):
    width = query.shape[1]
    heads = width // HEAD_DIM
    head, whole, column, gain, lse = attention_specs(width)
    low = jax.ShapeDtypeStruct((SEQ_LEN, width), LOW)
    return pl.pallas_call(
        functools.partial(attend_kernel, rows, parts, 1.0 / math.sqrt(HEAD_DIM)),
        grid_spec=pltpu.PrefetchScalarGridSpec(
            num_scalar_prefetch=1,
            grid=(heads,),
            in_specs=[head, head, head, column, column, gain, gain, whole, whole],
            out_specs=[head, head, head, lse],
            scratch_shapes=[
                pltpu.VMEM((SEQ_LEN, HEAD_DIM), LOW),
                pltpu.VMEM((SEQ_LEN, HEAD_DIM), LOW),
            ],
        ),
        out_shape=[low, low, low, jax.ShapeDtypeStruct((heads, SEQ_LEN, 1), F32)],
        compiler_params=pltpu.CompilerParams(vmem_limit_bytes=40 * 2**20),
        cost_estimate=pl.CostEstimate(
            flops=8 * heads * SEQ_LEN * SEQ_LEN * HEAD_DIM,
            bytes_accessed=16 * SEQ_LEN * width,
            transcendentals=heads * SEQ_LEN * SEQ_LEN,
        ),
        name="attend",
    )(place, query, key, value, *invs, *gains, *tables)


def attend_back(rows, parts, place, rots, value, grad, lse_all, pres, invs, gains, tables):
    width = value.shape[1]
    heads = width // HEAD_DIM
    head, whole, column, gain, lse = attention_specs(width)
    full = jax.ShapeDtypeStruct((SEQ_LEN, width), F32)
    gain_out = jax.ShapeDtypeStruct((1, width), F32)
    inner = jax.ShapeDtypeStruct((SEQ_LEN, 1), F32)
    return pl.pallas_call(
        functools.partial(attend_back_kernel, rows, parts, 1.0 / math.sqrt(HEAD_DIM)),
        grid_spec=pltpu.PrefetchScalarGridSpec(
            num_scalar_prefetch=1,
            grid=(heads,),
            in_specs=[head, head, head, head, lse, head, head]
            + [column, column, gain, gain, whole, whole],
            out_specs=[head, head, head, gain, gain, column, column],
            scratch_shapes=[
                pltpu.VMEM((SEQ_LEN, HEAD_DIM), LOW),
                pltpu.VMEM((SEQ_LEN, HEAD_DIM), LOW),
                pltpu.VMEM((SEQ_LEN, HEAD_DIM), F32),
                pltpu.VMEM((SEQ_LEN, HEAD_DIM), F32),
            ],
        ),
        out_shape=[
            full,
            full,
            jax.ShapeDtypeStruct((SEQ_LEN, width), LOW),
            gain_out,
            gain_out,
            inner,
            inner,
        ],
        compiler_params=pltpu.CompilerParams(vmem_limit_bytes=48 * 2**20),
        cost_estimate=pl.CostEstimate(
            flops=20 * heads * SEQ_LEN * SEQ_LEN * HEAD_DIM,
            bytes_accessed=32 * SEQ_LEN * width,
            transcendentals=heads * SEQ_LEN * SEQ_LEN,
        ),
        name="attend_back",
    )(place, *rots, value, grad, lse_all, *pres, *invs, *gains, *tables)


def norm_back(grad_hat, values_hat, inverse, width):
    inner = jnp.sum(grad_hat * values_hat, axis=1, keepdims=True) / width
    return inverse * (grad_hat - values_hat * inner)


def layer(fsdp, tensor, *arguments):
    layer_input, query_weight, key_weight, value_weight, out_weight = arguments[:5]
    gate_weight, up_weight, down_weight = arguments[5:8]
    query_gain, key_gain, attn_gain, ffn_gain, out_cotangent = arguments[8:]
    rows_here, width = layer_input.shape
    head_cols = query_weight.shape[1]
    parts = SEQ_LEN // rows_here
    spans = tensor // parts
    fsdp_rank = lax.axis_index("fsdp")
    rank = lax.axis_index("tensor")
    place, span = rank % parts, rank // parts
    core = fsdp_rank % 2

    def to_part(x, shift):
        pairs = [
            (s * parts + p, s * parts + (p + shift) % parts)
            for s in range(spans)
            for p in range(parts)
        ]
        return lax.ppermute(x, "tensor", pairs)

    def to_span(x, shift):
        pairs = [
            (s * parts + p, (s + shift) % spans * parts + p)
            for s in range(spans)
            for p in range(parts)
        ]
        return lax.ppermute(x, "tensor", pairs)

    def to_other_core(x):
        return lax.ppermute(x, "fsdp", [(f, f ^ 1) for f in range(fsdp)])

    def gather_weight(shard):
        wide = [shard] + [to_span(shard, s) for s in range(1, spans)]
        return lax.all_gather(jnp.concatenate(wide, axis=1), "fsdp", axis=0, tiled=True)

    def gather_rows(own):
        return jnp.concatenate([own] + [to_part(own, p) for p in range(1, parts)], axis=0)

    def scatter_rows(make):
        away = [
            to_part(make(slice(p * rows_here, (p + 1) * rows_here)).astype(LOW), -p)
            for p in range(1, parts)
        ]
        total = make(slice(0, rows_here))
        for piece in away:
            total = total + piece.astype(F32)
        return total

    def sum_parts(x):
        total = x
        for p in range(1, parts):
            total = total + jnp.roll(to_part(x, p), p * rows_here, axis=1)
        return total

    def core_halves(x):
        split = x.reshape(x.shape[0], fsdp // 2, 2, width // fsdp)
        return [
            lax.dynamic_index_in_dim(split, which, 2, keepdims=False).reshape(
                x.shape[0], width // 2
            )
            for which in (core, 1 - core)
        ]

    same_core = [list(range(c, fsdp, 2)) for c in range(2)]

    def weight_grad(halves, grads):
        mine, other = halves
        sent = to_other_core(tn(other, grads).astype(LOW))
        total = (tn(mine, grads) + sent.astype(F32)).astype(LOW)
        total = lax.psum_scatter(
            total, "fsdp", scatter_dimension=0, tiled=True, axis_index_groups=same_core
        )
        cols = total.shape[1] // spans
        result = total[:, :cols].astype(F32)
        for s in range(1, spans):
            result = result + to_span(total[:, s * cols : (s + 1) * cols], -s).astype(F32)
        return result

    def own_columns(s):
        return ((span + spans - s) % spans * parts + place) * head_cols

    def gain_here(gain):
        return jnp.concatenate(
            [lax.dynamic_slice_in_dim(gain, own_columns(s), head_cols) for s in range(spans)]
        )[None, :]

    def gain_whole(part):
        whole = jnp.zeros((width,), F32)
        for s in range(spans):
            whole = lax.dynamic_update_slice_in_dim(
                whole, part[0, s * head_cols : (s + 1) * head_cols], own_columns(s), 0
            )
        return whole

    inputs = gather_rows(layer_input)
    full_query = gather_weight(query_weight)
    full_key = gather_weight(key_weight)
    full_value = gather_weight(value_weight)
    full_out = gather_weight(out_weight.T)
    full_gate = gather_weight(gate_weight)
    full_up = gather_weight(up_weight)
    full_down = gather_weight(down_weight.T)

    local = jnp.arange(SEQ_LEN)
    position = (place + parts - local // rows_here) % parts * rows_here + local % rows_here
    inverse = THETA ** (-jnp.arange(0, HEAD_DIM, 2).astype(F32) / HEAD_DIM)
    angles = position.astype(F32)[:, None] * inverse[None, :]
    cos, sin = jnp.cos(angles), jnp.sin(angles)
    tables = (jnp.concatenate([cos, cos], axis=1), jnp.concatenate([-sin, sin], axis=1))
    gains = (gain_here(query_gain), gain_here(key_gain))
    place_arr = jnp.full((1,), place, jnp.int32)

    query_pre = nn(inputs, full_query)
    key_pre = nn(inputs, full_key)
    value_low = nn(inputs, full_value).astype(LOW)
    squares = jnp.stack(
        [jnp.sum(query_pre * query_pre, axis=1), jnp.sum(key_pre * key_pre, axis=1)]
    )
    invs = lax.rsqrt(sum_parts(squares) / width + EPSILON)
    invs = (invs[0][:, None], invs[1][:, None])
    attended, query_rot, key_rot, lse = attend(
        rows_here, parts, place_arr, query_pre, key_pre, value_low, invs, gains, tables
    )
    branch = scatter_rows(lambda part: nt(attended[part], full_out))
    branch_inv = lax.rsqrt(jnp.mean(branch * branch, axis=1, keepdims=True) + EPSILON)
    branch_hat = branch * branch_inv
    middle = layer_input.astype(F32) + branch_hat * attn_gain
    mixed = gather_rows(middle.astype(LOW))
    gate = nn(mixed, full_gate)
    upper = nn(mixed, full_up)
    hidden = (jax.nn.silu(gate) * upper).astype(LOW)
    second = scatter_rows(lambda part: nt(hidden[part], full_down))
    second_inv = lax.rsqrt(jnp.mean(second * second, axis=1, keepdims=True) + EPSILON)
    second_hat = second * second_inv
    output = (middle + second_hat * ffn_gain).astype(LOW)

    grad_out = out_cotangent.astype(F32)
    ffn_gain_part = jnp.sum(grad_out * second_hat, axis=0)
    grad_second = norm_back(grad_out * ffn_gain, second_hat, second_inv, width)
    grad_rows = gather_rows(grad_second.astype(LOW))
    grad_hidden = nn(grad_rows, full_down)
    down_grad = weight_grad(core_halves(grad_rows), hidden).T
    sigmoid = jax.nn.sigmoid(gate)
    grad_upper = (grad_hidden * gate * sigmoid).astype(LOW)
    grad_gate = (grad_hidden * upper * sigmoid * (1.0 + gate * (1.0 - sigmoid))).astype(LOW)
    mixed_halves = core_halves(mixed)
    gate_grad = weight_grad(mixed_halves, grad_gate)
    up_grad = weight_grad(mixed_halves, grad_upper)
    grad_mixed = scatter_rows(
        lambda part: nt(grad_gate[part], full_gate) + nt(grad_upper[part], full_up)
    )
    grad_middle = grad_out + grad_mixed
    attn_gain_part = jnp.sum(grad_middle * branch_hat, axis=0)
    grad_branch = norm_back(grad_middle * attn_gain, branch_hat, branch_inv, width)
    grad_branch_rows = gather_rows(grad_branch.astype(LOW))
    grad_attended = nn(grad_branch_rows, full_out).astype(LOW)
    out_grad = weight_grad(core_halves(grad_branch_rows), attended).T
    (
        query_gained,
        key_gained,
        grad_value,
        query_gain_part,
        key_gain_part,
        query_inner,
        key_inner,
    ) = attend_back(
        rows_here,
        parts,
        place_arr,
        (query_rot, key_rot),
        value_low,
        grad_attended,
        lse,
        (query_pre, key_pre),
        invs,
        gains,
        tables,
    )
    inners = sum_parts(jnp.concatenate([query_inner, key_inner], axis=1).T).T / width
    grad_query = (
        invs[0] * (query_gained - query_pre * invs[0] * inners[:, :1])
    ).astype(LOW)
    grad_key = (invs[1] * (key_gained - key_pre * invs[1] * inners[:, 1:])).astype(LOW)
    input_grad = grad_middle + scatter_rows(
        lambda part: nt(grad_query[part], full_query)
        + nt(grad_key[part], full_key)
        + nt(grad_value[part], full_value)
    )
    input_halves = core_halves(inputs)
    value_grad = weight_grad(input_halves, grad_value)
    query_grad = weight_grad(input_halves, grad_query)
    key_grad = weight_grad(input_halves, grad_key)
    gain_grads = lax.psum(
        (gain_whole(query_gain_part), gain_whole(key_gain_part), attn_gain_part, ffn_gain_part),
        ("fsdp", "tensor"),
    )
    return (
        output,
        input_grad,
        query_grad,
        key_grad,
        value_grad,
        out_grad,
        gate_grad,
        up_grad,
        down_grad,
        *gain_grads,
    )


def solution(mesh):
    columns, rows = P("fsdp", "tensor"), P("tensor", "fsdp")
    tokens = P(("fsdp", "tensor"), None)
    weights = (columns, columns, columns, rows, columns, columns, rows)
    return jax.shard_map(
        functools.partial(layer, mesh.shape["fsdp"], mesh.shape["tensor"]),
        mesh=mesh,
        in_specs=(tokens, *weights, P(), P(), P(), P(), tokens),
        out_specs=(tokens, tokens, *weights, P(), P(), P(), P()),
        check_vma=False,
    )
```

```python
import functools
import math

import jax
import jax.numpy as jnp
from jax import lax
from jax.experimental import pallas as pl
from jax.experimental.pallas import tpu as pltpu
from jax.sharding import PartitionSpec as P

HEAD_DIM = 128
SEQ_LEN = 1024
EPSILON = 1e-06
THETA = 500000.0
BLOCK = 256
LOW = jnp.bfloat16
F32 = jnp.float32


def nn(a, b):
    return lax.dot_general(a, b, (((1,), (0,)), ((), ())), preferred_element_type=F32)


def nt(a, b):
    return lax.dot_general(a, b, (((1,), (1,)), ((), ())), preferred_element_type=F32)


def tn(a, b):
    return lax.dot_general(a, b, (((0,), (0,)), ((), ())), preferred_element_type=F32)


def after(x, *earlier):
    return lax.optimization_barrier((x, *earlier))[0]


def block_start(place, block, rows, parts):
    part = block * BLOCK // rows
    return pl.multiple_of(
        lax.rem(place + parts - part, parts) * rows + block * BLOCK % rows, BLOCK
    )


def masked(scores):
    row = lax.broadcasted_iota(jnp.int32, scores.shape, 0)
    col = lax.broadcasted_iota(jnp.int32, scores.shape, 1)
    return jnp.where(row + (scores.shape[1] - scores.shape[0]) >= col, scores, -1e30)


def attend_kernel(
    rows,
    parts,
    scale,
    place_ref,
    query_ref,
    key_ref,
    value_ref,
    query_inv_ref,
    key_inv_ref,
    query_gain_ref,
    key_gain_ref,
    cos_ref,
    sin_ref,
    out_ref,
    query_rot_ref,
    key_rot_ref,
    lse_ref,
    key_seq,
    value_seq,
):
    place = place_ref[0]
    half = HEAD_DIM // 2
    for block in range(SEQ_LEN // BLOCK):
        here = pl.ds(block_start(place, block, rows, parts), BLOCK)
        there = pl.ds(block * BLOCK, BLOCK)
        cos, sin = cos_ref[here], sin_ref[here]
        key = key_ref[here] * key_inv_ref[here] * key_gain_ref[...]
        key = (key * cos + pltpu.roll(key, half, 1) * sin).astype(LOW)
        key_rot_ref[here] = key
        key_seq[there] = key
        value_seq[there] = value_ref[here]
        query = query_ref[here] * query_inv_ref[here] * query_gain_ref[...]
        query = (query * cos + pltpu.roll(query, half, 1) * sin).astype(LOW)
        query_rot_ref[here] = query
        span = (block + 1) * BLOCK
        scores = masked(nt(query, key_seq[:span]) * scale)
        top = jnp.max(scores, axis=1, keepdims=True)
        exps = jnp.exp(scores - top)
        total = jnp.sum(exps, axis=1, keepdims=True)
        weights = (exps * (1.0 / total)).astype(LOW)
        out_ref[here] = nn(weights, value_seq[:span]).astype(LOW)
        lse_ref[here] = top + jnp.log(total)


def attend_back_kernel(
    rows,
    parts,
    scale,
    place_ref,
    query_rot_ref,
    key_rot_ref,
    value_ref,
    grad_ref,
    lse_ref,
    query_ref,
    key_ref,
    query_inv_ref,
    key_inv_ref,
    query_gain_ref,
    key_gain_ref,
    cos_ref,
    sin_ref,
    query_out_ref,
    key_out_ref,
    value_out_ref,
    query_gain_out_ref,
    key_gain_out_ref,
    query_inner_ref,
    key_inner_ref,
    key_seq,
    value_seq,
    key_acc,
    value_acc,
):
    place = place_ref[0]
    half = HEAD_DIM // 2
    count = SEQ_LEN // BLOCK

    @pl.when(pl.program_id(0) == 0)
    def _():
        query_inner_ref[...] = jnp.zeros_like(query_inner_ref)
        key_inner_ref[...] = jnp.zeros_like(key_inner_ref)

    def finish(grad, here, values_ref, inv_ref, gain_ref, out_ref, inner_ref):
        back = grad * cos_ref[here] - pltpu.roll(grad, half, 1) * sin_ref[here]
        hat = values_ref[here] * inv_ref[here]
        gained = back * gain_ref[...]
        out_ref[here] = gained
        inner_ref[here] += jnp.sum(gained * hat, axis=1, keepdims=True)
        return jnp.sum(back * hat, axis=0, keepdims=True)

    query_gain_sum = jnp.zeros((1, HEAD_DIM), F32)
    for block in range(count):
        here = pl.ds(block_start(place, block, rows, parts), BLOCK)
        there = pl.ds(block * BLOCK, BLOCK)
        key_seq[there] = key_rot_ref[here]
        value_seq[there] = value_ref[here]
        query, grad = query_rot_ref[here], grad_ref[here]
        span = (block + 1) * BLOCK
        scores = masked(nt(query, key_seq[:span]) * scale)
        probs = jnp.exp(scores - lse_ref[here])
        weights = probs.astype(LOW)
        grad_probs = nt(grad, value_seq[:span])
        delta = jnp.sum(probs * grad_probs, axis=1, keepdims=True)
        grad_scores = (probs * (grad_probs - delta) * scale).astype(LOW)
        value_part = tn(weights, grad)
        key_part = tn(grad_scores, query)
        past = block * BLOCK
        if block:
            key_acc[:past] += key_part[:past]
            value_acc[:past] += value_part[:past]
        key_acc[past:span] = key_part[past:]
        value_acc[past:span] = value_part[past:]
        query_gain_sum += finish(
            nn(grad_scores, key_seq[:span]),
            here,
            query_ref,
            query_inv_ref,
            query_gain_ref,
            query_out_ref,
            query_inner_ref,
        )
    query_gain_out_ref[...] = query_gain_sum
    key_gain_sum = jnp.zeros((1, HEAD_DIM), F32)
    for block in range(count):
        here = pl.ds(block_start(place, block, rows, parts), BLOCK)
        there = pl.ds(block * BLOCK, BLOCK)
        value_out_ref[here] = value_acc[there].astype(LOW)
        key_gain_sum += finish(
            key_acc[there],
            here,
            key_ref,
            key_inv_ref,
            key_gain_ref,
            key_out_ref,
            key_inner_ref,
        )
    key_gain_out_ref[...] = key_gain_sum


MESH = pl.DeviceIdType.MESH
MIB = 2**20


def flip(index, bit):
    return index + bit - 2 * bit * lax.rem(lax.div(index, bit), 2)


def row_shares(rows, count):
    units = rows // 16
    sizes = [16 * (units // count + (i < units % count)) for i in range(count)]
    starts = [sum(sizes[:i]) for i in range(count)]
    return list(zip(starts, sizes))


class Copies:
    def __init__(self, send_sems, recv_sems):
        self.send_sems, self.recv_sems = send_sems, recv_sems
        self.used = 0
        self.open = []

    def send(self, src, dst, **device):
        copy = pltpu.make_async_remote_copy(
            src_ref=src,
            dst_ref=dst,
            send_sem=self.send_sems.at[self.used],
            recv_sem=self.recv_sems.at[self.used],
            device_id=device,
            device_id_type=MESH,
        )
        self.used += 1
        copy.start()
        self.open.append(copy.wait_send)
        return copy

    def move(self, src, dst):
        copy = pltpu.make_async_copy(src, dst, self.send_sems.at[self.used])
        self.used += 1
        copy.start()
        self.open.append(copy.wait)

    def finish(self):
        for wait in self.open:
            wait()


def exchange_kernel(fsdp, parts, spans, plan, counts, *refs):
    rows_count, shard_count, send_count, full_count, _ = counts
    rows_refs, refs = refs[:rows_count], refs[rows_count:]
    shard_refs, refs = refs[:shard_count], refs[shard_count:]
    span_refs, refs = refs[:send_count], refs[send_count + counts[4] :]
    rows_outs, refs = refs[:rows_count], refs[rows_count:]
    full_refs, refs = refs[:full_count], refs[full_count:]
    span_outs = refs[:send_count]
    copies = Copies(*refs[-2:])
    me, rank = lax.axis_index("fsdp"), lax.axis_index("tensor")
    place, span = lax.rem(rank, parts), lax.div(rank, parts)
    bits = [1 << b for b in range(1, fsdp.bit_length() - 1)]
    part_ranks = [span * parts + lax.rem(place + p, parts) for p in range(1, parts)]
    span_ranks = [lax.rem(span + s, spans) * parts + place for s in range(1, spans)]
    partners = [{"fsdp": flip(me, bit)} for bit in [1, *bits]]
    if rows_count:
        partners += [{"tensor": r} for r in part_ranks]
    if send_count or any(s and not here for _, s, _, here in plan):
        partners += [{"tensor": r} for r in span_ranks]
    barrier = pltpu.get_barrier_semaphore()
    for partner in partners:
        pl.semaphore_signal(barrier, inc=1, device_id=partner, device_id_type=MESH)
    pl.semaphore_wait(barrier, len(partners))

    def slot(job, mask, share=None):
        group, s, position, _ = plan[job]
        which = me
        for bit in [1, *bits]:
            if mask & bit:
                which = flip(which, bit)
        cols = shard_refs[job].shape[1]
        ref = full_refs[group].at[which, :, pl.ds(position * cols, cols)]
        return ref if share is None else ref.at[pl.ds(*share)]

    depth = shard_refs[0].shape[0]
    shares = row_shares(depth, len(bits))
    jobs = range(len(plan))
    remote = [s and not here for _, s, _, here in plan]
    from_span = {
        job: copies.send(shard_refs[job], slot(job, 0), tensor=span_ranks[plan[job][1] - 1])
        for job in jobs
        if remote[job]
    }
    over = []
    for ref, out in zip(rows_refs, rows_outs):
        for p, r in enumerate(part_ranks):
            over.append(copies.send(ref, out.at[p + 1], tensor=r))
        copies.move(ref, out.at[0])
    for ref, out in zip(span_refs, span_outs):
        for s, r in enumerate(span_ranks):
            over.append(copies.send(ref, out.at[s], tensor=r))
    for job in jobs:
        if not remote[job]:
            copies.move(shard_refs[job], slot(job, 0))

    arriving = {}
    held = {(job, p): [0] for job in jobs for p in range(len(shares))}

    def source(job, mask, share):
        if mask == 0 and not remote[job]:
            return shard_refs[job].at[pl.ds(*share)]
        return slot(job, mask, share)

    def send_step(job, step):
        for p, share in enumerate(shares):
            bit = bits[(p + step) % len(bits)]
            for mask in held[job, p]:
                arriving[job, p, mask | bit] = copies.send(
                    source(job, mask, share), slot(job, mask, share), fsdp=flip(me, bit)
                )

    def take_step(job, step):
        for p in range(len(shares)):
            bit = bits[(p + step) % len(bits)]
            came = [mask | bit for mask in held[job, p]]
            for mask in came:
                arriving[job, p, mask].wait_recv()
            held[job, p] += came

    for step in range(len(bits) + 1):
        for job in jobs:
            if step == 0 and remote[job]:
                from_span[job].wait_recv()
            if step:
                take_step(job, step - 1)
            if step < len(bits):
                send_step(job, step)
            else:
                for mask in range(0, fsdp, 2):
                    whole = (0, depth)
                    over.append(
                        copies.send(
                            source(job, mask, whole), slot(job, mask), fsdp=flip(me, 1)
                        )
                    )
    for copy in over:
        copy.wait_recv()
    copies.finish()


def exchange(number, fsdp, parts, spans, shards, plan, rows=(), sends=(), earlier=()):
    bits = fsdp.bit_length() - 2
    depth = shards[0].shape[0]
    per_job = 2 + bits * (2**bits - 1) + 2**bits
    count = parts * len(rows) + len(plan) * per_job + len(sends) * spans
    hbm = pl.BlockSpec(memory_space=pl.ANY)
    full_count = 1 + max(group for group, *_ in plan)
    widths = [0] * full_count
    for shard, (group, *_) in zip(shards, plan):
        widths[group] += shard.shape[1]
    outs = [jax.ShapeDtypeStruct((parts, *r.shape), LOW) for r in rows]
    outs += [jax.ShapeDtypeStruct((fsdp, depth, width), LOW) for width in widths]
    outs += [jax.ShapeDtypeStruct((spans - 1, *x.shape), LOW) for x in sends]
    counts = (len(rows), len(shards), len(sends), full_count, len(earlier))
    inputs = (*rows, *shards, *sends, *earlier)
    results = pl.pallas_call(
        functools.partial(exchange_kernel, fsdp, parts, spans, plan, counts),
        out_shape=outs,
        in_specs=[hbm] * len(inputs),
        out_specs=[hbm] * len(outs),
        scratch_shapes=[
            pltpu.SemaphoreType.DMA((count,)),
            pltpu.SemaphoreType.DMA((count,)),
        ],
        compiler_params=pltpu.CompilerParams(collective_id=number, has_side_effects=True),
        name="exchange",
    )(*inputs)
    gathered = [r.reshape(-1, r.shape[2]) for r in results[: len(rows)]]
    full = [r.reshape(fsdp * depth, -1) for r in results[len(rows) : len(rows) + full_count]]
    return gathered, full, results[len(rows) + full_count :]


def sum_kernel(pairs, has_addend, *refs):
    out_ref = refs[-1]
    total = refs[-2][...].astype(F32) if has_addend else None
    for i in range(pairs):
        term = nt(refs[2 * i][...], refs[2 * i + 1][...])
        total = term if total is None else total + term
    out_ref[...] = total.astype(out_ref.dtype)


def product_sum(rows, block, pairs, kind, addend=None):
    width = pairs[0][1].shape[0]
    tile = min(512, width)
    specs, operands, flops = [], [], 0
    for a, b, run in pairs:
        depth = a.shape[1]
        specs.append(pl.BlockSpec((rows, depth), lambda j: (block, 0)))
        specs.append(pl.BlockSpec((tile, depth), lambda j, run=run: (j, run)))
        operands += [a, b]
        flops += 2 * rows * depth * width
    out = pl.BlockSpec((rows, tile), lambda j: (0, j))
    if addend is not None:
        specs.append(out)
        operands.append(addend)
    return pl.pallas_call(
        functools.partial(sum_kernel, len(pairs), addend is not None),
        grid=(width // tile,),
        in_specs=specs,
        out_specs=out,
        out_shape=jax.ShapeDtypeStruct((rows, width), kind),
        compiler_params=pltpu.CompilerParams(vmem_limit_bytes=56 * MIB),
        cost_estimate=pl.CostEstimate(
            flops=flops, bytes_accessed=flops // rows + 4 * rows * width, transcendentals=0
        ),
        name="product_sum",
    )(*operands)


def up_kernel(mixed_ref, gate_weight_ref, up_weight_ref, gate_ref, upper_ref, hidden_ref):
    gate = nn(mixed_ref[...], gate_weight_ref[...])
    upper = nn(mixed_ref[...], up_weight_ref[...])
    gate_ref[...] = gate
    upper_ref[...] = upper
    hidden_ref[...] = (gate * jax.nn.sigmoid(gate) * upper).astype(LOW)


def feed_up(mixed, gate_up):
    rows, depth = mixed.shape
    cols = gate_up.shape[1] // 2
    tile = min(256, cols)
    tiles = cols // tile
    out = pl.BlockSpec((rows, tile), lambda j: (0, j))
    return pl.pallas_call(
        up_kernel,
        grid=(tiles,),
        in_specs=[
            pl.BlockSpec((rows, depth), lambda j: (0, 0)),
            pl.BlockSpec((depth, tile), lambda j: (0, j)),
            pl.BlockSpec((depth, tile), lambda j: (0, j + tiles)),
        ],
        out_specs=[out, out, out],
        out_shape=[
            jax.ShapeDtypeStruct((rows, cols), F32),
            jax.ShapeDtypeStruct((rows, cols), F32),
            jax.ShapeDtypeStruct((rows, cols), LOW),
        ],
        compiler_params=pltpu.CompilerParams(vmem_limit_bytes=48 * MIB),
        cost_estimate=pl.CostEstimate(
            flops=4 * rows * depth * cols,
            bytes_accessed=4 * depth * cols + 10 * rows * cols,
            transcendentals=rows * cols,
        ),
        name="feed_up",
    )(mixed, gate_up, gate_up)


def up_back_kernel(grad_ref, down_ref, gate_ref, upper_ref, gate_out_ref, up_out_ref):
    grad = nn(grad_ref[...], down_ref[...])
    gate = gate_ref[...]
    sigmoid = jax.nn.sigmoid(gate)
    scaled = grad * sigmoid
    up_out_ref[...] = (scaled * gate).astype(LOW)
    gate_out_ref[...] = (scaled * upper_ref[...] * (1.0 + gate * (1.0 - sigmoid))).astype(LOW)


def feed_up_back(grad_rows, down, gate, upper):
    rows, depth = grad_rows.shape
    cols = down.shape[1]
    tile = min(512, cols)
    spec = pl.BlockSpec((rows, tile), lambda j: (0, j))
    out = jax.ShapeDtypeStruct((rows, cols), LOW)
    return pl.pallas_call(
        up_back_kernel,
        grid=(cols // tile,),
        in_specs=[
            pl.BlockSpec((rows, depth), lambda j: (0, 0)),
            pl.BlockSpec((depth, tile), lambda j: (0, j)),
            spec,
            spec,
        ],
        out_specs=[spec, spec],
        out_shape=[out, out],
        compiler_params=pltpu.CompilerParams(vmem_limit_bytes=52 * MIB),
        cost_estimate=pl.CostEstimate(
            flops=2 * rows * depth * cols,
            bytes_accessed=2 * depth * cols + 12 * rows * cols,
            transcendentals=rows * cols,
        ),
        name="feed_up_back",
    )(grad_rows, down, gate, upper)


def weight_grad_kernel(pieces, tiles, has_addend, parity_ref, *refs):
    x_refs, grad_refs = refs[:pieces], refs[pieces : pieces + len(tiles)]
    addend_ref = refs[-3] if has_addend else None
    out_ref, x_half = refs[-2:]
    depth = x_refs[0].shape[1]
    step = pl.program_id(0)

    @pl.when(step == 0)
    def _():
        for i, ref in enumerate(x_refs):
            x_half[:, i * depth : (i + 1) * depth] = ref[...]

    first = 0
    for ref, count in zip(grad_refs, tiles):

        @pl.when(jnp.logical_and(step >= first, step < first + count))
        def _(ref=ref):
            total = tn(x_half[...], ref[...])
            if has_addend:
                total = total + addend_ref[...].astype(F32)
            out_ref[...] = total.astype(LOW)

        first += count


def weight_grad_half(fsdp, parity, x, grads, addend=None):
    rows, width = x.shape
    depth, pieces = width // fsdp, fsdp // 2
    tile = math.gcd(1024, *[g.shape[1] for g in grads])
    tiles = [g.shape[1] // tile for g in grads]
    firsts = [sum(tiles[:i]) for i in range(len(tiles))]
    cols = tile * sum(tiles)

    def x_spec(i):
        return pl.BlockSpec((rows, depth), lambda j, parity: (0, 2 * i + parity[0]))

    def grad_spec(first, count):
        return pl.BlockSpec(
            (rows, tile), lambda j, parity: (0, jnp.clip(j - first, 0, count - 1))
        )

    out = pl.BlockSpec((width // 2, tile), lambda j, parity: (0, j))
    specs = [x_spec(i) for i in range(pieces)]
    specs += [grad_spec(f, c) for f, c in zip(firsts, tiles)]
    extra = [] if addend is None else [addend]
    return pl.pallas_call(
        functools.partial(weight_grad_kernel, pieces, tiles, addend is not None),
        grid_spec=pltpu.PrefetchScalarGridSpec(
            num_scalar_prefetch=1,
            grid=(sum(tiles),),
            in_specs=specs + [out] * len(extra),
            out_specs=out,
            scratch_shapes=[pltpu.VMEM((rows, width // 2), LOW)],
        ),
        out_shape=jax.ShapeDtypeStruct((width // 2, cols), LOW),
        compiler_params=pltpu.CompilerParams(vmem_limit_bytes=52 * MIB),
        cost_estimate=pl.CostEstimate(
            flops=rows * width * cols,
            bytes_accessed=rows * width + 2 * rows * cols + width * cols,
            transcendentals=0,
        ),
        name="weight_grad",
    )(parity, *[x] * pieces, *grads, *extra)


def project_kernel(tiles, rows_ref, weight_ref, pre_ref, value_ref, query_sq_ref, key_sq_ref):
    step = pl.program_id(0)
    result = nn(rows_ref[...], weight_ref[...])
    squares = jnp.sum(result * result, axis=1, keepdims=True)

    @pl.when(step < 2 * tiles)
    def _():
        pre_ref[...] = result

    for first, ref in ((0, query_sq_ref), (tiles, key_sq_ref)):

        @pl.when(step == first)
        def _(ref=ref):
            ref[...] = squares

        @pl.when(jnp.logical_and(step > first, step < first + tiles))
        def _(ref=ref):
            ref[...] += squares

    @pl.when(step >= 2 * tiles)
    def _():
        value_ref[...] = result.astype(LOW)


def project(inputs, full):
    rows, depth = inputs.shape
    cols = full.shape[1] // 3
    tile = min(512, cols)
    tiles = cols // tile
    column = pl.BlockSpec((rows, 1), lambda j: (0, 0))
    return pl.pallas_call(
        functools.partial(project_kernel, tiles),
        grid=(3 * tiles,),
        in_specs=[
            pl.BlockSpec((rows, depth), lambda j: (0, 0)),
            pl.BlockSpec((depth, tile), lambda j: (0, j)),
        ],
        out_specs=[
            pl.BlockSpec((rows, tile), lambda j: (0, jnp.minimum(j, 2 * tiles - 1))),
            pl.BlockSpec((rows, tile), lambda j: (0, jnp.maximum(j - 2 * tiles, 0))),
            column,
            column,
        ],
        out_shape=[
            jax.ShapeDtypeStruct((rows, 2 * cols), F32),
            jax.ShapeDtypeStruct((rows, cols), LOW),
            jax.ShapeDtypeStruct((rows, 1), F32),
            jax.ShapeDtypeStruct((rows, 1), F32),
        ],
        compiler_params=pltpu.CompilerParams(vmem_limit_bytes=48 * MIB),
        cost_estimate=pl.CostEstimate(
            flops=6 * rows * depth * cols,
            bytes_accessed=6 * depth * cols + 10 * rows * cols + 2 * rows * depth,
            transcendentals=0,
        ),
        name="project",
    )(inputs, full)


def attention_specs(heads):
    head = pl.BlockSpec((SEQ_LEN, HEAD_DIM), lambda i, place: (0, i))
    later = pl.BlockSpec((SEQ_LEN, HEAD_DIM), lambda i, place: (0, i + heads))
    whole = pl.BlockSpec((SEQ_LEN, HEAD_DIM), lambda i, place: (0, 0))
    column = pl.BlockSpec((SEQ_LEN, 1), lambda i, place: (0, 0))
    gain = pl.BlockSpec((1, HEAD_DIM), lambda i, place: (0, i))
    lse = pl.BlockSpec((None, SEQ_LEN, 1), lambda i, place: (i, 0, 0))
    return head, later, whole, column, gain, lse


def attend(rows, parts, place, pre, value, invs, gains, tables):
    width = value.shape[1]
    heads = width // HEAD_DIM
    head, later, whole, column, gain, lse = attention_specs(heads)
    low = jax.ShapeDtypeStruct((SEQ_LEN, width), LOW)
    return pl.pallas_call(
        functools.partial(attend_kernel, rows, parts, 1.0 / math.sqrt(HEAD_DIM)),
        grid_spec=pltpu.PrefetchScalarGridSpec(
            num_scalar_prefetch=1,
            grid=(heads,),
            in_specs=[head, later, head, column, column, gain, gain, whole, whole],
            out_specs=[head, head, head, lse],
            scratch_shapes=[
                pltpu.VMEM((SEQ_LEN, HEAD_DIM), LOW),
                pltpu.VMEM((SEQ_LEN, HEAD_DIM), LOW),
            ],
        ),
        out_shape=[low, low, low, jax.ShapeDtypeStruct((heads, SEQ_LEN, 1), F32)],
        compiler_params=pltpu.CompilerParams(vmem_limit_bytes=40 * 2**20),
        cost_estimate=pl.CostEstimate(
            flops=8 * heads * SEQ_LEN * SEQ_LEN * HEAD_DIM,
            bytes_accessed=16 * SEQ_LEN * width,
            transcendentals=heads * SEQ_LEN * SEQ_LEN,
        ),
        name="attend",
    )(place, pre, pre, value, *invs, *gains, *tables)


def attend_back(rows, parts, place, rots, value, grad, lse_all, pre, invs, gains, tables):
    width = value.shape[1]
    heads = width // HEAD_DIM
    head, later, whole, column, gain, lse = attention_specs(heads)
    full = jax.ShapeDtypeStruct((SEQ_LEN, width), F32)
    gain_out = jax.ShapeDtypeStruct((1, width), F32)
    inner = jax.ShapeDtypeStruct((SEQ_LEN, 1), F32)
    return pl.pallas_call(
        functools.partial(attend_back_kernel, rows, parts, 1.0 / math.sqrt(HEAD_DIM)),
        grid_spec=pltpu.PrefetchScalarGridSpec(
            num_scalar_prefetch=1,
            grid=(heads,),
            in_specs=[head, head, head, head, lse, head, later]
            + [column, column, gain, gain, whole, whole],
            out_specs=[head, head, head, gain, gain, column, column],
            scratch_shapes=[
                pltpu.VMEM((SEQ_LEN, HEAD_DIM), LOW),
                pltpu.VMEM((SEQ_LEN, HEAD_DIM), LOW),
                pltpu.VMEM((SEQ_LEN, HEAD_DIM), F32),
                pltpu.VMEM((SEQ_LEN, HEAD_DIM), F32),
            ],
        ),
        out_shape=[
            full,
            full,
            jax.ShapeDtypeStruct((SEQ_LEN, width), LOW),
            gain_out,
            gain_out,
            inner,
            inner,
        ],
        compiler_params=pltpu.CompilerParams(vmem_limit_bytes=48 * 2**20),
        cost_estimate=pl.CostEstimate(
            flops=20 * heads * SEQ_LEN * SEQ_LEN * HEAD_DIM,
            bytes_accessed=32 * SEQ_LEN * width,
            transcendentals=heads * SEQ_LEN * SEQ_LEN,
        ),
        name="attend_back",
    )(place, *rots, value, grad, lse_all, pre, pre, *invs, *gains, *tables)


def norm_back(grad_hat, values_hat, inverse, width):
    inner = jnp.sum(grad_hat * values_hat, axis=1, keepdims=True) / width
    return inverse * (grad_hat - values_hat * inner)


def layer(fsdp, tensor, *arguments):
    layer_input, query_weight, key_weight, value_weight, out_weight = arguments[:5]
    gate_weight, up_weight, down_weight = arguments[5:8]
    query_gain, key_gain, attn_gain, ffn_gain, out_cotangent = arguments[8:]
    rows_here, width = layer_input.shape
    head_cols = query_weight.shape[1]
    parts = SEQ_LEN // rows_here
    spans = tensor // parts
    fsdp_rank = lax.axis_index("fsdp")
    rank = lax.axis_index("tensor")
    place, span = rank % parts, rank // parts
    core = fsdp_rank % 2

    def to_part(x, shift):
        pairs = [
            (s * parts + p, s * parts + (p + shift) % parts)
            for s in range(spans)
            for p in range(parts)
        ]
        return lax.ppermute(x, "tensor", pairs)

    def to_span(x, shift):
        pairs = [
            (s * parts + p, (s + shift) % spans * parts + p)
            for s in range(spans)
            for p in range(parts)
        ]
        return lax.ppermute(x, "tensor", pairs)

    def gather_shard(shard):
        return lax.all_gather(shard, "fsdp", axis=0, tiled=True)

    def gather_rows(own):
        return jnp.concatenate([own] + [to_part(own, p) for p in range(1, parts)], axis=0)

    def product_others(pairs):
        return [
            to_part(product_sum(rows_here, p, pairs, LOW), -p) for p in range(1, parts)
        ]

    def product_own(pairs, came):
        total = product_sum(rows_here, 0, pairs, F32)
        for piece in came:
            total = total + piece.astype(F32)
        return total

    def sum_parts(x):
        total = x
        for p in range(1, parts):
            total = total + jnp.roll(to_part(x, p), p * rows_here, axis=0)
        return total

    def sum_all(x):
        for axis, size in (("fsdp", fsdp), ("tensor", tensor)):
            bit = 1
            while bit < size:
                x = x + lax.ppermute(x, axis, [(i, i ^ bit) for i in range(size)])
                bit *= 2
        return x

    same_core = [list(range(c, fsdp, 2)) for c in range(2)]
    mine = jnp.full((1,), core, jnp.int32)

    def weight_grad_away(x, grads):
        sent = weight_grad_half(fsdp, 1 - mine, x, grads)
        return sent, lax.ppermute(sent, "fsdp", [(f, f ^ 1) for f in range(fsdp)])

    def weight_grad_here(x, grads, came):
        total = weight_grad_half(fsdp, mine, x, grads, came)
        return total, lax.psum_scatter(
            total, "fsdp", scatter_dimension=0, tiled=True, axis_index_groups=same_core
        )

    def sum_spans(total, weights):
        split = total.reshape(total.shape[0], weights, spans, -1)
        result = split[:, :, 0].astype(F32)
        for s in range(1, spans):
            result = result + to_span(split[:, :, s], -s).astype(F32)
        return [result[:, w] for w in range(weights)]

    def own_columns(s):
        return ((span + spans - s) % spans * parts + place) * head_cols

    def gain_here(gain):
        return jnp.concatenate(
            [lax.dynamic_slice_in_dim(gain, own_columns(s), head_cols) for s in range(spans)]
        )[None, :]

    def gain_whole(part):
        whole = jnp.zeros((width,), F32)
        for s in range(spans):
            whole = lax.dynamic_update_slice_in_dim(
                whole, part[0, s * head_cols : (s + 1) * head_cols], own_columns(s), 0
            )
        return whole

    gate_up_shard = jnp.concatenate([gate_weight, up_weight], axis=1)
    down_shard = down_weight.T
    first = [query_weight, key_weight, value_weight, out_weight.T]
    shards, plan = [], []
    for s in range(spans):
        for w, shard in enumerate(first):
            shards.append(shard)
            plan.append((w // 3, s, w % 3 * spans + s, False))
    (inputs,), (full_qkv, full_out), _ = exchange(
        0, fsdp, parts, spans, shards, plan, rows=[layer_input]
    )
    full_gate_up = [gather_shard(after(gate_up_shard, inputs))]
    gate_up_came = [to_span(after(gate_up_shard, inputs), s) for s in range(1, spans)]

    local = jnp.arange(SEQ_LEN)
    position = (place + parts - local // rows_here) % parts * rows_here + local % rows_here
    inverse = THETA ** (-jnp.arange(0, HEAD_DIM, 2).astype(F32) / HEAD_DIM)
    angles = position.astype(F32)[:, None] * inverse[None, :]
    cos, sin = jnp.cos(angles), jnp.sin(angles)
    tables = (jnp.concatenate([cos, cos], axis=1), jnp.concatenate([-sin, sin], axis=1))
    gains = (gain_here(query_gain), gain_here(key_gain))
    place_arr = jnp.full((1,), place, jnp.int32)

    pre, value_low, query_sq, key_sq = project(inputs, full_qkv)
    squares = sum_parts(jnp.concatenate([query_sq, key_sq], axis=1))
    invs = lax.rsqrt(squares / width + EPSILON)
    invs = (invs[:, :1], invs[:, 1:])
    attended, query_rot, key_rot, lse = attend(
        rows_here, parts, place_arr, pre, value_low, invs, gains, tables
    )
    full_gate_up += [gather_shard(after(came, attended)) for came in gate_up_came]
    others = product_others([(attended, full_out, 0)])
    _, (down_own,), (down_came,) = exchange(
        1, fsdp, parts, spans, [down_shard], [(0, 0, 0, True)], sends=[down_shard], earlier=others
    )
    branch = product_own([(attended, full_out, 0)], others)
    branch_inv = lax.rsqrt(jnp.mean(branch * branch, axis=1, keepdims=True) + EPSILON)
    branch_hat = branch * branch_inv
    middle = layer_input.astype(F32) + branch_hat * attn_gain
    middle_low = middle.astype(LOW)
    mixed_pieces = [to_part(middle_low, p) for p in range(1, parts)]
    _, full_down, _ = exchange(
        2,
        fsdp,
        parts,
        spans,
        [down_came[s] for s in range(spans - 1)],
        [(s, s + 1, 0, True) for s in range(spans - 1)],
        earlier=[middle_low, full_gate_up[0]],
    )
    full_down = [down_own, *full_down]
    mixed_pieces = [after(piece, full_down[-1]) for piece in mixed_pieces]
    mixed = jnp.concatenate([middle_low, *mixed_pieces], axis=0)
    gates, uppers, hiddens = zip(*[feed_up(mixed, full) for full in full_gate_up])
    pairs = [(hidden, down, 0) for hidden, down in zip(hiddens, full_down)]
    second = product_own(pairs, product_others(pairs))
    second_inv = lax.rsqrt(jnp.mean(second * second, axis=1, keepdims=True) + EPSILON)
    second_hat = second * second_inv
    output = (middle + second_hat * ffn_gain).astype(LOW)

    grad_out = out_cotangent.astype(F32)
    ffn_gain_part = jnp.sum(grad_out * second_hat, axis=0)
    grad_second = norm_back(grad_out * ffn_gain, second_hat, second_inv, width)
    grad_rows = gather_rows(grad_second.astype(LOW))
    sent, came = weight_grad_away(grad_rows, hiddens)
    cols = gate_weight.shape[1]
    back, now = [], sent
    for s, (down, gate, upper) in enumerate(zip(full_down, gates, uppers)):
        back.append(feed_up_back(after(grad_rows, now), down, gate, upper))
        now = back[-1][0]
        if s == 0:
            total, down_grad = weight_grad_here(after(grad_rows, now), hiddens, came)
            now = total

    pairs = [
        (grad, full, run) for pair, full in zip(back, full_gate_up) for run, grad in enumerate(pair)
    ]
    others = product_others(pairs)
    grad_mixed = product_sum(rows_here, 0, pairs, F32)
    now = grad_mixed
    gate_up_grad = {}
    for s in reversed(range(spans)):
        sent, came = weight_grad_away(after(mixed, now), back[s])
        total, gate_up_grad[s] = weight_grad_here(after(mixed, sent), back[s], came)
        now = total
        if s == spans - 1:
            for piece in others:
                grad_mixed = grad_mixed + after(piece, now, down_grad).astype(F32)
            grad_middle = grad_out + grad_mixed
            attn_gain_part = jnp.sum(grad_middle * branch_hat, axis=0)
            grad_branch = norm_back(grad_middle * attn_gain, branch_hat, branch_inv, width)
            grad_branch = grad_branch.astype(LOW)
            pieces = [to_part(grad_branch, p) for p in range(1, parts)]
            now = grad_branch
    grad_branch_rows = jnp.concatenate([grad_branch, *[after(p, now) for p in pieces]], axis=0)
    grad_attended = nn(grad_branch_rows, full_out).astype(LOW)
    sent, came = weight_grad_away(after(grad_branch_rows, grad_attended), [attended])
    (
        query_gained,
        key_gained,
        grad_value,
        query_gain_part,
        key_gain_part,
        query_inner,
        key_inner,
    ) = attend_back(
        rows_here,
        parts,
        place_arr,
        (query_rot, key_rot),
        value_low,
        after(grad_attended, sent, gate_up_grad[spans - 1]),
        lse,
        pre,
        invs,
        gains,
        tables,
    )
    total, out_grad = weight_grad_here(after(grad_branch_rows, grad_value), [attended], came)
    inners = sum_parts(jnp.concatenate([query_inner, key_inner], axis=1)) / width
    local_width = value_low.shape[1]
    grad_query = invs[0] * (query_gained - pre[:, :local_width] * invs[0] * inners[:, :1])
    grad_key = invs[1] * (key_gained - pre[:, local_width:] * invs[1] * inners[:, 1:])
    grad_qkv = jnp.concatenate(
        [grad_query.astype(LOW), grad_key.astype(LOW), grad_value], axis=1
    )
    sent, came = weight_grad_away(after(inputs, total, gate_up_grad[0]), [grad_qkv])
    total, qkv_grad = weight_grad_here(after(inputs, sent), [grad_qkv], came)
    pairs = [(after(grad_qkv, total), full_qkv, 0)]
    input_grad = grad_middle + product_own(pairs, product_others(pairs))
    gain_grads = sum_all(
        jnp.stack(
            [gain_whole(query_gain_part), gain_whole(key_gain_part), attn_gain_part, ffn_gain_part]
        )
    )
    (down_grad,) = sum_spans(down_grad, 1)
    gate_up_grad = gate_up_grad[0].astype(F32) + sum(
        to_span(gate_up_grad[s], -s).astype(F32) for s in range(1, spans)
    )
    (out_grad,) = sum_spans(out_grad, 1)
    query_grad, key_grad, value_grad = sum_spans(qkv_grad, 3)
    return (
        output,
        input_grad,
        query_grad,
        key_grad,
        value_grad,
        out_grad.T,
        gate_up_grad[:, :cols],
        gate_up_grad[:, cols:],
        down_grad.T,
        *gain_grads,
    )


def solution(mesh):
    columns, rows = P("fsdp", "tensor"), P("tensor", "fsdp")
    tokens = P(("fsdp", "tensor"), None)
    weights = (columns, columns, columns, rows, columns, columns, rows)
    return jax.shard_map(
        functools.partial(layer, mesh.shape["fsdp"], mesh.shape["tensor"]),
        mesh=mesh,
        in_specs=(tokens, *weights, P(), P(), P(), P(), tokens),
        out_specs=(tokens, tokens, *weights, P(), P(), P(), P()),
        check_vma=False,
    )
```

```python
import functools
import math

import jax
import jax.numpy as jnp
from jax import lax
from jax.experimental import pallas as pl
from jax.experimental.pallas import tpu as pltpu
from jax.sharding import PartitionSpec as P

HEAD_DIM = 128
SEQ_LEN = 1024
EPSILON = 1e-06
THETA = 500000.0
BLOCK = 256
LOW = jnp.bfloat16
F32 = jnp.float32


def nn(a, b):
    return lax.dot_general(a, b, (((1,), (0,)), ((), ())), preferred_element_type=F32)


def nt(a, b):
    return lax.dot_general(a, b, (((1,), (1,)), ((), ())), preferred_element_type=F32)


def tn(a, b):
    return lax.dot_general(a, b, (((0,), (0,)), ((), ())), preferred_element_type=F32)


def after(x, *earlier):
    return lax.optimization_barrier((x, *earlier))[0]


def block_start(place, block, rows, parts):
    part = block * BLOCK // rows
    return pl.multiple_of(
        lax.rem(place + parts - part, parts) * rows + block * BLOCK % rows, BLOCK
    )


def masked(scores):
    row = lax.broadcasted_iota(jnp.int32, scores.shape, 0)
    col = lax.broadcasted_iota(jnp.int32, scores.shape, 1)
    return jnp.where(row + (scores.shape[1] - scores.shape[0]) >= col, scores, -1e30)


def attend_kernel(rows, parts, scale, heads, sides, *refs):
    query_ref, key_ref, value_ref, query_inv_ref, key_inv_ref = refs[:5]
    query_gain_ref, key_gain_ref, cos_ref, sin_ref = refs[5:9]
    side_refs, refs = refs[9 : 9 + len(sides.operands)], refs[9 + len(sides.operands) :]
    out_ref, query_rot_ref, key_rot_ref, lse_ref = refs[:4]
    side_outs, refs = refs[4 : 4 + len(sides.out_shapes)], refs[4 + len(sides.out_shapes) :]
    key_seq, value_seq = refs[:2]
    sides_at = (side_refs, side_outs, refs[2:])
    place = lax.rem(lax.axis_index("tensor"), parts)

    @pl.when(pl.program_id(0) == 0)
    def _():
        greet(sides.partners())
        sides.start(*sides_at)
        sides.start_rest(*sides_at)

    half = HEAD_DIM // 2
    for block in range(SEQ_LEN // BLOCK):
        here = pl.ds(block_start(place, block, rows, parts), BLOCK)
        there = pl.ds(block * BLOCK, BLOCK)
        cos, sin = cos_ref[here], sin_ref[here]
        key = key_ref[here] * key_inv_ref[here] * key_gain_ref[...]
        key = (key * cos + pltpu.roll(key, half, 1) * sin).astype(LOW)
        key_rot_ref[here] = key
        key_seq[there] = key
        value_seq[there] = value_ref[here]
        query = query_ref[here] * query_inv_ref[here] * query_gain_ref[...]
        query = (query * cos + pltpu.roll(query, half, 1) * sin).astype(LOW)
        query_rot_ref[here] = query
        span = (block + 1) * BLOCK
        scores = masked(nt(query, key_seq[:span]) * scale)
        top = jnp.max(scores, axis=1, keepdims=True)
        exps = jnp.exp(scores - top)
        total = jnp.sum(exps, axis=1, keepdims=True)
        weights = (exps * (1.0 / total)).astype(LOW)
        out_ref[here] = nn(weights, value_seq[:span]).astype(LOW)
        lse_ref[here] = top + jnp.log(total)

    @pl.when(pl.program_id(0) == heads - 1)
    def _():
        sides.finish(*sides_at)


def attend_back_kernel(rows, parts, scale, heads, sides, *refs):
    query_rot_ref, key_rot_ref, value_ref, grad_ref, lse_ref, query_ref, key_ref = refs[:7]
    query_inv_ref, key_inv_ref, query_gain_ref, key_gain_ref, cos_ref, sin_ref = refs[7:13]
    side_refs, refs = refs[13 : 13 + len(sides.operands)], refs[13 + len(sides.operands) :]
    query_out_ref, key_out_ref, value_out_ref = refs[:3]
    query_gain_out_ref, key_gain_out_ref, query_inner_ref, key_inner_ref = refs[3:7]
    side_outs, refs = refs[7 : 7 + len(sides.out_shapes)], refs[7 + len(sides.out_shapes) :]
    key_seq, value_seq, key_acc, value_acc = refs[:4]
    sides_at = (side_refs, side_outs, refs[4:])
    place = lax.rem(lax.axis_index("tensor"), parts)
    half = HEAD_DIM // 2
    count = SEQ_LEN // BLOCK

    @pl.when(pl.program_id(0) == 0)
    def _():
        greet(sides.partners())
        sides.start(*sides_at)
        sides.start_rest(*sides_at)
        query_inner_ref[...] = jnp.zeros_like(query_inner_ref)
        key_inner_ref[...] = jnp.zeros_like(key_inner_ref)

    def finish(grad, here, values_ref, inv_ref, gain_ref, out_ref, inner_ref):
        back = grad * cos_ref[here] - pltpu.roll(grad, half, 1) * sin_ref[here]
        hat = values_ref[here] * inv_ref[here]
        gained = back * gain_ref[...]
        out_ref[here] = gained
        inner_ref[here] += jnp.sum(gained * hat, axis=1, keepdims=True)
        return jnp.sum(back * hat, axis=0, keepdims=True)

    query_gain_sum = jnp.zeros((1, HEAD_DIM), F32)
    for block in range(count):
        here = pl.ds(block_start(place, block, rows, parts), BLOCK)
        there = pl.ds(block * BLOCK, BLOCK)
        key_seq[there] = key_rot_ref[here]
        value_seq[there] = value_ref[here]
        query, grad = query_rot_ref[here], grad_ref[here]
        span = (block + 1) * BLOCK
        scores = masked(nt(query, key_seq[:span]) * scale)
        probs = jnp.exp(scores - lse_ref[here])
        weights = probs.astype(LOW)
        grad_probs = nt(grad, value_seq[:span])
        delta = jnp.sum(probs * grad_probs, axis=1, keepdims=True)
        grad_scores = (probs * (grad_probs - delta) * scale).astype(LOW)
        value_part = tn(weights, grad)
        key_part = tn(grad_scores, query)
        past = block * BLOCK
        if block:
            key_acc[:past] += key_part[:past]
            value_acc[:past] += value_part[:past]
        key_acc[past:span] = key_part[past:]
        value_acc[past:span] = value_part[past:]
        query_gain_sum += finish(
            nn(grad_scores, key_seq[:span]),
            here,
            query_ref,
            query_inv_ref,
            query_gain_ref,
            query_out_ref,
            query_inner_ref,
        )
    query_gain_out_ref[...] = query_gain_sum
    key_gain_sum = jnp.zeros((1, HEAD_DIM), F32)
    for block in range(count):
        here = pl.ds(block_start(place, block, rows, parts), BLOCK)
        there = pl.ds(block * BLOCK, BLOCK)
        value_out_ref[here] = value_acc[there].astype(LOW)
        key_gain_sum += finish(
            key_acc[there],
            here,
            key_ref,
            key_inv_ref,
            key_gain_ref,
            key_out_ref,
            key_inner_ref,
        )
    key_gain_out_ref[...] = key_gain_sum

    @pl.when(pl.program_id(0) == heads - 1)
    def _():
        sides.finish(*sides_at)


MESH = pl.DeviceIdType.MESH
MIB = 2**20


def flip(index, bit):
    return index + bit - 2 * bit * lax.rem(lax.div(index, bit), 2)


def row_shares(rows, count):
    units = rows // 16
    sizes = [16 * (units // count + (i < units % count)) for i in range(count)]
    starts = [sum(sizes[:i]) for i in range(count)]
    return list(zip(starts, sizes))


def call(kernel, operands, in_specs, earlier=(), **options):
    count = len(operands)

    def body(*refs):
        kernel(*refs[:count], *refs[count + len(earlier) :])

    specs = [*in_specs, *[pl.BlockSpec(memory_space=pl.ANY)] * len(earlier)]
    return pl.pallas_call(body, in_specs=specs, **options)(*operands, *earlier)


def greet(partners):
    barrier = pltpu.get_barrier_semaphore()
    for partner in partners:
        pl.semaphore_signal(barrier, inc=1, device_id=partner, device_id_type=MESH)
    pl.semaphore_wait(barrier, len(partners))


def remote(src, dst, send_sem, recv_sem, **device):
    return pltpu.make_async_remote_copy(
        src_ref=src,
        dst_ref=dst,
        send_sem=send_sem,
        recv_sem=recv_sem,
        device_id=device,
        device_id_type=MESH,
    )


class Copies:
    def __init__(self, send_sems, recv_sems):
        self.send_sems, self.recv_sems = send_sems, recv_sems
        self.used = 0
        self.open = []
        self.moves = []

    def send(self, src, dst, **device):
        copy = remote(
            src, dst, self.send_sems.at[self.used], self.recv_sems.at[self.used], **device
        )
        self.used += 1
        copy.start()
        self.open.append(copy.wait_send)
        return copy

    def move(self, src, hold, dst):
        load = pltpu.make_async_copy(src, hold, self.send_sems.at[self.used])
        store = pltpu.make_async_copy(hold, dst, self.recv_sems.at[self.used])
        self.used += 1
        load.start()
        self.moves.append((load, store))

    def finish(self):
        for load, store in self.moves:
            load.wait()
            store.start()
        for wait in self.open:
            wait()
        for _, store in self.moves:
            store.wait()


class Rows:
    def __init__(self, parts, gather=None, deliver=None):
        self.parts, self.gather = parts, gather is not None
        self.half = (gather if self.gather else deliver[0]).shape[0] // 2
        self.operands = [gather] if self.gather else list(deliver)
        first = self.operands[0]
        count = parts if self.gather else parts - 1
        self.out_shapes = [jax.ShapeDtypeStruct((count, *first.shape), LOW)]
        count = 2 * parts
        self.scratch = [pltpu.SemaphoreType.DMA((count,)), pltpu.SemaphoreType.DMA((count,))]
        if self.gather:
            self.scratch.append(pltpu.VMEM(first.shape, LOW))

    def ranks(self):
        rank = lax.axis_index("tensor")
        place = lax.rem(rank, self.parts)
        shifts = range(1, self.parts)
        if not self.gather:
            shifts = [self.parts - p for p in shifts]
        return [rank - place + lax.rem(place + p, self.parts) for p in shifts]

    def partners(self):
        return [{"tensor": rank} for rank in self.ranks()]

    def copies(self, halves, refs, outs, send_sems, recv_sems, hold=None):
        made = []
        for half in halves:
            rows = pl.ds(half * self.half, self.half)
            for i, rank in enumerate(self.ranks()):
                src = refs[0] if self.gather else refs[i]
                dst = outs[0].at[i + 1] if self.gather else outs[0].at[i]
                sem = 2 * i + half
                made.append(
                    remote(
                        src.at[rows], dst.at[rows], send_sems.at[sem], recv_sems.at[sem], tensor=rank
                    )
                )
        return made

    def load(self, refs, outs, send_sems, recv_sems, hold):
        return pltpu.make_async_copy(refs[0], hold, send_sems.at[2 * self.parts - 1])

    def store(self, refs, outs, send_sems, recv_sems, hold):
        return pltpu.make_async_copy(hold, outs[0].at[0], recv_sems.at[2 * self.parts - 1])

    def start(self, *where):
        for copy in self.copies([0], *where):
            copy.start()
        if self.gather:
            self.load(*where).start()

    def start_rest(self, *where):
        for copy in self.copies([1], *where):
            copy.start()

    def finish(self, *where):
        if self.gather:
            self.load(*where).wait()
            self.store(*where).start()
            self.store(*where).wait()
        for copy in self.copies([0, 1], *where):
            copy.wait()

    def results(self, outs):
        out = outs[0]
        if self.gather:
            return out.reshape(-1, out.shape[2])
        return [out[i] for i in range(self.parts - 1)]


class Spans:
    def __init__(self, parts, spans, terms):
        self.parts, self.spans, self.terms = parts, spans, terms
        self.operands = [array for array, *_ in terms]
        self.out_shapes = [
            jax.ShapeDtypeStruct((array.shape[0], width), LOW) for array, _, width, _ in terms
        ]
        count = max(1, len(terms))
        self.scratch = [pltpu.SemaphoreType.DMA((count,)), pltpu.SemaphoreType.DMA((count,))]

    def rank(self, back):
        rank = lax.axis_index("tensor")
        place, span = lax.rem(rank, self.parts), lax.div(rank, self.parts)
        return lax.rem(span + self.spans - back, self.spans) * self.parts + place

    def partners(self):
        return [{"tensor": self.rank(s)} for s in range(1, self.spans)]

    def copies(self, refs, outs, send_sems, recv_sems):
        return [
            remote(
                ref.at[:, pl.ds(run * width, width)],
                out,
                send_sems.at[i],
                recv_sems.at[i],
                tensor=self.rank(back),
            )
            for i, (ref, out, (_, run, width, back)) in enumerate(zip(refs, outs, self.terms))
        ]

    def start(self, *where):
        for copy in self.copies(*where):
            copy.start()

    def start_rest(self, *where):
        pass

    def finish(self, *where):
        for copy in self.copies(*where):
            copy.wait()

    def results(self, outs):
        return list(outs)


class Sides:
    def __init__(self, *jobs):
        self.jobs = jobs
        self.operands = [x for job in jobs for x in job.operands]
        self.out_shapes = [x for job in jobs for x in job.out_shapes]
        self.scratch = [x for job in jobs for x in job.scratch]

    def partners(self):
        return [partner for job in self.jobs for partner in job.partners()]

    def each(self, refs, outs, scratch):
        for job in self.jobs:
            counts = len(job.operands), len(job.out_shapes), len(job.scratch)
            yield job, (refs[: counts[0]], outs[: counts[1]], *scratch[: counts[2]])
            refs, outs, scratch = refs[counts[0] :], outs[counts[1] :], scratch[counts[2] :]

    def start(self, *where):
        for job, own in self.each(*where):
            job.start(*own)

    def start_rest(self, *where):
        for job, own in self.each(*where):
            job.start_rest(*own)

    def finish(self, *where):
        for job, own in self.each(*where):
            job.finish(*own)

    def results(self, outs):
        return [job.results(own) for job, (_, own, *_) in self.each([], outs, [])]

    def options(self, number):
        return {"collective_id": number, "has_side_effects": True} if self.jobs else {}


NO_SIDES = Sides()


def exchange_kernel(fsdp, parts, spans, plan, counts, *refs):
    sides, shard_count, send_count, full_count = counts
    rows_count = len(sides.operands)
    rows_refs, refs = refs[:rows_count], refs[rows_count:]
    shard_refs, refs = refs[:shard_count], refs[shard_count:]
    span_refs, refs = refs[:send_count], refs[send_count:]
    full_refs, refs = refs[:full_count], refs[full_count:]
    span_outs, refs = refs[:send_count], refs[send_count:]
    side_outs, refs = refs[: len(sides.out_shapes)], refs[len(sides.out_shapes) :]
    hold_refs, refs = refs[: len(plan)], refs[len(plan) :]
    sides_at = (rows_refs, side_outs, refs[:-2])
    copies = Copies(*refs[-2:])
    me, rank = lax.axis_index("fsdp"), lax.axis_index("tensor")
    place, span = lax.rem(rank, parts), lax.div(rank, parts)
    bits = [1 << b for b in range(1, fsdp.bit_length() - 1)]
    span_ranks = [lax.rem(span + s, spans) * parts + place for s in range(1, spans)]
    partners = [{"fsdp": flip(me, bit)} for bit in [1, *bits]] if plan else []
    partners += sides.partners()
    if send_count or any(s and not here for _, s, _, here in plan):
        partners += [{"tensor": r} for r in span_ranks]
    greet(partners)

    def slot(job, mask, share=None):
        group, s, position, _ = plan[job]
        which = me
        for bit in [1, *bits]:
            if mask & bit:
                which = flip(which, bit)
        cols = shard_refs[job].shape[1]
        ref = full_refs[group].at[which, :, pl.ds(position * cols, cols)]
        return ref if share is None else ref.at[pl.ds(*share)]

    depth = shard_refs[0].shape[0] if plan else 16
    shares = row_shares(depth, len(bits))
    jobs = range(len(plan))
    away = [s and not here for _, s, _, here in plan]
    sides.start(*sides_at)
    from_span = {
        job: copies.send(shard_refs[job], slot(job, 0), tensor=span_ranks[plan[job][1] - 1])
        for job in jobs
        if away[job]
    }
    sides.start_rest(*sides_at)
    over = []
    for ref, out in zip(span_refs, span_outs):
        for s, r in enumerate(span_ranks):
            over.append(copies.send(ref, out.at[s], tensor=r))
    for job in jobs:
        if not away[job]:
            copies.move(shard_refs[job], hold_refs[job], slot(job, 0))

    arriving = {}
    held = {(job, p): [0] for job in jobs for p in range(len(shares))}

    def source(job, mask, share):
        if mask == 0 and not away[job]:
            return shard_refs[job].at[pl.ds(*share)]
        return slot(job, mask, share)

    def send_step(job, step):
        for p, share in enumerate(shares):
            bit = bits[(p + step) % len(bits)]
            for mask in held[job, p]:
                arriving[job, p, mask | bit] = copies.send(
                    source(job, mask, share), slot(job, mask, share), fsdp=flip(me, bit)
                )

    def take_step(job, step):
        for p in range(len(shares)):
            bit = bits[(p + step) % len(bits)]
            came = [mask | bit for mask in held[job, p]]
            for mask in came:
                arriving[job, p, mask].wait_recv()
            held[job, p] += came

    for step in range(len(bits) + 1):
        for job in jobs:
            if step == 0 and away[job]:
                from_span[job].wait_recv()
            if step:
                take_step(job, step - 1)
            if step < len(bits):
                send_step(job, step)
            else:
                for mask in range(0, fsdp, 2):
                    whole = (0, depth)
                    over.append(
                        copies.send(
                            source(job, mask, whole), slot(job, mask), fsdp=flip(me, 1)
                        )
                    )
    for copy in over:
        copy.wait_recv()
    copies.finish()
    sides.finish(*sides_at)


def exchange(number, fsdp, parts, spans, shards=(), plan=(), sides=NO_SIDES, sends=(), earlier=()):
    bits = fsdp.bit_length() - 2
    per_job = 2 + bits * (2**bits - 1) + 2**bits
    count = len(plan) * per_job + len(sends) * spans + 1
    hbm = pl.BlockSpec(memory_space=pl.ANY)
    full_count = 1 + max([group for group, *_ in plan], default=-1)
    widths = [0] * full_count
    for shard, (group, *_) in zip(shards, plan):
        widths[group] += shard.shape[1]
    depth = shards[0].shape[0] if plan else 0
    outs = [jax.ShapeDtypeStruct((fsdp, depth, width), LOW) for width in widths]
    outs += [jax.ShapeDtypeStruct((spans - 1, *x.shape), LOW) for x in sends]
    inputs = [*shards, *sends]
    scratch = [pltpu.SemaphoreType.DMA((count,)), pltpu.SemaphoreType.DMA((count,))]
    inputs = [*sides.operands, *inputs]
    outs += sides.out_shapes
    scratch = [*sides.scratch, *scratch]
    scratch = [
        *[pltpu.VMEM(x.shape if here or not s else (16, 128), LOW) for x, (_, s, _, here) in zip(shards, plan)],
        *scratch,
    ]
    results = call(
        functools.partial(
            exchange_kernel,
            fsdp,
            parts,
            spans,
            plan,
            (sides, len(shards), len(sends), full_count),
        ),
        inputs,
        [hbm] * len(inputs),
        earlier,
        out_shape=outs,
        out_specs=[hbm] * len(outs),
        scratch_shapes=scratch,
        compiler_params=pltpu.CompilerParams(collective_id=number, has_side_effects=True),
        name="exchange",
    )
    full = [r.reshape(fsdp * depth, -1) for r in results[:full_count]]
    came = results[full_count : full_count + len(sends)]
    return full, came, *sides.results(results[full_count + len(sends) :])


def sum_kernel(pairs, sides, steps, *refs):
    step = pl.program_id(0)
    count = 2 * pairs + len(sides.operands)
    out_ref, outs = refs[count], refs[count + 1 : count + 1 + len(sides.out_shapes)]
    sides_at = (refs[2 * pairs : count], outs, refs[count + 1 + len(sides.out_shapes) :])
    if sides.jobs:

        @pl.when(step == 0)
        def _():
            greet(sides.partners())
            sides.start(*sides_at)
            sides.start_rest(*sides_at)

    total = None
    for i in range(pairs):
        term = nt(refs[2 * i][...], refs[2 * i + 1][...])
        total = term if total is None else total + term
    out_ref[...] = total.astype(out_ref.dtype)
    if sides.jobs:

        @pl.when(step == steps - 1)
        def _():
            sides.finish(*sides_at)


def product_sum(count, block, pairs, kind, earlier=(), number=None, sides=NO_SIDES):
    width = pairs[0][1].shape[0]
    tile = min(512, width)
    specs, operands, flops = [], [], 0
    for a, b, run in pairs:
        depth = a.shape[1]
        specs.append(pl.BlockSpec((count, depth), lambda j: (block, 0)))
        specs.append(pl.BlockSpec((tile, depth), lambda j, run=run: (j, run)))
        operands += [a, b]
        flops += 2 * count * depth * width
    hbm = pl.BlockSpec(memory_space=pl.ANY)
    outs = [jax.ShapeDtypeStruct((count, width), kind)]
    out_specs = [pl.BlockSpec((count, tile), lambda j: (0, j))]
    operands += sides.operands
    specs += [hbm] * len(sides.operands)
    outs += sides.out_shapes
    out_specs += [hbm] * len(sides.out_shapes)
    steps = width // tile
    results = call(
        functools.partial(sum_kernel, len(pairs), sides, steps),
        operands,
        specs,
        earlier,
        grid=(steps,),
        out_specs=out_specs,
        out_shape=outs,
        scratch_shapes=sides.scratch,
        compiler_params=pltpu.CompilerParams(
            vmem_limit_bytes=56 * MIB, **sides.options(number)
        ),
        cost_estimate=pl.CostEstimate(
            flops=flops, bytes_accessed=flops // count + 4 * count * width, transcendentals=0
        ),
        name="product_sum",
    )
    return results[0], *sides.results(results[1:])


def up_kernel(mixed_ref, gate_weight_ref, up_weight_ref, gate_ref, upper_ref, hidden_ref):
    gate = nn(mixed_ref[...], gate_weight_ref[...])
    upper = nn(mixed_ref[...], up_weight_ref[...])
    gate_ref[...] = gate
    upper_ref[...] = upper
    hidden_ref[...] = (gate * jax.nn.sigmoid(gate) * upper).astype(LOW)


def feed_up(mixed, gate_up, cols, earlier=()):
    rows, depth = mixed.shape
    (gate_weight, gate_run), (up_weight, up_run) = gate_up
    tile = min(256, cols)
    tiles = cols // tile
    out = pl.BlockSpec((rows, tile), lambda j: (0, j))
    return call(
        up_kernel,
        [mixed, gate_weight, up_weight],
        [
            pl.BlockSpec((rows, depth), lambda j: (0, 0)),
            pl.BlockSpec((depth, tile), lambda j: (0, j + gate_run * tiles)),
            pl.BlockSpec((depth, tile), lambda j: (0, j + up_run * tiles)),
        ],
        earlier,
        grid=(tiles,),
        out_specs=[out, out, out],
        out_shape=[
            jax.ShapeDtypeStruct((rows, cols), F32),
            jax.ShapeDtypeStruct((rows, cols), F32),
            jax.ShapeDtypeStruct((rows, cols), LOW),
        ],
        compiler_params=pltpu.CompilerParams(vmem_limit_bytes=48 * MIB),
        cost_estimate=pl.CostEstimate(
            flops=4 * rows * depth * cols,
            bytes_accessed=4 * depth * cols + 10 * rows * cols,
            transcendentals=rows * cols,
        ),
        name="feed_up",
    )


def up_back_kernel(grad_ref, down_ref, gate_ref, upper_ref, gate_out_ref, up_out_ref):
    grad = nn(grad_ref[...], down_ref[...])
    gate = gate_ref[...]
    sigmoid = jax.nn.sigmoid(gate)
    scaled = grad * sigmoid
    up_out_ref[...] = (scaled * gate).astype(LOW)
    gate_out_ref[...] = (scaled * upper_ref[...] * (1.0 + gate * (1.0 - sigmoid))).astype(LOW)


def feed_up_back(grad_rows, down, gate, upper, earlier=()):
    rows, depth = grad_rows.shape
    cols = down.shape[1]
    tile = min(512, cols)
    spec = pl.BlockSpec((rows, tile), lambda j: (0, j))
    out = jax.ShapeDtypeStruct((rows, cols), LOW)
    return call(
        up_back_kernel,
        [grad_rows, down, gate, upper],
        [
            pl.BlockSpec((rows, depth), lambda j: (0, 0)),
            pl.BlockSpec((depth, tile), lambda j: (0, j)),
            spec,
            spec,
        ],
        earlier,
        grid=(cols // tile,),
        out_specs=[spec, spec],
        out_shape=[out, out],
        compiler_params=pltpu.CompilerParams(vmem_limit_bytes=52 * MIB),
        cost_estimate=pl.CostEstimate(
            flops=2 * rows * depth * cols,
            bytes_accessed=2 * depth * cols + 12 * rows * cols,
            transcendentals=rows * cols,
        ),
        name="feed_up_back",
    )


def weight_grad_kernel(fsdp, tiles, sides, *refs):
    x_ref, grad_refs, refs = refs[0], refs[1 : 1 + len(tiles)], refs[1 + len(tiles) :]
    count, outs = len(sides.operands), len(sides.out_shapes)
    side_refs, out_ref, refs = refs[:count], refs[count], refs[count + 1 :]
    side_outs, refs = refs[:outs], refs[outs:]
    x_half, sent, came, send_sems, recv_sems = refs[:5]
    sides_at = (side_refs, side_outs, refs[5:])
    me = lax.axis_index("fsdp")
    core = lax.rem(me, 2)
    total_tiles = sum(tiles)
    depth = x_ref.shape[1] // fsdp
    step = pl.program_id(0)

    def load(which):
        for i in range(fsdp // 2):
            first = pl.multiple_of((2 * i + which) * depth, depth)
            x_half[:, i * depth : (i + 1) * depth] = x_ref[:, pl.ds(first, depth)]

    def copy(tile):
        slot = lax.rem(tile, 2)
        return remote(
            sent.at[slot], came.at[tile], send_sems.at[slot], recv_sems.at[tile], fsdp=flip(me, 1)
        )

    @pl.when(step == 0)
    def _():
        load(1 - core)
        greet([{"fsdp": flip(me, 1)}, *sides.partners()])
        sides.start(*sides_at)
        sides.start_rest(*sides_at)

    @pl.when(step == total_tiles)
    def _():
        load(core)

    @pl.when(jnp.logical_and(step >= 2, step < total_tiles))
    def _():
        copy(step - 2).wait_send()

    tile = lax.rem(step, total_tiles)
    first = 0
    for ref, count in zip(grad_refs, tiles):
        here = jnp.logical_and(tile >= first, tile < first + count)

        @pl.when(jnp.logical_and(here, step < total_tiles))
        def _(ref=ref):
            sent[lax.rem(step, 2)] = tn(x_half[...], ref[...]).astype(LOW)

        @pl.when(jnp.logical_and(here, step >= total_tiles))
        def _(ref=ref):
            total = tn(x_half[...], ref[...])
            copy(tile).wait_recv()
            out_ref[...] = (total + came[tile].astype(F32)).astype(LOW)

        first += count

    @pl.when(step < total_tiles)
    def _():
        copy(step).start()

    @pl.when(step == 2 * total_tiles - 1)
    def _():
        for last in range(max(0, total_tiles - 2), total_tiles):
            copy(last).wait_send()
        sides.finish(*sides_at)


def weight_grad_half(number, fsdp, x, grads, earlier=(), sides=NO_SIDES):
    count, width = x.shape
    tile = math.gcd(1024, *[g.shape[1] for g in grads])
    tiles = [g.shape[1] // tile for g in grads]
    total_tiles = sum(tiles)
    firsts = [sum(tiles[:i]) for i in range(len(tiles))]
    cols = tile * total_tiles

    def grad_spec(first, runs):
        return pl.BlockSpec(
            (count, tile),
            lambda j: (0, jnp.clip(lax.rem(j, total_tiles) - first, 0, runs - 1)),
        )

    hbm = pl.BlockSpec(memory_space=pl.ANY)
    operands = [x, *grads]
    specs = [pl.BlockSpec((count, width), lambda j: (0, 0))]
    specs += [grad_spec(f, c) for f, c in zip(firsts, tiles)]
    outs = [jax.ShapeDtypeStruct((width // 2, cols), LOW)]
    out_specs = [pl.BlockSpec((width // 2, tile), lambda j: (0, jnp.maximum(j - total_tiles, 0)))]
    scratch = [
        pltpu.VMEM((count, width // 2), LOW),
        pltpu.VMEM((2, width // 2, tile), LOW),
        pltpu.VMEM((total_tiles, width // 2, tile), LOW),
        pltpu.SemaphoreType.DMA((2,)),
        pltpu.SemaphoreType.DMA((total_tiles,)),
    ]
    operands += sides.operands
    specs += [hbm] * len(sides.operands)
    outs += sides.out_shapes
    out_specs += [hbm] * len(sides.out_shapes)
    scratch += sides.scratch
    results = call(
        functools.partial(weight_grad_kernel, fsdp, tiles, sides),
        operands,
        specs,
        earlier,
        grid=(2 * total_tiles,),
        out_specs=out_specs,
        out_shape=outs,
        scratch_shapes=scratch,
        compiler_params=pltpu.CompilerParams(
            collective_id=number, has_side_effects=True, vmem_limit_bytes=56 * MIB
        ),
        cost_estimate=pl.CostEstimate(
            flops=2 * count * width * cols,
            bytes_accessed=2 * count * width + 4 * count * cols + width * cols,
            transcendentals=0,
        ),
        name="weight_grad",
    )
    return results[0], *sides.results(results[1:])


def column_shares(cols, count):
    return [(8 * start, 8 * size) for start, size in row_shares(cols // 8, count)]


def grad_scatter_kernel(fsdp, parts, spans, tiles, sides, *refs):
    x_ref, grad_ref, refs = refs[0], refs[1], refs[2:]
    count, outs = len(sides.operands), len(sides.out_shapes)
    side_refs, out_ref, refs = refs[:count], refs[count], refs[count + 1 :]
    side_outs, refs = refs[:outs], refs[outs:]
    x_half, sent, held, send_sems, recv_sems, chip_sends, chip_recvs = refs[:7]
    span_came, span_sends, span_recvs, refs = *refs[7:10], refs[10:]
    bits = [1 << b for b in range(fsdp.bit_length() - 2)]
    turns = len(bits)
    chip_came, side_scratch = refs[: turns * turns], refs[turns * turns :]
    sides_at = (side_refs, side_outs, side_scratch)
    me, rank = lax.axis_index("fsdp"), lax.axis_index("tensor")
    core, chip = lax.rem(me, 2), lax.div(me, 2)
    place, span = lax.rem(rank, parts), lax.div(rank, parts)
    depth = x_ref.shape[1] // fsdp
    tile_cols = grad_ref.shape[1]
    own_cols = tile_cols // spans
    shares = column_shares(tile_cols, turns)
    step = pl.program_id(0)

    def load(which):
        for i in range(fsdp // 2):
            first = pl.multiple_of((2 * i + which) * depth, depth)
            x_half[:, i * depth : (i + 1) * depth] = x_ref[:, pl.ds(first, depth)]

    def core_copy(tile):
        slot = lax.rem(tile, 2)
        return remote(
            sent.at[slot], held.at[tile], send_sems.at[slot], recv_sems.at[tile], fsdp=flip(me, 1)
        )

    def turned(mask):
        which = chip
        for bit in bits:
            if mask & bit:
                which = flip(which, bit)
        return pl.ds(pl.multiple_of(which * depth, depth), depth)

    def swaps(share, turn):
        order = [bits[(share + i) % turns] for i in range(turns)]
        stay = [0]
        for bit in order[turn + 1 :]:
            stay += [mask | bit for mask in stay]
        return order[turn], [(mask | order[turn], mask, i) for i, mask in enumerate(stay)]

    def chip_copies(tile, turn):
        made, number = [], 0
        for share, (start, size) in enumerate(shares):
            for earlier in range(turns):
                bit, moves = swaps(share, earlier)
                for goes, _, slot in moves:
                    if earlier == turn:
                        made.append(
                            remote(
                                held.at[tile, turned(goes), pl.ds(start, size)],
                                chip_came[share * turns + turn].at[tile, slot],
                                chip_sends.at[tile, number],
                                chip_recvs.at[tile, number],
                                fsdp=flip(me, 2 * bit),
                            )
                        )
                    number += 1
        return made

    def span_copies(tile):
        return [
            remote(
                held.at[tile, turned(0), pl.ds(s * own_cols, own_cols)],
                span_came.at[tile, s - 1],
                span_sends.at[tile, s - 1],
                span_recvs.at[tile, s - 1],
                tensor=lax.rem(span + spans - s, spans) * parts + place,
            )
            for s in range(1, spans)
        ]

    @pl.when(step == 0)
    def _():
        load(1 - core)
        partners = [{"fsdp": flip(me, 1)}] + [{"fsdp": flip(me, 2 * bit)} for bit in bits]
        partners += [
            {"tensor": lax.rem(span + s, spans) * parts + place} for s in range(1, spans)
        ]
        side_partners = sides.partners()
        greet(partners + side_partners)
        sides.start(*sides_at)
        sides.start_rest(*sides_at)

    @pl.when(step == tiles)
    def _():
        load(core)

    @pl.when(step < tiles)
    def _():
        @pl.when(step >= 2)
        def _():
            core_copy(step - 2).wait_send()

        sent[lax.rem(step, 2)] = tn(x_half[...], grad_ref[...]).astype(LOW)
        core_copy(step).start()

    @pl.when(jnp.logical_and(step >= tiles, step < 2 * tiles))
    def _():
        tile = step - tiles
        total = tn(x_half[...], grad_ref[...])
        core_copy(tile).wait_recv()
        held[tile] = (total + held[tile].astype(F32)).astype(LOW)
        for copy in chip_copies(tile, 0):
            copy.start()

    for turn in range(1, turns + 2):
        tile = step - tiles - turn

        @pl.when(jnp.logical_and(tile >= 0, tile < tiles))
        def _(turn=turn, tile=tile):
            if turn <= turns:
                for copy in chip_copies(tile, turn - 1):
                    copy.wait()
                for share, (start, size) in enumerate(shares):
                    _, moves = swaps(share, turn - 1)
                    for _, stays, slot in moves:
                        where = (tile, turned(stays), pl.ds(start, size))
                        came = chip_came[share * turns + turn - 1][tile, slot]
                        held[where] = (held[where].astype(F32) + came.astype(F32)).astype(LOW)
                for copy in chip_copies(tile, turn) if turn < turns else span_copies(tile):
                    copy.start()
            else:
                total = held[tile, turned(0), :own_cols].astype(F32)
                for s, copy in enumerate(span_copies(tile)):
                    copy.wait()
                    total = total + span_came[tile, s].astype(F32)
                out_ref[...] = total

    @pl.when(step == 2 * tiles + turns)
    def _():
        for last in range(max(0, tiles - 2), tiles):
            core_copy(last).wait_send()
        sides.finish(*sides_at)


def grad_scatter(number, fsdp, parts, spans, x, grads, tiles, earlier=(), sides=NO_SIDES):
    count, width = x.shape
    depth = width // fsdp
    tile = grads.shape[1] // tiles
    own = tile // spans
    turns = fsdp.bit_length() - 2
    shares = column_shares(tile, turns)
    hbm = pl.BlockSpec(memory_space=pl.ANY)
    swapped = turns * (2**turns - 1)
    results = call(
        functools.partial(grad_scatter_kernel, fsdp, parts, spans, tiles, sides),
        [x, grads, *sides.operands],
        [
            pl.BlockSpec((count, width), lambda j: (0, 0)),
            pl.BlockSpec(
                (count, tile),
                lambda j: (0, jnp.where(j < tiles, j, jnp.minimum(j - tiles, tiles - 1))),
            ),
            *[hbm] * len(sides.operands),
        ],
        earlier,
        grid=(2 * tiles + turns + 1,),
        out_specs=[
            pl.BlockSpec((depth, own), lambda j: (0, jnp.maximum(j - (tiles + turns + 1), 0))),
            *[hbm] * len(sides.out_shapes),
        ],
        out_shape=[jax.ShapeDtypeStruct((depth, own * tiles), F32), *sides.out_shapes],
        scratch_shapes=[
            pltpu.VMEM((count, width // 2), LOW),
            pltpu.VMEM((2, width // 2, tile), LOW),
            pltpu.VMEM((tiles, width // 2, tile), LOW),
            pltpu.SemaphoreType.DMA((2,)),
            pltpu.SemaphoreType.DMA((tiles,)),
            pltpu.SemaphoreType.DMA((tiles, swapped)),
            pltpu.SemaphoreType.DMA((tiles, swapped)),
            pltpu.VMEM((tiles, spans - 1, depth, own), LOW),
            pltpu.SemaphoreType.DMA((tiles, spans - 1)),
            pltpu.SemaphoreType.DMA((tiles, spans - 1)),
            *[
                pltpu.VMEM((tiles, 2 ** (turns - 1 - turn), depth, size), LOW)
                for _, size in shares
                for turn in range(turns)
            ],
            *sides.scratch,
        ],
        compiler_params=pltpu.CompilerParams(
            collective_id=number, has_side_effects=True, vmem_limit_bytes=56 * MIB
        ),
        cost_estimate=pl.CostEstimate(
            flops=2 * count * width * tile * tiles,
            bytes_accessed=2 * count * width + 4 * count * tile * tiles,
            transcendentals=0,
        ),
        name="grad_scatter",
    )
    return results[0], *sides.results(results[1:])


def project_kernel(tiles, rows_ref, weight_ref, pre_ref, value_ref, query_sq_ref, key_sq_ref):
    step = pl.program_id(0)
    result = nn(rows_ref[...], weight_ref[...])
    squares = jnp.sum(result * result, axis=1, keepdims=True)

    @pl.when(step < 2 * tiles)
    def _():
        pre_ref[...] = result

    for first, ref in ((0, query_sq_ref), (tiles, key_sq_ref)):

        @pl.when(step == first)
        def _(ref=ref):
            ref[...] = squares

        @pl.when(jnp.logical_and(step > first, step < first + tiles))
        def _(ref=ref):
            ref[...] += squares

    @pl.when(step >= 2 * tiles)
    def _():
        value_ref[...] = result.astype(LOW)


def project(inputs, full):
    rows, depth = inputs.shape
    cols = full.shape[1] // 3
    tile = min(512, cols)
    tiles = cols // tile
    column = pl.BlockSpec((rows, 1), lambda j: (0, 0))
    return pl.pallas_call(
        functools.partial(project_kernel, tiles),
        grid=(3 * tiles,),
        in_specs=[
            pl.BlockSpec((rows, depth), lambda j: (0, 0)),
            pl.BlockSpec((depth, tile), lambda j: (0, j)),
        ],
        out_specs=[
            pl.BlockSpec((rows, tile), lambda j: (0, jnp.minimum(j, 2 * tiles - 1))),
            pl.BlockSpec((rows, tile), lambda j: (0, jnp.maximum(j - 2 * tiles, 0))),
            column,
            column,
        ],
        out_shape=[
            jax.ShapeDtypeStruct((rows, 2 * cols), F32),
            jax.ShapeDtypeStruct((rows, cols), LOW),
            jax.ShapeDtypeStruct((rows, 1), F32),
            jax.ShapeDtypeStruct((rows, 1), F32),
        ],
        compiler_params=pltpu.CompilerParams(vmem_limit_bytes=48 * MIB),
        cost_estimate=pl.CostEstimate(
            flops=6 * rows * depth * cols,
            bytes_accessed=6 * depth * cols + 10 * rows * cols + 2 * rows * depth,
            transcendentals=0,
        ),
        name="project",
    )(inputs, full)


def attention_specs(heads):
    return (
        pl.BlockSpec((SEQ_LEN, HEAD_DIM), lambda i: (0, i)),
        pl.BlockSpec((SEQ_LEN, HEAD_DIM), lambda i: (0, i + heads)),
        pl.BlockSpec((SEQ_LEN, HEAD_DIM), lambda i: (0, 0)),
        pl.BlockSpec((SEQ_LEN, 1), lambda i: (0, 0)),
        pl.BlockSpec((1, HEAD_DIM), lambda i: (0, i)),
        pl.BlockSpec((None, SEQ_LEN, 1), lambda i: (i, 0, 0)),
        pl.BlockSpec(memory_space=pl.ANY),
    )


def attend(number, rows, parts, pre, value, invs, gains, tables, sides):
    width = value.shape[1]
    heads = width // HEAD_DIM
    head, later, whole, column, gain, lse, hbm = attention_specs(heads)
    low = jax.ShapeDtypeStruct((SEQ_LEN, width), LOW)
    results = call(
        functools.partial(attend_kernel, rows, parts, 1.0 / math.sqrt(HEAD_DIM), heads, sides),
        [pre, pre, value, *invs, *gains, *tables, *sides.operands],
        [head, later, head, column, column, gain, gain, whole, whole]
        + [hbm] * len(sides.operands),
        grid=(heads,),
        out_specs=[head, head, head, lse, *[hbm] * len(sides.out_shapes)],
        out_shape=[
            low,
            low,
            low,
            jax.ShapeDtypeStruct((heads, SEQ_LEN, 1), F32),
            *sides.out_shapes,
        ],
        scratch_shapes=[
            pltpu.VMEM((SEQ_LEN, HEAD_DIM), LOW),
            pltpu.VMEM((SEQ_LEN, HEAD_DIM), LOW),
            *sides.scratch,
        ],
        compiler_params=pltpu.CompilerParams(
            vmem_limit_bytes=40 * MIB, **sides.options(number)
        ),
        cost_estimate=pl.CostEstimate(
            flops=8 * heads * SEQ_LEN * SEQ_LEN * HEAD_DIM,
            bytes_accessed=16 * SEQ_LEN * width,
            transcendentals=heads * SEQ_LEN * SEQ_LEN,
        ),
        name="attend",
    )
    return *results[:4], *sides.results(results[4:])


def attend_back(
    number, rows, parts, rots, value, grad, lse_all, pre, invs, gains, tables, earlier, sides
):
    width = value.shape[1]
    heads = width // HEAD_DIM
    head, later, whole, column, gain, lse, hbm = attention_specs(heads)
    full = jax.ShapeDtypeStruct((SEQ_LEN, width), F32)
    low = jax.ShapeDtypeStruct((SEQ_LEN, width), LOW)
    gain_out = jax.ShapeDtypeStruct((1, width), F32)
    inner = jax.ShapeDtypeStruct((SEQ_LEN, 1), F32)
    results = call(
        functools.partial(
            attend_back_kernel, rows, parts, 1.0 / math.sqrt(HEAD_DIM), heads, sides
        ),
        [*rots, value, grad, lse_all, pre, pre, *invs, *gains, *tables, *sides.operands],
        [head, head, head, head, lse, head, later, column, column, gain, gain, whole, whole]
        + [hbm] * len(sides.operands),
        earlier,
        grid=(heads,),
        out_specs=[head, head, head, gain, gain, column, column, *[hbm] * len(sides.out_shapes)],
        out_shape=[full, full, low, gain_out, gain_out, inner, inner, *sides.out_shapes],
        scratch_shapes=[
            pltpu.VMEM((SEQ_LEN, HEAD_DIM), LOW),
            pltpu.VMEM((SEQ_LEN, HEAD_DIM), LOW),
            pltpu.VMEM((SEQ_LEN, HEAD_DIM), F32),
            pltpu.VMEM((SEQ_LEN, HEAD_DIM), F32),
            *sides.scratch,
        ],
        compiler_params=pltpu.CompilerParams(
            vmem_limit_bytes=48 * MIB, **sides.options(number)
        ),
        cost_estimate=pl.CostEstimate(
            flops=20 * heads * SEQ_LEN * SEQ_LEN * HEAD_DIM,
            bytes_accessed=32 * SEQ_LEN * width,
            transcendentals=heads * SEQ_LEN * SEQ_LEN,
        ),
        name="attend_back",
    )
    return *results[:7], *sides.results(results[7:])


def norm_back(grad_hat, values_hat, inverse, width):
    inner = jnp.sum(grad_hat * values_hat, axis=1, keepdims=True) / width
    return inverse * (grad_hat - values_hat * inner)


def layer(fsdp, tensor, *arguments):
    layer_input, query_weight, key_weight, value_weight, out_weight = arguments[:5]
    gate_weight, up_weight, down_weight = arguments[5:8]
    query_gain, key_gain, attn_gain, ffn_gain, out_cotangent = arguments[8:]
    rows_here, width = layer_input.shape
    head_cols = query_weight.shape[1]
    parts = SEQ_LEN // rows_here
    spans = tensor // parts
    rank = lax.axis_index("tensor")
    place, span = rank % parts, rank // parts

    def to_part(x, shift):
        pairs = [
            (s * parts + p, s * parts + (p + shift) % parts)
            for s in range(spans)
            for p in range(parts)
        ]
        return lax.ppermute(x, "tensor", pairs)

    def to_span(x, shift):
        pairs = [
            (s * parts + p, (s + shift) % spans * parts + p)
            for s in range(spans)
            for p in range(parts)
        ]
        return lax.ppermute(x, "tensor", pairs)

    def gather_shard(shard):
        return lax.all_gather(shard, "fsdp", axis=0, tiled=True)

    def product_others(pairs, earlier=()):
        return [product_sum(rows_here, p, pairs, LOW, earlier)[0] for p in range(1, parts)]

    def product_own(number, pairs, others, earlier=()):
        sides = Sides(Rows(parts, deliver=others))
        total, came = product_sum(rows_here, 0, pairs, F32, earlier, number, sides)
        return add_pieces(total, came)

    def add_pieces(total, came):
        for piece in came:
            total = total + piece.astype(F32)
        return total

    def sum_parts(x):
        total = x
        for p in range(1, parts):
            total = total + jnp.roll(to_part(x, p), p * rows_here, axis=0)
        return total

    def sum_all(x):
        for axis, size in (("fsdp", fsdp), ("tensor", tensor)):
            bit = 1
            while bit < size:
                x = x + lax.ppermute(x, axis, [(i, i ^ bit) for i in range(size)])
                bit *= 2
        return x

    same_core = [list(range(c, fsdp, 2)) for c in range(2)]

    def scatter(total):
        return lax.psum_scatter(
            total, "fsdp", scatter_dimension=0, tiled=True, axis_index_groups=same_core
        )

    def sum_spans(total, weights):
        split = total.reshape(total.shape[0], weights, spans, -1)
        result = split[:, :, 0].astype(F32)
        for s in range(1, spans):
            result = result + to_span(split[:, :, s], -s).astype(F32)
        return [result[:, w] for w in range(weights)]

    def own_columns(s):
        return ((span + spans - s) % spans * parts + place) * head_cols

    def gain_here(gain):
        return jnp.concatenate(
            [lax.dynamic_slice_in_dim(gain, own_columns(s), head_cols) for s in range(spans)]
        )[None, :]

    def gain_whole(part):
        whole = jnp.zeros((width,), F32)
        for s in range(spans):
            whole = lax.dynamic_update_slice_in_dim(
                whole, part[0, s * head_cols : (s + 1) * head_cols], own_columns(s), 0
            )
        return whole

    gate_up_shard = jnp.concatenate([gate_weight, up_weight], axis=1)
    down_shard = down_weight.T
    out_shard = out_weight.T
    cols = gate_weight.shape[1]
    shards, plan = [], []
    for s in range(spans):
        for w, shard in enumerate([query_weight, key_weight, value_weight, out_shard]):
            shards.append(shard)
            plan.append((w // 3, s, w % 3 * spans + s, False))
    (full_qkv, full_out), _, inputs = exchange(
        0,
        fsdp,
        parts,
        spans,
        shards,
        plan,
        sides=Sides(Rows(parts, gather=layer_input)),
    )
    gate_up_first = gather_shard(after(gate_up_shard, inputs))

    local = jnp.arange(SEQ_LEN)
    position = (place + parts - local // rows_here) % parts * rows_here + local % rows_here
    inverse = THETA ** (-jnp.arange(0, HEAD_DIM, 2).astype(F32) / HEAD_DIM)
    angles = position.astype(F32)[:, None] * inverse[None, :]
    cos, sin = jnp.cos(angles), jnp.sin(angles)
    tables = (jnp.concatenate([cos, cos], axis=1), jnp.concatenate([-sin, sin], axis=1))
    gains = (gain_here(query_gain), gain_here(key_gain))

    pre, value_low, query_sq, key_sq = project(inputs, full_qkv)
    squares = sum_parts(jnp.concatenate([query_sq, key_sq], axis=1))
    invs = lax.rsqrt(squares / width + EPSILON)
    invs = (invs[:, :1], invs[:, 1:])
    others_spans = range(1, spans)
    sides = Sides(Spans(parts, spans, [(gate_up_shard, 0, cols, spans - s) for s in others_spans]))
    attended, query_rot, key_rot, lse, gate_came = attend(
        13, rows_here, parts, pre, value_low, invs, gains, tables, sides
    )
    pairs = [(attended, full_out, 0)]
    others = product_others(pairs)
    sides = Sides(
        Rows(parts, deliver=others),
        Spans(parts, spans, [(gate_up_shard, 1, cols, spans - s) for s in others_spans]),
    )
    full_gate, _, came, up_came = exchange(
        1, fsdp, parts, spans, gate_came, [(s - 1, s, 0, True) for s in others_spans], sides
    )
    came, down_shard = lax.optimization_barrier((came, down_shard))
    full_down = [gather_shard(down_shard)]
    total = product_sum(rows_here, 0, pairs, F32, [*others, gate_up_first])[0]
    branch = add_pieces(total, came)
    branch_inv = lax.rsqrt(jnp.mean(branch * branch, axis=1, keepdims=True) + EPSILON)
    branch_hat = branch * branch_inv
    middle = layer_input.astype(F32) + branch_hat * attn_gain
    sides = Sides(
        Rows(parts, gather=middle.astype(LOW)),
        Spans(parts, spans, [(down_shard, 0, cols, spans - s) for s in others_spans]),
    )
    full_up, _, mixed, down_came = exchange(
        2, fsdp, parts, spans, up_came, [(s - 1, s, 0, True) for s in others_spans], sides
    )
    full_gate_up = [((gate_up_first, 0), (gate_up_first, 1))]
    full_gate_up += [((gate, 0), (up, 0)) for gate, up in zip(full_gate, full_up)]
    full_down += [gather_shard(piece) for piece in down_came]
    gates, uppers, hiddens = zip(
        *[feed_up(mixed, pair, cols, full_down[:1]) for pair in full_gate_up]
    )
    pairs = [(hidden, down, 0) for hidden, down in zip(hiddens, full_down)]
    second = product_own(3, pairs, product_others(pairs))
    second_inv = lax.rsqrt(jnp.mean(second * second, axis=1, keepdims=True) + EPSILON)
    second_hat = second * second_inv
    output = (middle + second_hat * ffn_gain).astype(LOW)

    grad_out = out_cotangent.astype(F32)
    ffn_gain_part = jnp.sum(grad_out * second_hat, axis=0)
    grad_second = norm_back(grad_out * ffn_gain, second_hat, second_inv, width)
    _, _, grad_rows = exchange(
        4, fsdp, parts, spans, sides=Sides(Rows(parts, gather=grad_second.astype(LOW)))
    )
    (now,) = weight_grad_half(5, fsdp, grad_rows, hiddens)
    down_terms = scatter(now)
    back, gate_up_grad = {}, {}
    for s in reversed(range(spans)):
        back[s] = feed_up_back(grad_rows, full_down[s], gates[s], uppers[s], [now])
        now = back[s][0]
        if s:
            (now,) = weight_grad_half(6, fsdp, mixed, back[s])
            gate_up_grad[s] = scatter(now)
    pairs = [
        (grad, *full) for s in range(spans) for grad, full in zip(back[s], full_gate_up[s])
    ]
    grad_mixed = product_own(7, pairs, product_others(pairs), [down_terms])
    grad_middle = grad_out + grad_mixed
    attn_gain_part = jnp.sum(grad_middle * branch_hat, axis=0)
    grad_branch = norm_back(grad_middle * attn_gain, branch_hat, branch_inv, width)
    sides = Sides(
        Rows(parts, gather=grad_branch.astype(LOW)),
        Spans(parts, spans, [(down_terms, s, cols, s) for s in others_spans]),
    )
    now, grad_branch_rows, down_came = weight_grad_half(8, fsdp, mixed, back[0], sides=sides)
    gate_up_grad[0] = scatter(now)
    grad_attended = nn(grad_branch_rows, full_out).astype(LOW)
    (
        query_gained,
        key_gained,
        grad_value,
        query_gain_part,
        key_gain_part,
        query_inner,
        key_inner,
        gate_came,
    ) = attend_back(
        12,
        rows_here,
        parts,
        (query_rot, key_rot),
        value_low,
        grad_attended,
        lse,
        pre,
        invs,
        gains,
        tables,
        [],
        Sides(Spans(parts, spans, [(gate_up_grad[s], 0, cols, s) for s in others_spans])),
    )
    down_grad = add_pieces(down_terms[:, :cols].astype(F32), down_came)
    (out_total,) = weight_grad_half(9, fsdp, grad_branch_rows, [attended], [grad_value])
    inners = sum_parts(jnp.concatenate([query_inner, key_inner], axis=1)) / width
    local_width = value_low.shape[1]
    grad_query = invs[0] * (query_gained - pre[:, :local_width] * invs[0] * inners[:, :1])
    grad_key = invs[1] * (key_gained - pre[:, local_width:] * invs[1] * inners[:, 1:])
    grad_qkv = jnp.concatenate(
        [grad_query.astype(LOW), grad_key.astype(LOW), grad_value], axis=1
    )
    pairs = [(grad_qkv, full_qkv, 0)]
    others = product_others(pairs, [out_total, gate_up_grad[0]])
    others[0], out_total = lax.optimization_barrier((others[0], out_total))
    out_terms = scatter(out_total)
    sides = Sides(
        Rows(parts, deliver=others),
        Spans(parts, spans, [(gate_up_grad[s], 1, cols, s) for s in others_spans]),
    )
    qkv_grad, came, up_came = grad_scatter(
        10, fsdp, parts, spans, inputs, grad_qkv, 3, [], sides
    )
    total = product_sum(rows_here, 0, pairs, F32, [qkv_grad])[0]
    input_grad = grad_middle + add_pieces(total, came)
    gate_grad = add_pieces(gate_up_grad[0][:, :cols].astype(F32), gate_came)
    up_grad = add_pieces(gate_up_grad[0][:, cols:].astype(F32), up_came)
    gain_grads = sum_all(
        jnp.stack(
            [gain_whole(query_gain_part), gain_whole(key_gain_part), attn_gain_part, ffn_gain_part]
        )
    )
    (out_grad,) = sum_spans(out_terms, 1)
    query_grad, key_grad, value_grad = jnp.split(qkv_grad, 3, axis=1)
    return (
        output,
        input_grad,
        query_grad,
        key_grad,
        value_grad,
        out_grad.T,
        gate_grad,
        up_grad,
        down_grad.T,
        *gain_grads,
    )


def solution(mesh):
    columns, rows = P("fsdp", "tensor"), P("tensor", "fsdp")
    tokens = P(("fsdp", "tensor"), None)
    weights = (columns, columns, columns, rows, columns, columns, rows)
    return jax.shard_map(
        functools.partial(layer, mesh.shape["fsdp"], mesh.shape["tensor"]),
        mesh=mesh,
        in_specs=(tokens, *weights, P(), P(), P(), P(), tokens),
        out_specs=(tokens, tokens, *weights, P(), P(), P(), P()),
        check_vma=False,
    )
```

```python
import functools
import math

import jax
import jax.numpy as jnp
from jax import lax
from jax.experimental import pallas as pl
from jax.experimental.pallas import tpu as pltpu
from jax.sharding import PartitionSpec as P

HEAD_DIM = 128
SEQ_LEN = 1024
EPSILON = 1e-06
THETA = 500000.0
BLOCK = 256
LOW = jnp.bfloat16
F32 = jnp.float32


def nn(a, b):
    return lax.dot_general(a, b, (((1,), (0,)), ((), ())), preferred_element_type=F32)


def nt(a, b):
    return lax.dot_general(a, b, (((1,), (1,)), ((), ())), preferred_element_type=F32)


def tn(a, b):
    return lax.dot_general(a, b, (((0,), (0,)), ((), ())), preferred_element_type=F32)


def after(x, *earlier):
    return lax.optimization_barrier((x, *earlier))[0]


def block_start(place, block, rows, parts):
    part = block * BLOCK // rows
    return pl.multiple_of(
        lax.rem(place + parts - part, parts) * rows + block * BLOCK % rows, BLOCK
    )


def masked(scores):
    row = lax.broadcasted_iota(jnp.int32, scores.shape, 0)
    col = lax.broadcasted_iota(jnp.int32, scores.shape, 1)
    return jnp.where(row + (scores.shape[1] - scores.shape[0]) >= col, scores, -1e30)


def attend_kernel(rows, parts, scale, heads, sides, *refs):
    query_ref, key_ref, value_ref, query_inv_ref, key_inv_ref = refs[:5]
    query_gain_ref, key_gain_ref, cos_ref, sin_ref = refs[5:9]
    side_refs, refs = refs[9 : 9 + len(sides.operands)], refs[9 + len(sides.operands) :]
    out_ref, query_rot_ref, key_rot_ref, lse_ref = refs[:4]
    side_outs, refs = refs[4 : 4 + len(sides.out_shapes)], refs[4 + len(sides.out_shapes) :]
    key_seq, value_seq = refs[:2]
    sides_at = (side_refs, side_outs, refs[2:])
    place = lax.rem(lax.axis_index("tensor"), parts)

    @pl.when(pl.program_id(0) == 0)
    def _():
        greet(sides.partners())

    sides.start_over(pl.program_id(0), heads, *sides_at)
    half = HEAD_DIM // 2
    for block in range(SEQ_LEN // BLOCK):
        here = pl.ds(block_start(place, block, rows, parts), BLOCK)
        there = pl.ds(block * BLOCK, BLOCK)
        cos, sin = cos_ref[here], sin_ref[here]
        key = key_ref[here] * key_inv_ref[here] * key_gain_ref[...]
        key = (key * cos + pltpu.roll(key, half, 1) * sin).astype(LOW)
        key_rot_ref[here] = key
        key_seq[there] = key
        value_seq[there] = value_ref[here]
        query = query_ref[here] * query_inv_ref[here] * query_gain_ref[...]
        query = (query * cos + pltpu.roll(query, half, 1) * sin).astype(LOW)
        query_rot_ref[here] = query
        span = (block + 1) * BLOCK
        scores = masked(nt(query, key_seq[:span]) * scale)
        top = jnp.max(scores, axis=1, keepdims=True)
        exps = jnp.exp(scores - top)
        total = jnp.sum(exps, axis=1, keepdims=True)
        weights = (exps * (1.0 / total)).astype(LOW)
        out_ref[here] = nn(weights, value_seq[:span]).astype(LOW)
        lse_ref[here] = top + jnp.log(total)

    @pl.when(pl.program_id(0) == heads - 1)
    def _():
        sides.finish(*sides_at)


def attend_back_kernel(rows, parts, scale, heads, sides, *refs):
    query_rot_ref, key_rot_ref, value_ref, grad_ref, lse_ref, query_ref, key_ref = refs[:7]
    query_inv_ref, key_inv_ref, query_gain_ref, key_gain_ref, cos_ref, sin_ref = refs[7:13]
    side_refs, refs = refs[13 : 13 + len(sides.operands)], refs[13 + len(sides.operands) :]
    query_out_ref, key_out_ref, value_out_ref = refs[:3]
    query_gain_out_ref, key_gain_out_ref, query_inner_ref, key_inner_ref = refs[3:7]
    side_outs, refs = refs[7 : 7 + len(sides.out_shapes)], refs[7 + len(sides.out_shapes) :]
    key_seq, value_seq, key_acc, value_acc = refs[:4]
    sides_at = (side_refs, side_outs, refs[4:])
    place = lax.rem(lax.axis_index("tensor"), parts)
    half = HEAD_DIM // 2
    count = SEQ_LEN // BLOCK

    @pl.when(pl.program_id(0) == 0)
    def _():
        if sides.jobs:
            greet(sides.partners())
        query_inner_ref[...] = jnp.zeros_like(query_inner_ref)
        key_inner_ref[...] = jnp.zeros_like(key_inner_ref)

    sides.start_over(pl.program_id(0), heads, *sides_at)

    def finish(grad, here, values_ref, inv_ref, gain_ref, out_ref, inner_ref):
        back = grad * cos_ref[here] - pltpu.roll(grad, half, 1) * sin_ref[here]
        hat = values_ref[here] * inv_ref[here]
        gained = back * gain_ref[...]
        out_ref[here] = gained
        inner_ref[here] += jnp.sum(gained * hat, axis=1, keepdims=True)
        return jnp.sum(back * hat, axis=0, keepdims=True)

    query_gain_sum = jnp.zeros((1, HEAD_DIM), F32)
    for block in range(count):
        here = pl.ds(block_start(place, block, rows, parts), BLOCK)
        there = pl.ds(block * BLOCK, BLOCK)
        key_seq[there] = key_rot_ref[here]
        value_seq[there] = value_ref[here]
        query, grad = query_rot_ref[here], grad_ref[here]
        span = (block + 1) * BLOCK
        scores = masked(nt(query, key_seq[:span]) * scale)
        probs = jnp.exp(scores - lse_ref[here])
        weights = probs.astype(LOW)
        grad_probs = nt(grad, value_seq[:span])
        delta = jnp.sum(probs * grad_probs, axis=1, keepdims=True)
        grad_scores = (probs * (grad_probs - delta) * scale).astype(LOW)
        value_part = tn(weights, grad)
        key_part = tn(grad_scores, query)
        past = block * BLOCK
        if block:
            key_acc[:past] += key_part[:past]
            value_acc[:past] += value_part[:past]
        key_acc[past:span] = key_part[past:]
        value_acc[past:span] = value_part[past:]
        query_gain_sum += finish(
            nn(grad_scores, key_seq[:span]),
            here,
            query_ref,
            query_inv_ref,
            query_gain_ref,
            query_out_ref,
            query_inner_ref,
        )
    query_gain_out_ref[...] = query_gain_sum
    key_gain_sum = jnp.zeros((1, HEAD_DIM), F32)
    for block in range(count):
        here = pl.ds(block_start(place, block, rows, parts), BLOCK)
        there = pl.ds(block * BLOCK, BLOCK)
        value_out_ref[here] = value_acc[there].astype(LOW)
        key_gain_sum += finish(
            key_acc[there],
            here,
            key_ref,
            key_inv_ref,
            key_gain_ref,
            key_out_ref,
            key_inner_ref,
        )
    key_gain_out_ref[...] = key_gain_sum

    @pl.when(pl.program_id(0) == heads - 1)
    def _():
        sides.finish(*sides_at)


MESH = pl.DeviceIdType.MESH
MIB = 2**20
CHUNKS = 4


def flip(index, bit):
    return index + bit - 2 * bit * lax.rem(lax.div(index, bit), 2)


def row_shares(rows, count):
    units = rows // 16
    sizes = [16 * (units // count + (i < units % count)) for i in range(count)]
    starts = [sum(sizes[:i]) for i in range(count)]
    return list(zip(starts, sizes))


def call(kernel, operands, in_specs, earlier=(), **options):
    count = len(operands)

    def body(*refs):
        kernel(*refs[:count], *refs[count + len(earlier) :])

    specs = [*in_specs, *[pl.BlockSpec(memory_space=pl.ANY)] * len(earlier)]
    return pl.pallas_call(body, in_specs=specs, **options)(*operands, *earlier)


def greet(partners):
    barrier = pltpu.get_barrier_semaphore()
    for partner in partners:
        pl.semaphore_signal(barrier, inc=1, device_id=partner, device_id_type=MESH)
    pl.semaphore_wait(barrier, len(partners))


def remote(src, dst, send_sem, recv_sem, **device):
    return pltpu.make_async_remote_copy(
        src_ref=src,
        dst_ref=dst,
        send_sem=send_sem,
        recv_sem=recv_sem,
        device_id=device,
        device_id_type=MESH,
    )


class Copies:
    def __init__(self, send_sems, recv_sems):
        self.send_sems, self.recv_sems = send_sems, recv_sems
        self.used = 0
        self.open = []
        self.moves = []

    def send(self, src, dst, **device):
        copy = remote(
            src, dst, self.send_sems.at[self.used], self.recv_sems.at[self.used], **device
        )
        self.used += 1
        copy.start()
        self.open.append(copy.wait_send)
        return copy

    def move(self, src, hold, dst):
        load = pltpu.make_async_copy(src, hold, self.send_sems.at[self.used])
        store = pltpu.make_async_copy(hold, dst, self.recv_sems.at[self.used])
        self.used += 1
        load.start()
        self.moves.append((load, store))

    def finish(self):
        for load, store in self.moves:
            load.wait()
            store.start()
        for wait in self.open:
            wait()
        for _, store in self.moves:
            store.wait()


class Rows:
    def __init__(self, parts, gather=None, deliver=None):
        self.parts, self.gather = parts, gather is not None
        self.operands = [gather if self.gather else deliver]
        rows, width = self.operands[0].shape
        self.rows = rows if self.gather else rows // parts
        self.chunk = self.rows // CHUNKS
        count = parts if self.gather else parts - 1
        self.out_shapes = [jax.ShapeDtypeStruct((count, self.rows, width), LOW)]
        count = CHUNKS * parts
        self.scratch = [pltpu.SemaphoreType.DMA((count,)), pltpu.SemaphoreType.DMA((count,))]
        if self.gather:
            self.scratch.append(pltpu.VMEM((rows, width), LOW))

    def ranks(self):
        rank = lax.axis_index("tensor")
        place = lax.rem(rank, self.parts)
        shifts = range(1, self.parts)
        if not self.gather:
            shifts = [self.parts - p for p in shifts]
        return [rank - place + lax.rem(place + p, self.parts) for p in shifts]

    def partners(self):
        return [{"tensor": rank} for rank in self.ranks()]

    def copies(self, chunks, refs, outs, send_sems, recv_sems, hold=None):
        made = []
        for chunk in chunks:
            for i, rank in enumerate(self.ranks()):
                first = 0 if self.gather else (i + 1) * self.rows
                src = refs[0].at[pl.ds(first + chunk * self.chunk, self.chunk)]
                dst = outs[0].at[i + 1] if self.gather else outs[0].at[i]
                dst = dst.at[pl.ds(chunk * self.chunk, self.chunk)]
                sem = CHUNKS * i + chunk
                made.append(
                    remote(src, dst, send_sems.at[sem], recv_sems.at[sem], tensor=rank)
                )
        return made

    def load(self, refs, outs, send_sems, recv_sems, hold):
        return pltpu.make_async_copy(refs[0], hold, send_sems.at[CHUNKS * self.parts - 1])

    def store(self, refs, outs, send_sems, recv_sems, hold):
        return pltpu.make_async_copy(hold, outs[0].at[0], recv_sems.at[CHUNKS * self.parts - 1])

    def start(self, chunk, *where):
        if self.gather and chunk == 0:
            self.load(*where).start()
        for copy in self.copies([chunk], *where):
            copy.start()

    def finish(self, *where):
        if self.gather:
            self.load(*where).wait()
            self.store(*where).start()
            self.store(*where).wait()
        for copy in self.copies(range(CHUNKS), *where):
            copy.wait()

    def results(self, outs):
        out = outs[0]
        if self.gather:
            return out.reshape(-1, out.shape[2])
        return [out[i] for i in range(self.parts - 1)]


class Spans:
    def __init__(self, parts, spans, terms):
        self.parts, self.spans, self.terms = parts, spans, terms
        self.operands = [array for array, *_ in terms]
        self.out_shapes = [
            jax.ShapeDtypeStruct((array.shape[0], width), LOW) for array, _, width, _ in terms
        ]
        count = CHUNKS * max(1, len(terms))
        self.scratch = [pltpu.SemaphoreType.DMA((count,)), pltpu.SemaphoreType.DMA((count,))]

    def rank(self, back):
        rank = lax.axis_index("tensor")
        place, span = lax.rem(rank, self.parts), lax.div(rank, self.parts)
        return lax.rem(span + self.spans - back, self.spans) * self.parts + place

    def partners(self):
        return [{"tensor": self.rank(s)} for s in range(1, self.spans)]

    def copies(self, chunks, refs, outs, send_sems, recv_sems):
        made = []
        for chunk in chunks:
            for i, (ref, out, (array, run, width, back)) in enumerate(zip(refs, outs, self.terms)):
                size = array.shape[0] // CHUNKS
                rows, sem = pl.ds(chunk * size, size), CHUNKS * i + chunk
                made.append(
                    remote(
                        ref.at[rows, pl.ds(run * width, width)],
                        out.at[rows],
                        send_sems.at[sem],
                        recv_sems.at[sem],
                        tensor=self.rank(back),
                    )
                )
        return made

    def start(self, chunk, *where):
        for copy in self.copies([chunk], *where):
            copy.start()

    def finish(self, *where):
        for copy in self.copies(range(CHUNKS), *where):
            copy.wait()

    def results(self, outs):
        return list(outs)


class SumAll:
    def __init__(self, fsdp, tensor, array):
        self.operands = [array]
        self.out_shapes = [jax.ShapeDtypeStruct(array.shape, F32)]
        self.turns = [
            (axis, 1 << b)
            for axis, size in (("fsdp", fsdp), ("tensor", tensor))
            for b in range(size.bit_length() - 1)
        ]
        count = len(self.turns)
        self.scratch = [
            pltpu.SemaphoreType.DMA((count + 1,)),
            pltpu.SemaphoreType.DMA((count,)),
            pltpu.VMEM(array.shape, F32),
            pltpu.VMEM((count, *array.shape), F32),
        ]

    def partners(self):
        return [{axis: flip(lax.axis_index(axis), bit)} for axis, bit in self.turns]

    def copy(self, turn, refs, outs, send_sems, recv_sems, total, came):
        axis, bit = self.turns[turn]
        device = {axis: flip(lax.axis_index(axis), bit)}
        return remote(total, came.at[turn], send_sems.at[turn], recv_sems.at[turn], **device)

    def take(self, turn, *where):
        self.copy(turn, *where).wait()
        total, came = where[-2:]
        total[...] += came[turn]

    def start(self, chunk, *where):
        refs, _, send_sems, _, total, _ = where
        if chunk == 0:
            load = pltpu.make_async_copy(refs[0], total, send_sems.at[len(self.turns)])
            load.start()
            load.wait()
        elif chunk < len(self.turns):
            self.take(chunk - 1, *where)
        if chunk < len(self.turns):
            self.copy(chunk, *where).start()

    def finish(self, *where):
        _, outs, send_sems, _, total, _ = where
        count = len(self.turns)
        for turn in range(min(CHUNKS, count) - 1, count):
            self.take(turn, *where)
            if turn + 1 < count:
                self.copy(turn + 1, *where).start()
        store = pltpu.make_async_copy(total, outs[0], send_sems.at[count])
        store.start()
        store.wait()

    def results(self, outs):
        return outs[0]


class Sides:
    def __init__(self, *jobs):
        self.jobs = jobs
        self.operands = [x for job in jobs for x in job.operands]
        self.out_shapes = [x for job in jobs for x in job.out_shapes]
        self.scratch = [x for job in jobs for x in job.scratch]

    def partners(self):
        return [partner for job in self.jobs for partner in job.partners()]

    def each(self, refs, outs, scratch):
        for job in self.jobs:
            counts = len(job.operands), len(job.out_shapes), len(job.scratch)
            yield job, (refs[: counts[0]], outs[: counts[1]], *scratch[: counts[2]])
            refs, outs, scratch = refs[counts[0] :], outs[counts[1] :], scratch[counts[2] :]

    def start(self, chunk, *where):
        for job, own in self.each(*where):
            job.start(chunk, *own)

    def start_over(self, step, steps, *where):
        for job, own in self.each(*where):
            stride = steps // CHUNKS
            if stride < 2 and isinstance(job, Spans):
                stride = 0
            elif stride == 0:
                stride = 1
            for chunk in range(CHUNKS):

                @pl.when(step == min(chunk * stride, steps - 1))
                def _(job=job, own=own, chunk=chunk):
                    job.start(chunk, *own)

    def finish(self, *where):
        for job, own in self.each(*where):
            job.finish(*own)

    def results(self, outs):
        return [job.results(own) for job, (_, own, *_) in self.each([], outs, [])]

    def options(self, number):
        return {"collective_id": number, "has_side_effects": True} if self.jobs else {}


NO_SIDES = Sides()


def exchange_kernel(fsdp, parts, spans, plan, counts, *refs):
    sides, shard_count, send_count, full_count = counts
    rows_count = len(sides.operands)
    rows_refs, refs = refs[:rows_count], refs[rows_count:]
    shard_refs, refs = refs[:shard_count], refs[shard_count:]
    span_refs, refs = refs[:send_count], refs[send_count:]
    full_refs, refs = refs[:full_count], refs[full_count:]
    span_outs, refs = refs[:send_count], refs[send_count:]
    side_outs, refs = refs[: len(sides.out_shapes)], refs[len(sides.out_shapes) :]
    hold_refs, refs = refs[: len(plan)], refs[len(plan) :]
    sides_at = (rows_refs, side_outs, refs[:-2])
    copies = Copies(*refs[-2:])
    me, rank = lax.axis_index("fsdp"), lax.axis_index("tensor")
    place, span = lax.rem(rank, parts), lax.div(rank, parts)
    bits = [1 << b for b in range(1, fsdp.bit_length() - 1)]
    span_ranks = [lax.rem(span + s, spans) * parts + place for s in range(1, spans)]
    partners = [{"fsdp": flip(me, bit)} for bit in [1, *bits]] if plan else []
    partners += sides.partners()
    if send_count or any(s and not here for _, s, _, here in plan):
        partners += [{"tensor": r} for r in span_ranks]
    greet(partners)

    def slot(job, mask, share=None):
        group, s, position, _ = plan[job]
        which = me
        for bit in [1, *bits]:
            if mask & bit:
                which = flip(which, bit)
        cols = shard_refs[job].shape[1]
        ref = full_refs[group].at[which, :, pl.ds(position * cols, cols)]
        return ref if share is None else ref.at[pl.ds(*share)]

    depth = shard_refs[0].shape[0] if plan else 16
    shares = row_shares(depth, len(bits))
    jobs = range(len(plan))
    away = [s and not here for _, s, _, here in plan]
    for chunk in range(CHUNKS // 2):
        sides.start(chunk, *sides_at)
    from_span = {
        job: copies.send(shard_refs[job], slot(job, 0), tensor=span_ranks[plan[job][1] - 1])
        for job in jobs
        if away[job]
    }
    for chunk in range(CHUNKS // 2, CHUNKS):
        sides.start(chunk, *sides_at)
    over = []
    for ref, out in zip(span_refs, span_outs):
        for s, r in enumerate(span_ranks):
            over.append(copies.send(ref, out.at[s], tensor=r))
    for job in jobs:
        if not away[job]:
            copies.move(shard_refs[job], hold_refs[job], slot(job, 0))

    arriving = {}
    held = {(job, p): [0] for job in jobs for p in range(len(shares))}

    def source(job, mask, share):
        if mask == 0 and not away[job]:
            return shard_refs[job].at[pl.ds(*share)]
        return slot(job, mask, share)

    def send_step(job, step):
        for p, share in enumerate(shares):
            bit = bits[(p + step) % len(bits)]
            for mask in held[job, p]:
                arriving[job, p, mask | bit] = copies.send(
                    source(job, mask, share), slot(job, mask, share), fsdp=flip(me, bit)
                )

    def take_step(job, step):
        for p in range(len(shares)):
            bit = bits[(p + step) % len(bits)]
            came = [mask | bit for mask in held[job, p]]
            for mask in came:
                arriving[job, p, mask].wait_recv()
            held[job, p] += came

    for step in range(len(bits) + 1):
        for job in jobs:
            if step == 0 and away[job]:
                from_span[job].wait_recv()
            if step:
                take_step(job, step - 1)
            if step < len(bits):
                send_step(job, step)
            else:
                for mask in range(0, fsdp, 2):
                    whole = (0, depth)
                    over.append(
                        copies.send(
                            source(job, mask, whole), slot(job, mask), fsdp=flip(me, 1)
                        )
                    )
    for copy in over:
        copy.wait_recv()
    copies.finish()
    sides.finish(*sides_at)


def exchange(number, fsdp, parts, spans, shards=(), plan=(), sides=NO_SIDES, sends=(), earlier=()):
    bits = fsdp.bit_length() - 2
    per_job = 2 + bits * (2**bits - 1) + 2**bits
    count = len(plan) * per_job + len(sends) * spans + 1
    hbm = pl.BlockSpec(memory_space=pl.ANY)
    full_count = 1 + max([group for group, *_ in plan], default=-1)
    widths = [0] * full_count
    for shard, (group, *_) in zip(shards, plan):
        widths[group] += shard.shape[1]
    depth = shards[0].shape[0] if plan else 0
    outs = [jax.ShapeDtypeStruct((fsdp, depth, width), LOW) for width in widths]
    outs += [jax.ShapeDtypeStruct((spans - 1, *x.shape), LOW) for x in sends]
    inputs = [*shards, *sends]
    scratch = [pltpu.SemaphoreType.DMA((count,)), pltpu.SemaphoreType.DMA((count,))]
    inputs = [*sides.operands, *inputs]
    outs += sides.out_shapes
    scratch = [*sides.scratch, *scratch]
    scratch = [
        *[pltpu.VMEM(x.shape if here or not s else (16, 128), LOW) for x, (_, s, _, here) in zip(shards, plan)],
        *scratch,
    ]
    results = call(
        functools.partial(
            exchange_kernel,
            fsdp,
            parts,
            spans,
            plan,
            (sides, len(shards), len(sends), full_count),
        ),
        inputs,
        [hbm] * len(inputs),
        earlier,
        out_shape=outs,
        out_specs=[hbm] * len(outs),
        scratch_shapes=scratch,
        compiler_params=pltpu.CompilerParams(collective_id=number, has_side_effects=True),
        name="exchange",
    )
    full = [r.reshape(fsdp * depth, -1) for r in results[:full_count]]
    came = results[full_count : full_count + len(sends)]
    return full, came, *sides.results(results[full_count + len(sends) :])


def sum_kernel(pairs, own, sides, steps, *refs):
    step = pl.program_id(0)
    count = 2 * pairs + len(sides.operands)
    own_ref, low_ref, outs = refs[count], refs[count + 1], refs[count + 2 :]
    outs, scratch = outs[: len(sides.out_shapes)], outs[len(sides.out_shapes) :]
    sides_at = (refs[2 * pairs : count], outs, scratch)
    if sides.jobs:

        @pl.when(step == 0)
        def _():
            greet(sides.partners())

    sides.start_over(step, steps, *sides_at)
    total = None
    for i in range(pairs):
        term = nt(refs[2 * i][...], refs[2 * i + 1][...])
        total = term if total is None else total + term
    own_ref[...] = total[:own]
    low_ref[...] = total.astype(LOW)
    if sides.jobs:

        @pl.when(step == steps - 1)
        def _():
            sides.finish(*sides_at)


def product_sum(parts, pairs, earlier=(), number=None, sides=NO_SIDES):
    rows, width = pairs[0][0].shape[0], pairs[0][2].shape[0]
    own = rows // parts
    tile = min(512 if rows * sum(depth for *_, depth in pairs) < 5 * MIB else 256, width)
    specs, operands, flops = [], [], 0
    for a, a_run, b, b_run, depth in pairs:
        specs.append(pl.BlockSpec((rows, depth), lambda j, run=a_run: (0, run)))
        specs.append(pl.BlockSpec((tile, depth), lambda j, run=b_run: (j, run)))
        operands += [a, b]
        flops += 2 * rows * depth * width
    hbm = pl.BlockSpec(memory_space=pl.ANY)
    steps = width // tile
    results = call(
        functools.partial(sum_kernel, len(pairs), own, sides, steps),
        [*operands, *sides.operands],
        [*specs, *[hbm] * len(sides.operands)],
        earlier,
        grid=(steps,),
        out_specs=[
            pl.BlockSpec((own, tile), lambda j: (0, j)),
            pl.BlockSpec((rows, tile), lambda j: (0, j)),
            *[hbm] * len(sides.out_shapes),
        ],
        out_shape=[
            jax.ShapeDtypeStruct((own, width), F32),
            jax.ShapeDtypeStruct((rows, width), LOW),
            *sides.out_shapes,
        ],
        scratch_shapes=sides.scratch,
        compiler_params=pltpu.CompilerParams(
            vmem_limit_bytes=56 * MIB, **sides.options(number)
        ),
        cost_estimate=pl.CostEstimate(
            flops=flops, bytes_accessed=flops // rows + 4 * rows * width, transcendentals=0
        ),
        name="product_sum",
    )
    return *results[:2], *sides.results(results[2:])


def up_kernel(spans, tiles, sides, *refs):
    mixed_ref, weight_refs = refs[0], refs[1 : 1 + 2 * spans]
    refs = refs[1 + 2 * spans :]
    side_refs, refs = refs[: len(sides.operands)], refs[len(sides.operands) :]
    gate_ref, upper_ref, hidden_ref, outs = *refs[:3], refs[3:]
    outs, scratch = outs[: len(sides.out_shapes)], outs[len(sides.out_shapes) :]
    sides_at = (side_refs, outs, scratch)
    step = pl.program_id(0)
    if sides.jobs:

        @pl.when(step == 0)
        def _():
            greet(sides.partners())

    sides.start_over(step, spans * tiles, *sides_at)
    for s in range(spans):

        @pl.when(jnp.logical_and(step >= s * tiles, step < (s + 1) * tiles))
        def _(s=s):
            gate = nn(mixed_ref[...], weight_refs[2 * s][...])
            upper = nn(mixed_ref[...], weight_refs[2 * s + 1][...])
            gate_ref[...] = gate
            upper_ref[...] = upper
            hidden_ref[...] = (gate * jax.nn.sigmoid(gate) * upper).astype(LOW)

    if sides.jobs:

        @pl.when(step == spans * tiles - 1)
        def _():
            sides.finish(*sides_at)


def feed_up(mixed, gate_ups, cols, number=None, sides=NO_SIDES):
    rows, depth = mixed.shape
    spans = len(gate_ups)
    tile = min(512, cols)
    tiles = cols // tile
    hbm = pl.BlockSpec(memory_space=pl.ANY)
    out = pl.BlockSpec((rows, tile), lambda j: (0, j))
    operands, specs = [mixed], [pl.BlockSpec((rows, depth), lambda j: (0, 0))]
    for s, pair in enumerate(gate_ups):
        for array, run in pair:
            operands.append(array)
            specs.append(
                pl.BlockSpec(
                    (depth, tile),
                    lambda j, s=s, run=run: (0, jnp.clip(j - s * tiles, 0, tiles - 1) + run * tiles),
                )
            )
    whole = (rows, spans * cols)
    results = call(
        functools.partial(up_kernel, spans, tiles, sides),
        [*operands, *sides.operands],
        [*specs, *[hbm] * len(sides.operands)],
        grid=(spans * tiles,),
        out_specs=[out, out, out, *[hbm] * len(sides.out_shapes)],
        out_shape=[
            jax.ShapeDtypeStruct(whole, F32),
            jax.ShapeDtypeStruct(whole, F32),
            jax.ShapeDtypeStruct(whole, LOW),
            *sides.out_shapes,
        ],
        scratch_shapes=sides.scratch,
        compiler_params=pltpu.CompilerParams(
            vmem_limit_bytes=56 * MIB, **sides.options(number)
        ),
        cost_estimate=pl.CostEstimate(
            flops=4 * rows * depth * spans * cols,
            bytes_accessed=4 * depth * spans * cols + 10 * rows * spans * cols,
            transcendentals=rows * spans * cols,
        ),
        name="feed_up",
    )
    return *results[:3], *sides.results(results[3:])


def up_back_kernel(spans, tiles, sides, *refs):
    steps = spans * tiles
    grad_ref, down_refs, refs = refs[0], refs[1 : 1 + spans], refs[1 + spans :]
    gate_ref, upper_ref, refs = refs[0], refs[1], refs[2:]
    side_refs, refs = refs[: len(sides.operands)], refs[len(sides.operands) :]
    gate_out_ref, up_out_ref, outs = refs[0], refs[1], refs[2:]
    outs, scratch = outs[: len(sides.out_shapes)], outs[len(sides.out_shapes) :]
    sides_at = (side_refs, outs, scratch)
    step = pl.program_id(0)
    if sides.jobs:

        @pl.when(step == 0)
        def _():
            greet(sides.partners())

    sides.start_over(step, steps, *sides_at)
    for s, down_ref in enumerate(down_refs):

        @pl.when(jnp.logical_and(step >= s * tiles, step < (s + 1) * tiles))
        def _(down_ref=down_ref):
            grad = nn(grad_ref[...], down_ref[...])
            gate = gate_ref[...]
            sigmoid = jax.nn.sigmoid(gate)
            scaled = grad * sigmoid
            slope = 1.0 + gate * (1.0 - sigmoid)
            up_out_ref[...] = (scaled * gate).astype(LOW)
            gate_out_ref[...] = (scaled * upper_ref[...] * slope).astype(LOW)

    if sides.jobs:

        @pl.when(step == steps - 1)
        def _():
            sides.finish(*sides_at)


def feed_up_back(grad_rows, down, gate, upper, earlier=(), number=None, sides=NO_SIDES):
    rows, depth = grad_rows.shape
    downs, spans = [down], 1
    tile = min(512, downs[0].shape[1])
    tiles = downs[0].shape[1] // tile
    cols = spans * tiles * tile
    hbm = pl.BlockSpec(memory_space=pl.ANY)
    spec = pl.BlockSpec((rows, tile), lambda j: (0, j))
    out = jax.ShapeDtypeStruct((rows, cols), LOW)
    results = call(
        functools.partial(up_back_kernel, spans, tiles, sides),
        [grad_rows, *downs, gate, upper, *sides.operands],
        [
            pl.BlockSpec((rows, depth), lambda j: (0, 0)),
            *[
                pl.BlockSpec(
                    (depth, tile), lambda j, s=s: (0, jnp.clip(j - s * tiles, 0, tiles - 1))
                )
                for s in range(spans)
            ],
            spec,
            spec,
            *[hbm] * len(sides.operands),
        ],
        earlier,
        grid=(cols // tile,),
        out_specs=[spec, spec, *[hbm] * len(sides.out_shapes)],
        out_shape=[out, out, *sides.out_shapes],
        scratch_shapes=sides.scratch,
        compiler_params=pltpu.CompilerParams(
            vmem_limit_bytes=52 * MIB, **sides.options(number)
        ),
        cost_estimate=pl.CostEstimate(
            flops=2 * rows * depth * cols,
            bytes_accessed=2 * depth * cols + 12 * rows * cols,
            transcendentals=rows * cols,
        ),
        name="feed_up_back",
    )
    return *results[:2], *sides.results(results[2:])


def weight_grad_kernel(fsdp, chunks, tiles, sides, *refs):
    x_refs, refs = refs[:chunks], refs[chunks:]
    grad_refs, refs = refs[: chunks * len(tiles)], refs[chunks * len(tiles) :]
    rows = x_refs[0].shape[0]
    count, outs = len(sides.operands), len(sides.out_shapes)
    side_refs, out_ref, refs = refs[:count], refs[count], refs[count + 1 :]
    side_outs, refs = refs[:outs], refs[outs:]
    x_half, sent, came, send_sems, recv_sems = refs[:5]
    sides_at = (side_refs, side_outs, refs[5:])
    me = lax.axis_index("fsdp")
    core = lax.rem(me, 2)
    total_tiles = sum(tiles)
    depth = x_refs[0].shape[1] // fsdp
    step = pl.program_id(0)

    def load(which):
        for c, x_ref in enumerate(x_refs):
            for i in range(fsdp // 2):
                first = pl.multiple_of((2 * i + which) * depth, depth)
                x_half[c * rows : (c + 1) * rows, i * depth : (i + 1) * depth] = x_ref[
                    :, pl.ds(first, depth)
                ]

    def product(entry):
        total = None
        for c, ref in enumerate(grad_refs[entry * chunks : (entry + 1) * chunks]):
            term = tn(x_half[c * rows : (c + 1) * rows], ref[...])
            total = term if total is None else total + term
        return total

    def copy(tile):
        slot = lax.rem(tile, 2)
        return remote(
            sent.at[slot], came.at[tile], send_sems.at[slot], recv_sems.at[tile], fsdp=flip(me, 1)
        )

    @pl.when(step == 0)
    def _():
        load(1 - core)
        greet([{"fsdp": flip(me, 1)}, *sides.partners()])

    sides.start_over(step, 2 * total_tiles, *sides_at)

    @pl.when(step == total_tiles)
    def _():
        load(core)

    @pl.when(jnp.logical_and(step >= 2, step < total_tiles))
    def _():
        copy(step - 2).wait_send()

    tile = lax.rem(step, total_tiles)
    first = 0
    for entry, count in enumerate(tiles):
        here = jnp.logical_and(tile >= first, tile < first + count)

        @pl.when(jnp.logical_and(here, step < total_tiles))
        def _(entry=entry):
            sent[lax.rem(step, 2)] = product(entry).astype(LOW)

        @pl.when(jnp.logical_and(here, step >= total_tiles))
        def _(entry=entry):
            total = product(entry)
            copy(tile).wait_recv()
            out_ref[...] = (total + came[tile].astype(F32)).astype(LOW)

        first += count

    @pl.when(step < total_tiles)
    def _():
        copy(step).start()

    @pl.when(step == 2 * total_tiles - 1)
    def _():
        for last in range(max(0, total_tiles - 2), total_tiles):
            copy(last).wait_send()
        sides.finish(*sides_at)


def weight_grad_half(number, fsdp, xs, grads, earlier=(), sides=NO_SIDES):
    chunks = len(xs)
    count, width = xs[0].shape
    tile = math.gcd(1024, *[cols for _, _, cols in grads])
    tiles = [cols // tile for _, _, cols in grads]
    total_tiles = sum(tiles)
    firsts = [sum(tiles[:i]) for i in range(len(tiles))]
    cols = tile * total_tiles

    def grad_spec(first, runs, base):
        return pl.BlockSpec(
            (count, tile),
            lambda j: (0, base + jnp.clip(lax.rem(j, total_tiles) - first, 0, runs - 1)),
        )

    hbm = pl.BlockSpec(memory_space=pl.ANY)
    operands = [*xs, *[array for arrays, _, _ in grads for array in arrays]]
    specs = [pl.BlockSpec((count, width), lambda j: (0, 0))] * chunks
    for first, runs, (_, start, _) in zip(firsts, tiles, grads):
        specs += [grad_spec(first, runs, start // tile)] * chunks
    outs = [jax.ShapeDtypeStruct((width // 2, cols), LOW)]
    out_specs = [pl.BlockSpec((width // 2, tile), lambda j: (0, jnp.maximum(j - total_tiles, 0)))]
    scratch = [
        pltpu.VMEM((chunks * count, width // 2), LOW),
        pltpu.VMEM((2, width // 2, tile), LOW),
        pltpu.VMEM((total_tiles, width // 2, tile), LOW),
        pltpu.SemaphoreType.DMA((2,)),
        pltpu.SemaphoreType.DMA((total_tiles,)),
    ]
    operands += sides.operands
    specs += [hbm] * len(sides.operands)
    outs += sides.out_shapes
    out_specs += [hbm] * len(sides.out_shapes)
    scratch += sides.scratch
    results = call(
        functools.partial(weight_grad_kernel, fsdp, chunks, tiles, sides),
        operands,
        specs,
        earlier,
        grid=(2 * total_tiles,),
        out_specs=out_specs,
        out_shape=outs,
        scratch_shapes=scratch,
        compiler_params=pltpu.CompilerParams(
            collective_id=number, has_side_effects=True, vmem_limit_bytes=56 * MIB
        ),
        cost_estimate=pl.CostEstimate(
            flops=2 * chunks * count * width * cols,
            bytes_accessed=chunks * (2 * count * width + 4 * count * cols) + width * cols,
            transcendentals=0,
        ),
        name="weight_grad",
    )
    return results[0], *sides.results(results[1:])


def column_shares(cols, count):
    return [(8 * start, 8 * size) for start, size in row_shares(cols // 8, count)]


def grad_scatter_kernel(fsdp, parts, spans, tiles, sides, *refs):
    x_ref, grad_ref, refs = refs[0], refs[1], refs[2:]
    count, outs = len(sides.operands), len(sides.out_shapes)
    side_refs, out_ref, refs = refs[:count], refs[count], refs[count + 1 :]
    side_outs, refs = refs[:outs], refs[outs:]
    x_half, sent, held, send_sems, recv_sems, chip_sends, chip_recvs = refs[:7]
    span_came, span_sends, span_recvs, refs = *refs[7:10], refs[10:]
    bits = [1 << b for b in range(fsdp.bit_length() - 2)]
    turns = len(bits)
    chip_came, side_scratch = refs[: turns * turns], refs[turns * turns :]
    sides_at = (side_refs, side_outs, side_scratch)
    me, rank = lax.axis_index("fsdp"), lax.axis_index("tensor")
    core, chip = lax.rem(me, 2), lax.div(me, 2)
    place, span = lax.rem(rank, parts), lax.div(rank, parts)
    depth = x_ref.shape[1] // fsdp
    tile_cols = grad_ref.shape[1]
    own_cols = tile_cols // spans
    shares = column_shares(tile_cols, turns)
    step = pl.program_id(0)

    def load(which):
        for i in range(fsdp // 2):
            first = pl.multiple_of((2 * i + which) * depth, depth)
            x_half[:, i * depth : (i + 1) * depth] = x_ref[:, pl.ds(first, depth)]

    def core_copy(tile):
        slot = lax.rem(tile, 2)
        return remote(
            sent.at[slot], held.at[tile], send_sems.at[slot], recv_sems.at[tile], fsdp=flip(me, 1)
        )

    def turned(mask):
        which = chip
        for bit in bits:
            if mask & bit:
                which = flip(which, bit)
        return pl.ds(pl.multiple_of(which * depth, depth), depth)

    def swaps(share, turn):
        order = [bits[(share + i) % turns] for i in range(turns)]
        stay = [0]
        for bit in order[turn + 1 :]:
            stay += [mask | bit for mask in stay]
        return order[turn], [(mask | order[turn], mask, i) for i, mask in enumerate(stay)]

    def chip_copies(tile, turn):
        made, number = [], 0
        for share, (start, size) in enumerate(shares):
            for earlier in range(turns):
                bit, moves = swaps(share, earlier)
                for goes, _, slot in moves:
                    if earlier == turn:
                        made.append(
                            remote(
                                held.at[tile, turned(goes), pl.ds(start, size)],
                                chip_came[share * turns + turn].at[tile, slot],
                                chip_sends.at[tile, number],
                                chip_recvs.at[tile, number],
                                fsdp=flip(me, 2 * bit),
                            )
                        )
                    number += 1
        return made

    def span_copies(tile):
        return [
            remote(
                held.at[tile, turned(0), pl.ds(s * own_cols, own_cols)],
                span_came.at[tile, s - 1],
                span_sends.at[tile, s - 1],
                span_recvs.at[tile, s - 1],
                tensor=lax.rem(span + spans - s, spans) * parts + place,
            )
            for s in range(1, spans)
        ]

    @pl.when(step == 0)
    def _():
        load(1 - core)
        partners = [{"fsdp": flip(me, 1)}] + [{"fsdp": flip(me, 2 * bit)} for bit in bits]
        partners += [
            {"tensor": lax.rem(span + s, spans) * parts + place} for s in range(1, spans)
        ]
        side_partners = sides.partners()
        greet(partners + side_partners)

    sides.start_over(step, 2 * tiles, *sides_at)

    @pl.when(step == tiles)
    def _():
        load(core)

    @pl.when(step < tiles)
    def _():
        @pl.when(step >= 2)
        def _():
            core_copy(step - 2).wait_send()

        sent[lax.rem(step, 2)] = tn(x_half[...], grad_ref[...]).astype(LOW)
        core_copy(step).start()

    @pl.when(jnp.logical_and(step >= tiles, step < 2 * tiles))
    def _():
        tile = step - tiles
        total = tn(x_half[...], grad_ref[...])
        core_copy(tile).wait_recv()
        held[tile] = (total + held[tile].astype(F32)).astype(LOW)
        for copy in chip_copies(tile, 0):
            copy.start()

    for turn in range(1, turns + 2):
        tile = step - tiles - turn

        @pl.when(jnp.logical_and(tile >= 0, tile < tiles))
        def _(turn=turn, tile=tile):
            if turn <= turns:
                for copy in chip_copies(tile, turn - 1):
                    copy.wait()
                for share, (start, size) in enumerate(shares):
                    _, moves = swaps(share, turn - 1)
                    for _, stays, slot in moves:
                        where = (tile, turned(stays), pl.ds(start, size))
                        came = chip_came[share * turns + turn - 1][tile, slot]
                        held[where] = (held[where].astype(F32) + came.astype(F32)).astype(LOW)
                for copy in chip_copies(tile, turn) if turn < turns else span_copies(tile):
                    copy.start()
            else:
                total = held[tile, turned(0), :own_cols].astype(F32)
                for s, copy in enumerate(span_copies(tile)):
                    copy.wait()
                    total = total + span_came[tile, s].astype(F32)
                out_ref[...] = total

    @pl.when(step == 2 * tiles + turns)
    def _():
        for last in range(max(0, tiles - 2), tiles):
            core_copy(last).wait_send()
        sides.finish(*sides_at)


def grad_scatter(number, fsdp, parts, spans, x, grads, tiles, earlier=(), sides=NO_SIDES):
    count, width = x.shape
    depth = width // fsdp
    tile = grads.shape[1] // tiles
    own = tile // spans
    turns = fsdp.bit_length() - 2
    shares = column_shares(tile, turns)
    hbm = pl.BlockSpec(memory_space=pl.ANY)
    swapped = turns * (2**turns - 1)
    results = call(
        functools.partial(grad_scatter_kernel, fsdp, parts, spans, tiles, sides),
        [x, grads, *sides.operands],
        [
            pl.BlockSpec((count, width), lambda j: (0, 0)),
            pl.BlockSpec(
                (count, tile),
                lambda j: (0, jnp.where(j < tiles, j, jnp.minimum(j - tiles, tiles - 1))),
            ),
            *[hbm] * len(sides.operands),
        ],
        earlier,
        grid=(2 * tiles + turns + 1,),
        out_specs=[
            pl.BlockSpec((depth, own), lambda j: (0, jnp.maximum(j - (tiles + turns + 1), 0))),
            *[hbm] * len(sides.out_shapes),
        ],
        out_shape=[jax.ShapeDtypeStruct((depth, own * tiles), F32), *sides.out_shapes],
        scratch_shapes=[
            pltpu.VMEM((count, width // 2), LOW),
            pltpu.VMEM((2, width // 2, tile), LOW),
            pltpu.VMEM((tiles, width // 2, tile), LOW),
            pltpu.SemaphoreType.DMA((2,)),
            pltpu.SemaphoreType.DMA((tiles,)),
            pltpu.SemaphoreType.DMA((tiles, swapped)),
            pltpu.SemaphoreType.DMA((tiles, swapped)),
            pltpu.VMEM((tiles, spans - 1, depth, own), LOW),
            pltpu.SemaphoreType.DMA((tiles, spans - 1)),
            pltpu.SemaphoreType.DMA((tiles, spans - 1)),
            *[
                pltpu.VMEM((tiles, 2 ** (turns - 1 - turn), depth, size), LOW)
                for _, size in shares
                for turn in range(turns)
            ],
            *sides.scratch,
        ],
        compiler_params=pltpu.CompilerParams(
            collective_id=number, has_side_effects=True, vmem_limit_bytes=56 * MIB
        ),
        cost_estimate=pl.CostEstimate(
            flops=2 * count * width * tile * tiles,
            bytes_accessed=2 * count * width + 4 * count * tile * tiles,
            transcendentals=0,
        ),
        name="grad_scatter",
    )
    return results[0], *sides.results(results[1:])


def project_kernel(tiles, rows_ref, weight_ref, pre_ref, value_ref, query_sq_ref, key_sq_ref):
    step = pl.program_id(0)
    result = nn(rows_ref[...], weight_ref[...])
    squares = jnp.sum(result * result, axis=1, keepdims=True)

    @pl.when(step < 2 * tiles)
    def _():
        pre_ref[...] = result

    for first, ref in ((0, query_sq_ref), (tiles, key_sq_ref)):

        @pl.when(step == first)
        def _(ref=ref):
            ref[...] = squares

        @pl.when(jnp.logical_and(step > first, step < first + tiles))
        def _(ref=ref):
            ref[...] += squares

    @pl.when(step >= 2 * tiles)
    def _():
        value_ref[...] = result.astype(LOW)


def project(inputs, full):
    rows, depth = inputs.shape
    cols = full.shape[1] // 3
    tile = min(512, cols)
    tiles = cols // tile
    column = pl.BlockSpec((rows, 1), lambda j: (0, 0))
    return pl.pallas_call(
        functools.partial(project_kernel, tiles),
        grid=(3 * tiles,),
        in_specs=[
            pl.BlockSpec((rows, depth), lambda j: (0, 0)),
            pl.BlockSpec((depth, tile), lambda j: (0, j)),
        ],
        out_specs=[
            pl.BlockSpec((rows, tile), lambda j: (0, jnp.minimum(j, 2 * tiles - 1))),
            pl.BlockSpec((rows, tile), lambda j: (0, jnp.maximum(j - 2 * tiles, 0))),
            column,
            column,
        ],
        out_shape=[
            jax.ShapeDtypeStruct((rows, 2 * cols), F32),
            jax.ShapeDtypeStruct((rows, cols), LOW),
            jax.ShapeDtypeStruct((rows, 1), F32),
            jax.ShapeDtypeStruct((rows, 1), F32),
        ],
        compiler_params=pltpu.CompilerParams(vmem_limit_bytes=48 * MIB),
        cost_estimate=pl.CostEstimate(
            flops=6 * rows * depth * cols,
            bytes_accessed=6 * depth * cols + 10 * rows * cols + 2 * rows * depth,
            transcendentals=0,
        ),
        name="project",
    )(inputs, full)


def attention_specs(heads):
    return (
        pl.BlockSpec((SEQ_LEN, HEAD_DIM), lambda i: (0, i)),
        pl.BlockSpec((SEQ_LEN, HEAD_DIM), lambda i: (0, i + heads)),
        pl.BlockSpec((SEQ_LEN, HEAD_DIM), lambda i: (0, 0)),
        pl.BlockSpec((SEQ_LEN, 1), lambda i: (0, 0)),
        pl.BlockSpec((1, HEAD_DIM), lambda i: (0, i)),
        pl.BlockSpec((None, SEQ_LEN, 1), lambda i: (i, 0, 0)),
        pl.BlockSpec(memory_space=pl.ANY),
    )


def attend(number, rows, parts, pre, value, invs, gains, tables, sides):
    width = value.shape[1]
    heads = width // HEAD_DIM
    head, later, whole, column, gain, lse, hbm = attention_specs(heads)
    low = jax.ShapeDtypeStruct((SEQ_LEN, width), LOW)
    results = call(
        functools.partial(attend_kernel, rows, parts, 1.0 / math.sqrt(HEAD_DIM), heads, sides),
        [pre, pre, value, *invs, *gains, *tables, *sides.operands],
        [head, later, head, column, column, gain, gain, whole, whole]
        + [hbm] * len(sides.operands),
        grid=(heads,),
        out_specs=[head, head, head, lse, *[hbm] * len(sides.out_shapes)],
        out_shape=[
            low,
            low,
            low,
            jax.ShapeDtypeStruct((heads, SEQ_LEN, 1), F32),
            *sides.out_shapes,
        ],
        scratch_shapes=[
            pltpu.VMEM((SEQ_LEN, HEAD_DIM), LOW),
            pltpu.VMEM((SEQ_LEN, HEAD_DIM), LOW),
            *sides.scratch,
        ],
        compiler_params=pltpu.CompilerParams(
            vmem_limit_bytes=40 * MIB, **sides.options(number)
        ),
        cost_estimate=pl.CostEstimate(
            flops=8 * heads * SEQ_LEN * SEQ_LEN * HEAD_DIM,
            bytes_accessed=16 * SEQ_LEN * width,
            transcendentals=heads * SEQ_LEN * SEQ_LEN,
        ),
        name="attend",
    )
    return *results[:4], *sides.results(results[4:])


def attend_back(
    number, rows, parts, rots, value, grad, lse_all, pre, invs, gains, tables, earlier, sides
):
    width = value.shape[1]
    heads = width // HEAD_DIM
    head, later, whole, column, gain, lse, hbm = attention_specs(heads)
    full = jax.ShapeDtypeStruct((SEQ_LEN, width), F32)
    low = jax.ShapeDtypeStruct((SEQ_LEN, width), LOW)
    gain_out = jax.ShapeDtypeStruct((1, width), F32)
    inner = jax.ShapeDtypeStruct((SEQ_LEN, 1), F32)
    results = call(
        functools.partial(
            attend_back_kernel, rows, parts, 1.0 / math.sqrt(HEAD_DIM), heads, sides
        ),
        [*rots, value, grad, lse_all, pre, pre, *invs, *gains, *tables, *sides.operands],
        [head, head, head, head, lse, head, later, column, column, gain, gain, whole, whole]
        + [hbm] * len(sides.operands),
        earlier,
        grid=(heads,),
        out_specs=[head, head, head, gain, gain, column, column, *[hbm] * len(sides.out_shapes)],
        out_shape=[full, full, low, gain_out, gain_out, inner, inner, *sides.out_shapes],
        scratch_shapes=[
            pltpu.VMEM((SEQ_LEN, HEAD_DIM), LOW),
            pltpu.VMEM((SEQ_LEN, HEAD_DIM), LOW),
            pltpu.VMEM((SEQ_LEN, HEAD_DIM), F32),
            pltpu.VMEM((SEQ_LEN, HEAD_DIM), F32),
            *sides.scratch,
        ],
        compiler_params=pltpu.CompilerParams(
            vmem_limit_bytes=48 * MIB, **sides.options(number)
        ),
        cost_estimate=pl.CostEstimate(
            flops=20 * heads * SEQ_LEN * SEQ_LEN * HEAD_DIM,
            bytes_accessed=32 * SEQ_LEN * width,
            transcendentals=heads * SEQ_LEN * SEQ_LEN,
        ),
        name="attend_back",
    )
    return *results[:7], *sides.results(results[7:])


def norm_back(grad_hat, values_hat, inverse, width):
    inner = jnp.sum(grad_hat * values_hat, axis=1, keepdims=True) / width
    return inverse * (grad_hat - values_hat * inner)


def layer(fsdp, tensor, *arguments):
    layer_input, query_weight, key_weight, value_weight, out_weight = arguments[:5]
    gate_weight, up_weight, down_weight = arguments[5:8]
    query_gain, key_gain, attn_gain, ffn_gain, out_cotangent = arguments[8:]
    rows_here, width = layer_input.shape
    head_cols = query_weight.shape[1]
    parts = SEQ_LEN // rows_here
    spans = tensor // parts
    rank = lax.axis_index("tensor")
    place, span = rank % parts, rank // parts

    def to_part(x, shift):
        pairs = [
            (s * parts + p, s * parts + (p + shift) % parts)
            for s in range(spans)
            for p in range(parts)
        ]
        return lax.ppermute(x, "tensor", pairs)

    def to_span(x, shift):
        pairs = [
            (s * parts + p, (s + shift) % spans * parts + p)
            for s in range(spans)
            for p in range(parts)
        ]
        return lax.ppermute(x, "tensor", pairs)

    def gather_shard(shard):
        return lax.all_gather(shard, "fsdp", axis=0, tiled=True)

    def add_pieces(total, came):
        for piece in came:
            total = total + piece.astype(F32)
        return total

    def sum_parts(x):
        total = x
        for p in range(1, parts):
            total = total + jnp.roll(to_part(x, p), p * rows_here, axis=0)
        return total

    same_core = [list(range(c, fsdp, 2)) for c in range(2)]

    def scatter(total):
        return lax.psum_scatter(
            total, "fsdp", scatter_dimension=0, tiled=True, axis_index_groups=same_core
        )

    def own_columns(s):
        return ((span + spans - s) % spans * parts + place) * head_cols

    def gain_here(gain):
        return jnp.concatenate(
            [lax.dynamic_slice_in_dim(gain, own_columns(s), head_cols) for s in range(spans)]
        )[None, :]

    def gain_whole(part):
        whole = jnp.zeros((width,), F32)
        for s in range(spans):
            whole = lax.dynamic_update_slice_in_dim(
                whole, part[0, s * head_cols : (s + 1) * head_cols], own_columns(s), 0
            )
        return whole

    gate_up_shard = jnp.concatenate([gate_weight, up_weight], axis=1)
    down_shard = down_weight.T
    out_shard = out_weight.T
    cols = gate_weight.shape[1]
    shards, plan = [], []
    for s in range(spans):
        for w, shard in enumerate([query_weight, key_weight, value_weight, out_shard]):
            shards.append(shard)
            plan.append((w // 3, s, w % 3 * spans + s, False))
    (full_qkv, full_out), (down_came,), inputs = exchange(
        0,
        fsdp,
        parts,
        spans,
        shards,
        plan,
        sides=Sides(Rows(parts, gather=layer_input)),
        sends=[down_shard],
    )
    gate_up_first = gather_shard(after(gate_up_shard, inputs))

    local = jnp.arange(SEQ_LEN)
    position = (place + parts - local // rows_here) % parts * rows_here + local % rows_here
    inverse = THETA ** (-jnp.arange(0, HEAD_DIM, 2).astype(F32) / HEAD_DIM)
    angles = position.astype(F32)[:, None] * inverse[None, :]
    cos, sin = jnp.cos(angles), jnp.sin(angles)
    tables = (jnp.concatenate([cos, cos], axis=1), jnp.concatenate([-sin, sin], axis=1))
    gains = (gain_here(query_gain), gain_here(key_gain))

    pre, value_low, query_sq, key_sq = project(inputs, full_qkv)
    squares = sum_parts(jnp.concatenate([query_sq, key_sq], axis=1))
    invs = lax.rsqrt(squares / width + EPSILON)
    invs = (invs[:, :1], invs[:, 1:])
    others_spans = range(1, spans)
    sides = Sides(Spans(parts, spans, [(gate_up_shard, 0, cols, spans - s) for s in others_spans]))
    attended, query_rot, key_rot, lse, gate_came = attend(
        13, rows_here, parts, pre, value_low, invs, gains, tables, sides
    )
    branch, low = product_sum(parts, [(attended, 0, full_out, 0, full_out.shape[1])])
    down_shards = jnp.concatenate([down_shard, *[down_came[s - 1] for s in others_spans]], axis=1)
    gate_up_first, low, down_shards = lax.optimization_barrier((gate_up_first, low, down_shards))
    full_down = gather_shard(down_shards)
    sides = Sides(
        Rows(parts, deliver=low),
        Spans(parts, spans, [(gate_up_shard, 1, cols, spans - s) for s in others_spans]),
    )
    full_gate, _, came, up_came = exchange(
        1, fsdp, parts, spans, gate_came, [(s - 1, s, 0, True) for s in others_spans], sides=sides
    )
    branch = add_pieces(branch, came)
    branch_inv = lax.rsqrt(jnp.mean(branch * branch, axis=1, keepdims=True) + EPSILON)
    branch_hat = branch * branch_inv
    middle = layer_input.astype(F32) + branch_hat * attn_gain
    half = rows_here // 2
    halves = [slice(0, half), slice(half, rows_here)]
    middle_low = [middle[h].astype(LOW) for h in halves]
    grad_out = out_cotangent.astype(F32)
    full_up, _, mixed_first = exchange(
        2,
        fsdp,
        parts,
        spans,
        up_came,
        [(s - 1, s, 0, True) for s in others_spans],
        sides=Sides(Rows(parts, gather=middle_low[0])),
    )
    full_gate_up = [((gate_up_first, 0), (gate_up_first, 1))]
    full_gate_up += [((gate, 0), (up, 0)) for gate, up in zip(full_gate, full_up)]
    mixed = [mixed_first, None]
    gates, uppers, hiddens = [None] * 2, [None] * 2, [None] * 2
    back, outputs, ffn_gain_parts, grad_middles, attn_gain_parts = [None] * 2, [], [], [], []

    def down_pairs(c):
        return [(hiddens[c], s, full_down, s, cols) for s in range(spans)]

    def up_pairs(c):
        return [
            (grad, s, array, run, cols)
            for s in range(spans)
            for grad, (array, run) in zip(back[c], full_gate_up[s])
        ]

    def turn(c, total, came):
        second = add_pieces(total, came)
        second_inv = lax.rsqrt(jnp.mean(second * second, axis=1, keepdims=True) + EPSILON)
        second_hat = second * second_inv
        outputs.append((middle[halves[c]] + second_hat * ffn_gain).astype(LOW))
        grad = grad_out[halves[c]]
        ffn_gain_parts.append(jnp.sum(grad * second_hat, axis=0))
        return norm_back(grad * ffn_gain, second_hat, second_inv, width).astype(LOW)

    part_cols = cols // 2

    def to_spans(array, run, width):
        each = array.shape[1] // spans // width
        return Spans(parts, spans, [(array, s * each + run, width, s) for s in others_spans])

    def back_to_branch(c, total, came):
        grad_middle = grad_out[halves[c]] + add_pieces(total, came)
        hat = branch_hat[halves[c]]
        grad_middles.append(grad_middle)
        attn_gain_parts.append(jnp.sum(grad_middle * hat, axis=0))
        return norm_back(grad_middle * attn_gain, hat, branch_inv[halves[c]], width).astype(LOW)

    gates[0], uppers[0], hiddens[0], mixed[1] = feed_up(
        mixed[0], full_gate_up, cols, 3, Sides(Rows(parts, gather=middle_low[1]))
    )
    second_first, low = product_sum(parts, down_pairs(0))
    gates[1], uppers[1], hiddens[1], came = feed_up(
        mixed[1], full_gate_up, cols, 4, Sides(Rows(parts, deliver=low))
    )
    grad_second = turn(0, second_first, came)
    second_last, low, grad_rows_first = product_sum(
        parts, down_pairs(1), [], 5, Sides(Rows(parts, gather=grad_second))
    )
    *back[0], came = feed_up_back(
        grad_rows_first, full_down, gates[0], uppers[0], [], 6, Sides(Rows(parts, deliver=low))
    )
    grad_second = turn(1, second_last, came)
    mixed_grad_first, low, grad_rows_last = product_sum(
        parts, up_pairs(0), [], 7, Sides(Rows(parts, gather=grad_second))
    )
    grad_rows = [grad_rows_first, grad_rows_last]
    now, came = weight_grad_half(
        8,
        fsdp,
        grad_rows,
        [(hiddens, 0, spans * cols)],
        sides=Sides(Rows(parts, deliver=low)),
    )
    down_terms = scatter(now)
    grad_branch = back_to_branch(0, mixed_grad_first, came)
    *back[1], branch_first = feed_up_back(
        grad_rows_last,
        full_down,
        gates[1],
        uppers[1],
        [now],
        9,
        Sides(Rows(parts, gather=grad_branch)),
    )
    mixed_grad_last, low = product_sum(parts, up_pairs(1))
    backs = list(zip(*back))
    gate_up_grad = {}
    for s in reversed(range(spans)):
        entries = [(list(arrays), s * cols, cols) for arrays in backs]
        if s == spans - 1:
            jobs = [Rows(parts, deliver=low)]
        elif s:
            jobs = []
        else:
            jobs = [Rows(parts, gather=grad_branch), to_spans(down_terms, 0, part_cols)]
        now, *results = weight_grad_half(10 + s, fsdp, mixed, entries, [now], Sides(*jobs))
        if s:
            gate_up_grad[s] = scatter(now)
        if s == spans - 1:
            grad_branch = back_to_branch(1, mixed_grad_last, results[0])
    branch_last, down_came_first = results
    output = jnp.concatenate(outputs, axis=0)
    ffn_gain_part, attn_gain_part = sum(ffn_gain_parts), sum(attn_gain_parts)
    grad_middle = jnp.concatenate(grad_middles, axis=0)
    grad_branch_rows = jnp.concatenate(
        [
            piece[p * half : (p + 1) * half]
            for p in range(parts)
            for piece in (branch_first, branch_last)
        ],
        axis=0,
    )
    grad_attended = nn(grad_branch_rows, full_out).astype(LOW)
    out_total, down_came_last = weight_grad_half(
        30,
        fsdp,
        [grad_branch_rows],
        [([attended], 0, attended.shape[1])],
        [grad_attended],
        Sides(to_spans(down_terms, 1, part_cols)),
    )
    *away, out_total = lax.optimization_barrier(
        (*[gate_up_grad[s] for s in others_spans], out_total)
    )
    gate_up_grad.update(zip(others_spans, away))
    out_terms = scatter(out_total)
    (
        query_gained,
        key_gained,
        grad_value,
        query_gain_part,
        key_gain_part,
        query_inner,
        key_inner,
        gate_came,
    ) = attend_back(
        12,
        rows_here,
        parts,
        (query_rot, key_rot),
        value_low,
        grad_attended,
        lse,
        pre,
        invs,
        gains,
        tables,
        [out_total],
        Sides(Spans(parts, spans, [(gate_up_grad[s], 0, cols, s) for s in others_spans])),
    )
    out_terms, now, grad_value = lax.optimization_barrier((out_terms, now, grad_value))
    gate_up_grad[0] = scatter(now)
    down_came = [jnp.concatenate(pair, axis=1) for pair in zip(down_came_first, down_came_last)]
    down_grad = add_pieces(down_terms[:, :cols].astype(F32), down_came)
    inners = sum_parts(jnp.concatenate([query_inner, key_inner], axis=1)) / width
    local_width = value_low.shape[1]
    grad_query = invs[0] * (query_gained - pre[:, :local_width] * invs[0] * inners[:, :1])
    grad_key = invs[1] * (key_gained - pre[:, local_width:] * invs[1] * inners[:, 1:])
    grad_qkv = jnp.concatenate(
        [grad_query.astype(LOW), grad_key.astype(LOW), grad_value], axis=1
    )
    sides = Sides(Spans(parts, spans, [(gate_up_grad[s], 2, part_cols, s) for s in others_spans]))
    total, low, up_came_first = product_sum(
        parts, [(grad_qkv, 0, full_qkv, 0, full_qkv.shape[1])], [], 32, sides
    )
    gain_parts = [gain_whole(query_gain_part), gain_whole(key_gain_part)]
    sides = Sides(
        SumAll(fsdp, tensor, jnp.stack([*gain_parts, attn_gain_part, ffn_gain_part])),
        Rows(parts, deliver=low),
        Spans(parts, spans, [(out_terms, s, head_cols, s) for s in others_spans]),
        Spans(parts, spans, [(gate_up_grad[s], 3, part_cols, s) for s in others_spans]),
    )
    qkv_grad, gain_grads, came, out_came, up_came_last = grad_scatter(
        31, fsdp, parts, spans, inputs, grad_qkv, 3, [], sides
    )
    input_grad = grad_middle + add_pieces(total, came)
    out_grad = add_pieces(out_terms[:, :head_cols].astype(F32), out_came)
    up_came = [jnp.concatenate(pair, axis=1) for pair in zip(up_came_first, up_came_last)]
    gate_grad = add_pieces(gate_up_grad[0][:, :cols].astype(F32), gate_came)
    up_grad = add_pieces(gate_up_grad[0][:, cols:].astype(F32), up_came)
    query_grad, key_grad, value_grad = jnp.split(qkv_grad, 3, axis=1)
    return (
        output,
        input_grad,
        query_grad,
        key_grad,
        value_grad,
        out_grad.T,
        gate_grad,
        up_grad,
        down_grad.T,
        *gain_grads,
    )


def solution(mesh):
    columns, rows = P("fsdp", "tensor"), P("tensor", "fsdp")
    tokens = P(("fsdp", "tensor"), None)
    weights = (columns, columns, columns, rows, columns, columns, rows)
    return jax.shard_map(
        functools.partial(layer, mesh.shape["fsdp"], mesh.shape["tensor"]),
        mesh=mesh,
        in_specs=(tokens, *weights, P(), P(), P(), P(), tokens),
        out_specs=(tokens, tokens, *weights, P(), P(), P(), P()),
        check_vma=False,
    )
```

```python
import functools
import math

import jax
import jax.numpy as jnp
from jax import lax
from jax.experimental import pallas as pl
from jax.experimental.pallas import tpu as pltpu
from jax.sharding import PartitionSpec as P

HEAD_DIM = 128
SEQ_LEN = 1024
EPSILON = 1e-06
THETA = 500000.0
BLOCK = 256
LOW = jnp.bfloat16
F32 = jnp.float32


def nn(a, b):
    return lax.dot_general(a, b, (((1,), (0,)), ((), ())), preferred_element_type=F32)


def nt(a, b):
    return lax.dot_general(a, b, (((1,), (1,)), ((), ())), preferred_element_type=F32)


def tn(a, b):
    return lax.dot_general(a, b, (((0,), (0,)), ((), ())), preferred_element_type=F32)


def after(x, *earlier):
    return lax.optimization_barrier((x, *earlier))[0]


def block_start(place, block, rows, parts):
    part = block * BLOCK // rows
    return pl.multiple_of(
        lax.rem(place + parts - part, parts) * rows + block * BLOCK % rows, BLOCK
    )


def masked(scores):
    row = lax.broadcasted_iota(jnp.int32, scores.shape, 0)
    col = lax.broadcasted_iota(jnp.int32, scores.shape, 1)
    return jnp.where(row + (scores.shape[1] - scores.shape[0]) >= col, scores, -1e30)


def attend_kernel(rows, parts, scale, heads, sides, *refs):
    query_ref, key_ref, value_ref, query_inv_ref, key_inv_ref = refs[:5]
    query_gain_ref, key_gain_ref, cos_ref, sin_ref = refs[5:9]
    side_refs, refs = refs[9 : 9 + len(sides.operands)], refs[9 + len(sides.operands) :]
    out_ref, query_rot_ref, key_rot_ref, lse_ref = refs[:4]
    side_outs, refs = refs[4 : 4 + len(sides.out_shapes)], refs[4 + len(sides.out_shapes) :]
    key_seq, value_seq = refs[:2]
    sides_at = (side_refs, side_outs, refs[2:])
    place = lax.rem(lax.axis_index("tensor"), parts)

    @pl.when(pl.program_id(0) == 0)
    def _():
        greet(sides.partners())

    sides.start_over(pl.program_id(0), heads, *sides_at)
    half = HEAD_DIM // 2
    for block in range(SEQ_LEN // BLOCK):
        here = pl.ds(block_start(place, block, rows, parts), BLOCK)
        there = pl.ds(block * BLOCK, BLOCK)
        cos, sin = cos_ref[here], sin_ref[here]
        key = key_ref[here] * key_inv_ref[here] * key_gain_ref[...]
        key = (key * cos + pltpu.roll(key, half, 1) * sin).astype(LOW)
        key_rot_ref[here] = key
        key_seq[there] = key
        value_seq[there] = value_ref[here]
        query = query_ref[here] * query_inv_ref[here] * query_gain_ref[...]
        query = (query * cos + pltpu.roll(query, half, 1) * sin).astype(LOW)
        query_rot_ref[here] = query
        span = (block + 1) * BLOCK
        scores = masked(nt(query, key_seq[:span]) * scale)
        top = jnp.max(scores, axis=1, keepdims=True)
        exps = jnp.exp(scores - top)
        total = jnp.sum(exps, axis=1, keepdims=True)
        weights = (exps * (1.0 / total)).astype(LOW)
        out_ref[here] = nn(weights, value_seq[:span]).astype(LOW)
        lse_ref[here] = top + jnp.log(total)

    @pl.when(pl.program_id(0) == heads - 1)
    def _():
        sides.finish(*sides_at)


def attend_back_kernel(rows, parts, scale, heads, sides, *refs):
    query_rot_ref, key_rot_ref, value_ref, grad_ref, lse_ref, query_ref, key_ref = refs[:7]
    query_inv_ref, key_inv_ref, query_gain_ref, key_gain_ref, cos_ref, sin_ref = refs[7:13]
    side_refs, refs = refs[13 : 13 + len(sides.operands)], refs[13 + len(sides.operands) :]
    query_out_ref, key_out_ref, value_out_ref = refs[:3]
    query_gain_out_ref, key_gain_out_ref, query_inner_ref, key_inner_ref = refs[3:7]
    side_outs, refs = refs[7 : 7 + len(sides.out_shapes)], refs[7 + len(sides.out_shapes) :]
    key_seq, value_seq, key_acc, value_acc = refs[:4]
    sides_at = (side_refs, side_outs, refs[4:])
    place = lax.rem(lax.axis_index("tensor"), parts)
    half = HEAD_DIM // 2
    count = SEQ_LEN // BLOCK

    @pl.when(pl.program_id(0) == 0)
    def _():
        if sides.jobs:
            greet(sides.partners())
        query_inner_ref[...] = jnp.zeros_like(query_inner_ref)
        key_inner_ref[...] = jnp.zeros_like(key_inner_ref)

    sides.start_over(pl.program_id(0), heads, *sides_at)

    def finish(grad, here, values_ref, inv_ref, gain_ref, out_ref, inner_ref):
        back = grad * cos_ref[here] - pltpu.roll(grad, half, 1) * sin_ref[here]
        hat = values_ref[here] * inv_ref[here]
        gained = back * gain_ref[...]
        out_ref[here] = gained
        inner_ref[here] += jnp.sum(gained * hat, axis=1, keepdims=True)
        return jnp.sum(back * hat, axis=0, keepdims=True)

    query_gain_sum = jnp.zeros((1, HEAD_DIM), F32)
    for block in range(count):
        here = pl.ds(block_start(place, block, rows, parts), BLOCK)
        there = pl.ds(block * BLOCK, BLOCK)
        key_seq[there] = key_rot_ref[here]
        value_seq[there] = value_ref[here]
        query, grad = query_rot_ref[here], grad_ref[here]
        span = (block + 1) * BLOCK
        scores = masked(nt(query, key_seq[:span]) * scale)
        probs = jnp.exp(scores - lse_ref[here])
        weights = probs.astype(LOW)
        grad_probs = nt(grad, value_seq[:span])
        delta = jnp.sum(probs * grad_probs, axis=1, keepdims=True)
        grad_scores = (probs * (grad_probs - delta) * scale).astype(LOW)
        value_part = tn(weights, grad)
        key_part = tn(grad_scores, query)
        past = block * BLOCK
        if block:
            key_acc[:past] += key_part[:past]
            value_acc[:past] += value_part[:past]
        key_acc[past:span] = key_part[past:]
        value_acc[past:span] = value_part[past:]
        query_gain_sum += finish(
            nn(grad_scores, key_seq[:span]),
            here,
            query_ref,
            query_inv_ref,
            query_gain_ref,
            query_out_ref,
            query_inner_ref,
        )
    query_gain_out_ref[...] = query_gain_sum
    key_gain_sum = jnp.zeros((1, HEAD_DIM), F32)
    for block in range(count):
        here = pl.ds(block_start(place, block, rows, parts), BLOCK)
        there = pl.ds(block * BLOCK, BLOCK)
        value_out_ref[here] = value_acc[there].astype(LOW)
        key_gain_sum += finish(
            key_acc[there],
            here,
            key_ref,
            key_inv_ref,
            key_gain_ref,
            key_out_ref,
            key_inner_ref,
        )
    key_gain_out_ref[...] = key_gain_sum

    @pl.when(pl.program_id(0) == heads - 1)
    def _():
        sides.finish(*sides_at)


MESH = pl.DeviceIdType.MESH
MIB = 2**20
CHUNKS = 4


def flip(index, bit):
    return index + bit - 2 * bit * lax.rem(lax.div(index, bit), 2)


def row_shares(rows, count):
    units = rows // 16
    sizes = [16 * (units // count + (i < units % count)) for i in range(count)]
    starts = [sum(sizes[:i]) for i in range(count)]
    return list(zip(starts, sizes))


def call(kernel, operands, in_specs, earlier=(), **options):
    count = len(operands)

    def body(*refs):
        kernel(*refs[:count], *refs[count + len(earlier) :])

    specs = [*in_specs, *[pl.BlockSpec(memory_space=pl.ANY)] * len(earlier)]
    return pl.pallas_call(body, in_specs=specs, **options)(*operands, *earlier)


def greet(partners):
    barrier = pltpu.get_barrier_semaphore()
    for partner in partners:
        pl.semaphore_signal(barrier, inc=1, device_id=partner, device_id_type=MESH)
    pl.semaphore_wait(barrier, len(partners))


def remote(src, dst, send_sem, recv_sem, **device):
    return pltpu.make_async_remote_copy(
        src_ref=src,
        dst_ref=dst,
        send_sem=send_sem,
        recv_sem=recv_sem,
        device_id=device,
        device_id_type=MESH,
    )


class Copies:
    def __init__(self, send_sems, recv_sems):
        self.send_sems, self.recv_sems = send_sems, recv_sems
        self.used = 0
        self.open = []
        self.moves = []

    def send(self, src, dst, **device):
        copy = remote(
            src, dst, self.send_sems.at[self.used], self.recv_sems.at[self.used], **device
        )
        self.used += 1
        copy.start()
        self.open.append(copy.wait_send)
        return copy

    def move(self, src, hold, dst):
        load = pltpu.make_async_copy(src, hold, self.send_sems.at[self.used])
        store = pltpu.make_async_copy(hold, dst, self.recv_sems.at[self.used])
        self.used += 1
        load.start()
        self.moves.append((load, store))

    def finish(self):
        for load, store in self.moves:
            load.wait()
            store.start()
        for wait in self.open:
            wait()
        for _, store in self.moves:
            store.wait()


class Rows:
    def __init__(self, parts, gather=None, deliver=None):
        self.parts, self.gather = parts, gather is not None
        self.operands = [gather if self.gather else deliver]
        rows, width = self.operands[0].shape
        self.rows = rows if self.gather else rows // parts
        self.chunk = self.rows // CHUNKS
        count = parts if self.gather else parts - 1
        self.out_shapes = [jax.ShapeDtypeStruct((count, self.rows, width), LOW)]
        count = CHUNKS * parts
        self.scratch = [pltpu.SemaphoreType.DMA((count,)), pltpu.SemaphoreType.DMA((count,))]
        if self.gather:
            self.scratch.append(pltpu.VMEM((rows, width), LOW))

    def ranks(self):
        rank = lax.axis_index("tensor")
        place = lax.rem(rank, self.parts)
        shifts = range(1, self.parts)
        if not self.gather:
            shifts = [self.parts - p for p in shifts]
        return [rank - place + lax.rem(place + p, self.parts) for p in shifts]

    def partners(self):
        return [{"tensor": rank} for rank in self.ranks()]

    def copies(self, chunks, refs, outs, send_sems, recv_sems, hold=None):
        made = []
        for chunk in chunks:
            for i, rank in enumerate(self.ranks()):
                first = 0 if self.gather else (i + 1) * self.rows
                src = refs[0].at[pl.ds(first + chunk * self.chunk, self.chunk)]
                dst = outs[0].at[i + 1] if self.gather else outs[0].at[i]
                dst = dst.at[pl.ds(chunk * self.chunk, self.chunk)]
                sem = CHUNKS * i + chunk
                made.append(
                    remote(src, dst, send_sems.at[sem], recv_sems.at[sem], tensor=rank)
                )
        return made

    def load(self, refs, outs, send_sems, recv_sems, hold):
        return pltpu.make_async_copy(refs[0], hold, send_sems.at[CHUNKS * self.parts - 1])

    def store(self, refs, outs, send_sems, recv_sems, hold):
        return pltpu.make_async_copy(hold, outs[0].at[0], recv_sems.at[CHUNKS * self.parts - 1])

    def start(self, chunk, *where):
        if self.gather and chunk == 0:
            self.load(*where).start()
        for copy in self.copies([chunk], *where):
            copy.start()

    def finish(self, *where):
        if self.gather:
            self.load(*where).wait()
            self.store(*where).start()
            self.store(*where).wait()
        for copy in self.copies(range(CHUNKS), *where):
            copy.wait()

    def results(self, outs):
        out = outs[0]
        if self.gather:
            return out.reshape(-1, out.shape[2])
        return [out[i] for i in range(self.parts - 1)]


class Spans:
    def __init__(self, parts, spans, terms):
        self.parts, self.spans, self.terms = parts, spans, terms
        self.operands = [array for array, *_ in terms]
        self.out_shapes = [
            jax.ShapeDtypeStruct((array.shape[0], width), LOW) for array, _, width, _ in terms
        ]
        count = CHUNKS * max(1, len(terms))
        self.scratch = [pltpu.SemaphoreType.DMA((count,)), pltpu.SemaphoreType.DMA((count,))]

    def rank(self, back):
        rank = lax.axis_index("tensor")
        place, span = lax.rem(rank, self.parts), lax.div(rank, self.parts)
        return lax.rem(span + self.spans - back, self.spans) * self.parts + place

    def partners(self):
        return [{"tensor": self.rank(s)} for s in range(1, self.spans)]

    def copies(self, chunks, refs, outs, send_sems, recv_sems):
        made = []
        for chunk in chunks:
            for i, (ref, out, (array, run, width, back)) in enumerate(zip(refs, outs, self.terms)):
                size = array.shape[0] // CHUNKS
                rows, sem = pl.ds(chunk * size, size), CHUNKS * i + chunk
                made.append(
                    remote(
                        ref.at[rows, pl.ds(run * width, width)],
                        out.at[rows],
                        send_sems.at[sem],
                        recv_sems.at[sem],
                        tensor=self.rank(back),
                    )
                )
        return made

    def start(self, chunk, *where):
        for copy in self.copies([chunk], *where):
            copy.start()

    def finish(self, *where):
        for copy in self.copies(range(CHUNKS), *where):
            copy.wait()

    def results(self, outs):
        return list(outs)


class SumAll:
    def __init__(self, fsdp, tensor, array):
        self.operands = [array]
        self.out_shapes = [jax.ShapeDtypeStruct(array.shape, F32)]
        self.turns = [
            (axis, 1 << b)
            for axis, size in (("fsdp", fsdp), ("tensor", tensor))
            for b in range(size.bit_length() - 1)
        ]
        count = len(self.turns)
        self.scratch = [
            pltpu.SemaphoreType.DMA((count + 1,)),
            pltpu.SemaphoreType.DMA((count,)),
            pltpu.VMEM(array.shape, F32),
            pltpu.VMEM((count, *array.shape), F32),
        ]

    def partners(self):
        return [{axis: flip(lax.axis_index(axis), bit)} for axis, bit in self.turns]

    def copy(self, turn, refs, outs, send_sems, recv_sems, total, came):
        axis, bit = self.turns[turn]
        device = {axis: flip(lax.axis_index(axis), bit)}
        return remote(total, came.at[turn], send_sems.at[turn], recv_sems.at[turn], **device)

    def take(self, turn, *where):
        self.copy(turn, *where).wait()
        total, came = where[-2:]
        total[...] += came[turn]

    def start(self, chunk, *where):
        refs, _, send_sems, _, total, _ = where
        if chunk == 0:
            load = pltpu.make_async_copy(refs[0], total, send_sems.at[len(self.turns)])
            load.start()
            load.wait()
        elif chunk < len(self.turns):
            self.take(chunk - 1, *where)
        if chunk < len(self.turns):
            self.copy(chunk, *where).start()

    def finish(self, *where):
        _, outs, send_sems, _, total, _ = where
        count = len(self.turns)
        for turn in range(min(CHUNKS, count) - 1, count):
            self.take(turn, *where)
            if turn + 1 < count:
                self.copy(turn + 1, *where).start()
        store = pltpu.make_async_copy(total, outs[0], send_sems.at[count])
        store.start()
        store.wait()

    def results(self, outs):
        return outs[0]


class Sides:
    def __init__(self, *jobs):
        self.jobs = jobs
        self.operands = [x for job in jobs for x in job.operands]
        self.out_shapes = [x for job in jobs for x in job.out_shapes]
        self.scratch = [x for job in jobs for x in job.scratch]

    def partners(self):
        return [partner for job in self.jobs for partner in job.partners()]

    def each(self, refs, outs, scratch):
        for job in self.jobs:
            counts = len(job.operands), len(job.out_shapes), len(job.scratch)
            yield job, (refs[: counts[0]], outs[: counts[1]], *scratch[: counts[2]])
            refs, outs, scratch = refs[counts[0] :], outs[counts[1] :], scratch[counts[2] :]

    def start(self, chunk, *where):
        for job, own in self.each(*where):
            job.start(chunk, *own)

    def start_over(self, step, steps, *where):
        for job, own in self.each(*where):
            stride = steps // CHUNKS
            if stride < 2 and isinstance(job, Spans):
                stride = 0
            elif stride == 0:
                stride = 1
            for chunk in range(CHUNKS):

                @pl.when(step == min(chunk * stride, steps - 1))
                def _(job=job, own=own, chunk=chunk):
                    job.start(chunk, *own)

    def finish(self, *where):
        for job, own in self.each(*where):
            job.finish(*own)

    def results(self, outs):
        return [job.results(own) for job, (_, own, *_) in self.each([], outs, [])]

    def options(self, number):
        return {"collective_id": number, "has_side_effects": True} if self.jobs else {}


NO_SIDES = Sides()


def exchange_kernel(fsdp, parts, spans, plan, counts, *refs):
    sides, shard_count, send_count, full_count = counts
    rows_count = len(sides.operands)
    rows_refs, refs = refs[:rows_count], refs[rows_count:]
    shard_refs, refs = refs[:shard_count], refs[shard_count:]
    span_refs, refs = refs[:send_count], refs[send_count:]
    full_refs, refs = refs[:full_count], refs[full_count:]
    span_outs, refs = refs[:send_count], refs[send_count:]
    side_outs, refs = refs[: len(sides.out_shapes)], refs[len(sides.out_shapes) :]
    hold_refs, refs = refs[: len(plan)], refs[len(plan) :]
    sides_at = (rows_refs, side_outs, refs[:-2])
    copies = Copies(*refs[-2:])
    me, rank = lax.axis_index("fsdp"), lax.axis_index("tensor")
    place, span = lax.rem(rank, parts), lax.div(rank, parts)
    bits = [1 << b for b in range(1, fsdp.bit_length() - 1)]
    span_ranks = [lax.rem(span + s, spans) * parts + place for s in range(1, spans)]
    partners = [{"fsdp": flip(me, bit)} for bit in [1, *bits]] if plan else []
    partners += sides.partners()
    if send_count or any(s and not here for _, s, _, here in plan):
        partners += [{"tensor": r} for r in span_ranks]
    greet(partners)

    def slot(job, mask, share=None):
        group, s, position, _ = plan[job]
        which = me
        for bit in [1, *bits]:
            if mask & bit:
                which = flip(which, bit)
        cols = shard_refs[job].shape[1]
        ref = full_refs[group].at[which, :, pl.ds(position * cols, cols)]
        return ref if share is None else ref.at[pl.ds(*share)]

    depth = shard_refs[0].shape[0] if plan else 16
    shares = row_shares(depth, len(bits))
    jobs = range(len(plan))
    away = [s and not here for _, s, _, here in plan]
    for chunk in range(CHUNKS // 2):
        sides.start(chunk, *sides_at)
    from_span = {
        job: copies.send(shard_refs[job], slot(job, 0), tensor=span_ranks[plan[job][1] - 1])
        for job in jobs
        if away[job]
    }
    for chunk in range(CHUNKS // 2, CHUNKS):
        sides.start(chunk, *sides_at)
    over = []
    for ref, out in zip(span_refs, span_outs):
        for s, r in enumerate(span_ranks):
            over.append(copies.send(ref, out.at[s], tensor=r))
    for job in jobs:
        if not away[job]:
            copies.move(shard_refs[job], hold_refs[job], slot(job, 0))

    arriving = {}
    held = {(job, p): [0] for job in jobs for p in range(len(shares))}

    def source(job, mask, share):
        if mask == 0 and not away[job]:
            return shard_refs[job].at[pl.ds(*share)]
        return slot(job, mask, share)

    def send_step(job, step):
        for p, share in enumerate(shares):
            bit = bits[(p + step) % len(bits)]
            for mask in held[job, p]:
                arriving[job, p, mask | bit] = copies.send(
                    source(job, mask, share), slot(job, mask, share), fsdp=flip(me, bit)
                )

    def take_step(job, step):
        for p in range(len(shares)):
            bit = bits[(p + step) % len(bits)]
            came = [mask | bit for mask in held[job, p]]
            for mask in came:
                arriving[job, p, mask].wait_recv()
            held[job, p] += came

    for step in range(len(bits) + 1):
        for job in jobs:
            if step == 0 and away[job]:
                from_span[job].wait_recv()
            if step:
                take_step(job, step - 1)
            if step < len(bits):
                send_step(job, step)
            else:
                for mask in range(0, fsdp, 2):
                    whole = (0, depth)
                    over.append(
                        copies.send(
                            source(job, mask, whole), slot(job, mask), fsdp=flip(me, 1)
                        )
                    )
    for copy in over:
        copy.wait_recv()
    copies.finish()
    sides.finish(*sides_at)


def exchange(number, fsdp, parts, spans, shards=(), plan=(), sides=NO_SIDES, sends=(), earlier=()):
    bits = fsdp.bit_length() - 2
    per_job = 2 + bits * (2**bits - 1) + 2**bits
    count = len(plan) * per_job + len(sends) * spans + 1
    hbm = pl.BlockSpec(memory_space=pl.ANY)
    full_count = 1 + max([group for group, *_ in plan], default=-1)
    widths = [0] * full_count
    for shard, (group, *_) in zip(shards, plan):
        widths[group] += shard.shape[1]
    depth = shards[0].shape[0] if plan else 0
    outs = [jax.ShapeDtypeStruct((fsdp, depth, width), LOW) for width in widths]
    outs += [jax.ShapeDtypeStruct((spans - 1, *x.shape), LOW) for x in sends]
    inputs = [*shards, *sends]
    scratch = [pltpu.SemaphoreType.DMA((count,)), pltpu.SemaphoreType.DMA((count,))]
    inputs = [*sides.operands, *inputs]
    outs += sides.out_shapes
    scratch = [*sides.scratch, *scratch]
    scratch = [
        *[pltpu.VMEM(x.shape if here or not s else (16, 128), LOW) for x, (_, s, _, here) in zip(shards, plan)],
        *scratch,
    ]
    results = call(
        functools.partial(
            exchange_kernel,
            fsdp,
            parts,
            spans,
            plan,
            (sides, len(shards), len(sends), full_count),
        ),
        inputs,
        [hbm] * len(inputs),
        earlier,
        out_shape=outs,
        out_specs=[hbm] * len(outs),
        scratch_shapes=scratch,
        compiler_params=pltpu.CompilerParams(collective_id=number, has_side_effects=True),
        name="exchange",
    )
    full = [r.reshape(fsdp * depth, -1) for r in results[:full_count]]
    came = results[full_count : full_count + len(sends)]
    return full, came, *sides.results(results[full_count + len(sends) :])


def sum_kernel(pairs, own, has_addend, sides, steps, *refs):
    step = pl.program_id(0)
    first_side = 2 * pairs + has_addend
    count = first_side + len(sides.operands)
    own_ref, low_ref, outs = refs[count], refs[count + 1], refs[count + 2 :]
    outs, scratch = outs[: len(sides.out_shapes)], outs[len(sides.out_shapes) :]
    sides_at = (refs[first_side:count], outs, scratch)
    if sides.jobs:

        @pl.when(step == 0)
        def _():
            greet(sides.partners())

    sides.start_over(step, steps, *sides_at)
    total = None
    for i in range(pairs):
        term = nt(refs[2 * i][...], refs[2 * i + 1][...])
        total = term if total is None else total + term
    own_ref[...] = total[:own] + refs[2 * pairs][...] if has_addend else total[:own]
    low_ref[...] = total.astype(LOW)
    if sides.jobs:

        @pl.when(step == steps - 1)
        def _():
            sides.finish(*sides_at)


def product_sum(parts, pairs, earlier=(), number=None, sides=NO_SIDES, addend=None):
    rows, width = pairs[0][0].shape[0], pairs[0][2].shape[0]
    own = rows // parts
    tile = min(512 if rows * sum(depth for *_, depth in pairs) < 5 * MIB else 256, width)
    specs, operands, flops = [], [], 0
    for a, a_run, b, b_run, depth in pairs:
        specs.append(pl.BlockSpec((rows, depth), lambda j, run=a_run: (0, run)))
        specs.append(pl.BlockSpec((tile, depth), lambda j, run=b_run: (j, run)))
        operands += [a, b]
        flops += 2 * rows * depth * width
    if addend is not None:
        specs.append(pl.BlockSpec((own, tile), lambda j: (0, j)))
        operands.append(addend)
    hbm = pl.BlockSpec(memory_space=pl.ANY)
    steps = width // tile
    results = call(
        functools.partial(sum_kernel, len(pairs), own, addend is not None, sides, steps),
        [*operands, *sides.operands],
        [*specs, *[hbm] * len(sides.operands)],
        earlier,
        grid=(steps,),
        out_specs=[
            pl.BlockSpec((own, tile), lambda j: (0, j)),
            pl.BlockSpec((rows, tile), lambda j: (0, j)),
            *[hbm] * len(sides.out_shapes),
        ],
        out_shape=[
            jax.ShapeDtypeStruct((own, width), F32),
            jax.ShapeDtypeStruct((rows, width), LOW),
            *sides.out_shapes,
        ],
        scratch_shapes=sides.scratch,
        compiler_params=pltpu.CompilerParams(
            vmem_limit_bytes=56 * MIB, **sides.options(number)
        ),
        cost_estimate=pl.CostEstimate(
            flops=flops, bytes_accessed=flops // rows + 4 * rows * width, transcendentals=0
        ),
        name="product_sum",
    )
    return *results[:2], *sides.results(results[2:])


def up_kernel(spans, tiles, sides, *refs):
    mixed_ref, weight_refs = refs[0], refs[1 : 1 + 2 * spans]
    refs = refs[1 + 2 * spans :]
    side_refs, refs = refs[: len(sides.operands)], refs[len(sides.operands) :]
    gate_ref, upper_ref, hidden_ref, outs = *refs[:3], refs[3:]
    outs, scratch = outs[: len(sides.out_shapes)], outs[len(sides.out_shapes) :]
    sides_at = (side_refs, outs, scratch)
    step = pl.program_id(0)
    if sides.jobs:

        @pl.when(step == 0)
        def _():
            greet(sides.partners())

    sides.start_over(step, spans * tiles, *sides_at)
    for s in range(spans):

        @pl.when(jnp.logical_and(step >= s * tiles, step < (s + 1) * tiles))
        def _(s=s):
            gate = nn(mixed_ref[...], weight_refs[2 * s][...])
            upper = nn(mixed_ref[...], weight_refs[2 * s + 1][...])
            gate_ref[...] = gate
            upper_ref[...] = upper
            hidden_ref[...] = (gate * jax.nn.sigmoid(gate) * upper).astype(LOW)

    if sides.jobs:

        @pl.when(step == spans * tiles - 1)
        def _():
            sides.finish(*sides_at)


def feed_up(mixed, gate_ups, cols, number=None, sides=NO_SIDES):
    rows, depth = mixed.shape
    spans = len(gate_ups)
    tile = min(512, cols)
    tiles = cols // tile
    hbm = pl.BlockSpec(memory_space=pl.ANY)
    out = pl.BlockSpec((rows, tile), lambda j: (0, j))
    operands, specs = [mixed], [pl.BlockSpec((rows, depth), lambda j: (0, 0))]
    for s, pair in enumerate(gate_ups):
        for array, run in pair:
            operands.append(array)
            specs.append(
                pl.BlockSpec(
                    (depth, tile),
                    lambda j, s=s, run=run: (0, jnp.clip(j - s * tiles, 0, tiles - 1) + run * tiles),
                )
            )
    whole = (rows, spans * cols)
    results = call(
        functools.partial(up_kernel, spans, tiles, sides),
        [*operands, *sides.operands],
        [*specs, *[hbm] * len(sides.operands)],
        grid=(spans * tiles,),
        out_specs=[out, out, out, *[hbm] * len(sides.out_shapes)],
        out_shape=[
            jax.ShapeDtypeStruct(whole, F32),
            jax.ShapeDtypeStruct(whole, F32),
            jax.ShapeDtypeStruct(whole, LOW),
            *sides.out_shapes,
        ],
        scratch_shapes=sides.scratch,
        compiler_params=pltpu.CompilerParams(
            vmem_limit_bytes=56 * MIB, **sides.options(number)
        ),
        cost_estimate=pl.CostEstimate(
            flops=4 * rows * depth * spans * cols,
            bytes_accessed=4 * depth * spans * cols + 10 * rows * spans * cols,
            transcendentals=rows * spans * cols,
        ),
        name="feed_up",
    )
    return *results[:3], *sides.results(results[3:])


def up_back_kernel(spans, tiles, sides, *refs):
    steps = spans * tiles
    grad_ref, down_refs, refs = refs[0], refs[1 : 1 + spans], refs[1 + spans :]
    gate_ref, upper_ref, refs = refs[0], refs[1], refs[2:]
    side_refs, refs = refs[: len(sides.operands)], refs[len(sides.operands) :]
    gate_out_ref, up_out_ref, outs = refs[0], refs[1], refs[2:]
    outs, scratch = outs[: len(sides.out_shapes)], outs[len(sides.out_shapes) :]
    sides_at = (side_refs, outs, scratch)
    step = pl.program_id(0)
    if sides.jobs:

        @pl.when(step == 0)
        def _():
            greet(sides.partners())

    sides.start_over(step, steps, *sides_at)
    for s, down_ref in enumerate(down_refs):

        @pl.when(jnp.logical_and(step >= s * tiles, step < (s + 1) * tiles))
        def _(down_ref=down_ref):
            grad = nn(grad_ref[...], down_ref[...])
            gate = gate_ref[...]
            sigmoid = jax.nn.sigmoid(gate)
            scaled = grad * sigmoid
            slope = 1.0 + gate * (1.0 - sigmoid)
            up_out_ref[...] = (scaled * gate).astype(LOW)
            gate_out_ref[...] = (scaled * upper_ref[...] * slope).astype(LOW)

    if sides.jobs:

        @pl.when(step == steps - 1)
        def _():
            sides.finish(*sides_at)


def feed_up_back(grad_rows, down, gate, upper, earlier=(), number=None, sides=NO_SIDES):
    rows, depth = grad_rows.shape
    downs, spans = [down], 1
    tile = min(512, downs[0].shape[1])
    tiles = downs[0].shape[1] // tile
    cols = spans * tiles * tile
    hbm = pl.BlockSpec(memory_space=pl.ANY)
    spec = pl.BlockSpec((rows, tile), lambda j: (0, j))
    out = jax.ShapeDtypeStruct((rows, cols), LOW)
    results = call(
        functools.partial(up_back_kernel, spans, tiles, sides),
        [grad_rows, *downs, gate, upper, *sides.operands],
        [
            pl.BlockSpec((rows, depth), lambda j: (0, 0)),
            *[
                pl.BlockSpec(
                    (depth, tile), lambda j, s=s: (0, jnp.clip(j - s * tiles, 0, tiles - 1))
                )
                for s in range(spans)
            ],
            spec,
            spec,
            *[hbm] * len(sides.operands),
        ],
        earlier,
        grid=(cols // tile,),
        out_specs=[spec, spec, *[hbm] * len(sides.out_shapes)],
        out_shape=[out, out, *sides.out_shapes],
        scratch_shapes=sides.scratch,
        compiler_params=pltpu.CompilerParams(
            vmem_limit_bytes=52 * MIB, **sides.options(number)
        ),
        cost_estimate=pl.CostEstimate(
            flops=2 * rows * depth * cols,
            bytes_accessed=2 * depth * cols + 12 * rows * cols,
            transcendentals=rows * cols,
        ),
        name="feed_up_back",
    )
    return *results[:2], *sides.results(results[2:])


def weight_grad_kernel(fsdp, chunks, tiles, sides, *refs):
    x_refs, refs = refs[:chunks], refs[chunks:]
    grad_refs, refs = refs[: chunks * len(tiles)], refs[chunks * len(tiles) :]
    rows = x_refs[0].shape[0]
    count, outs = len(sides.operands), len(sides.out_shapes)
    side_refs, out_ref, refs = refs[:count], refs[count], refs[count + 1 :]
    side_outs, refs = refs[:outs], refs[outs:]
    x_half, sent, came, send_sems, recv_sems = refs[:5]
    sides_at = (side_refs, side_outs, refs[5:])
    me = lax.axis_index("fsdp")
    core = lax.rem(me, 2)
    total_tiles = sum(tiles)
    depth = x_refs[0].shape[1] // fsdp
    step = pl.program_id(0)

    def load(which):
        for c, x_ref in enumerate(x_refs):
            for i in range(fsdp // 2):
                first = pl.multiple_of((2 * i + which) * depth, depth)
                x_half[c * rows : (c + 1) * rows, i * depth : (i + 1) * depth] = x_ref[
                    :, pl.ds(first, depth)
                ]

    def product(entry):
        total = None
        for c, ref in enumerate(grad_refs[entry * chunks : (entry + 1) * chunks]):
            term = tn(x_half[c * rows : (c + 1) * rows], ref[...])
            total = term if total is None else total + term
        return total

    def copy(tile):
        slot = lax.rem(tile, 2)
        return remote(
            sent.at[slot], came.at[tile], send_sems.at[slot], recv_sems.at[tile], fsdp=flip(me, 1)
        )

    @pl.when(step == 0)
    def _():
        load(1 - core)
        greet([{"fsdp": flip(me, 1)}, *sides.partners()])

    sides.start_over(step, 2 * total_tiles, *sides_at)

    @pl.when(step == total_tiles)
    def _():
        load(core)

    @pl.when(jnp.logical_and(step >= 2, step < total_tiles))
    def _():
        copy(step - 2).wait_send()

    tile = lax.rem(step, total_tiles)
    first = 0
    for entry, count in enumerate(tiles):
        here = jnp.logical_and(tile >= first, tile < first + count)

        @pl.when(jnp.logical_and(here, step < total_tiles))
        def _(entry=entry):
            sent[lax.rem(step, 2)] = product(entry).astype(LOW)

        @pl.when(jnp.logical_and(here, step >= total_tiles))
        def _(entry=entry):
            total = product(entry)
            copy(tile).wait_recv()
            out_ref[...] = (total + came[tile].astype(F32)).astype(LOW)

        first += count

    @pl.when(step < total_tiles)
    def _():
        copy(step).start()

    @pl.when(step == 2 * total_tiles - 1)
    def _():
        for last in range(max(0, total_tiles - 2), total_tiles):
            copy(last).wait_send()
        sides.finish(*sides_at)


def weight_grad_half(number, fsdp, xs, grads, earlier=(), sides=NO_SIDES):
    chunks = len(xs)
    count, width = xs[0].shape
    tile = math.gcd(1024, *[cols for _, _, cols in grads])
    tiles = [cols // tile for _, _, cols in grads]
    total_tiles = sum(tiles)
    firsts = [sum(tiles[:i]) for i in range(len(tiles))]
    cols = tile * total_tiles

    def grad_spec(first, runs, base):
        return pl.BlockSpec(
            (count, tile),
            lambda j: (0, base + jnp.clip(lax.rem(j, total_tiles) - first, 0, runs - 1)),
        )

    hbm = pl.BlockSpec(memory_space=pl.ANY)
    operands = [*xs, *[array for arrays, _, _ in grads for array in arrays]]
    specs = [pl.BlockSpec((count, width), lambda j: (0, 0))] * chunks
    for first, runs, (_, start, _) in zip(firsts, tiles, grads):
        specs += [grad_spec(first, runs, start // tile)] * chunks
    outs = [jax.ShapeDtypeStruct((width // 2, cols), LOW)]
    out_specs = [pl.BlockSpec((width // 2, tile), lambda j: (0, jnp.maximum(j - total_tiles, 0)))]
    scratch = [
        pltpu.VMEM((chunks * count, width // 2), LOW),
        pltpu.VMEM((2, width // 2, tile), LOW),
        pltpu.VMEM((total_tiles, width // 2, tile), LOW),
        pltpu.SemaphoreType.DMA((2,)),
        pltpu.SemaphoreType.DMA((total_tiles,)),
    ]
    operands += sides.operands
    specs += [hbm] * len(sides.operands)
    outs += sides.out_shapes
    out_specs += [hbm] * len(sides.out_shapes)
    scratch += sides.scratch
    results = call(
        functools.partial(weight_grad_kernel, fsdp, chunks, tiles, sides),
        operands,
        specs,
        earlier,
        grid=(2 * total_tiles,),
        out_specs=out_specs,
        out_shape=outs,
        scratch_shapes=scratch,
        compiler_params=pltpu.CompilerParams(
            collective_id=number, has_side_effects=True, vmem_limit_bytes=56 * MIB
        ),
        cost_estimate=pl.CostEstimate(
            flops=2 * chunks * count * width * cols,
            bytes_accessed=chunks * (2 * count * width + 4 * count * cols) + width * cols,
            transcendentals=0,
        ),
        name="weight_grad",
    )
    return results[0], *sides.results(results[1:])


def column_shares(cols, count):
    return [(8 * start, 8 * size) for start, size in row_shares(cols // 8, count)]


def grad_scatter_kernel(fsdp, parts, spans, tiles, sides, *refs):
    x_ref, grad_ref, refs = refs[0], refs[1], refs[2:]
    count, outs = len(sides.operands), len(sides.out_shapes)
    side_refs, out_ref, refs = refs[:count], refs[count], refs[count + 1 :]
    side_outs, refs = refs[:outs], refs[outs:]
    x_half, sent, held, send_sems, recv_sems, chip_sends, chip_recvs = refs[:7]
    span_came, span_sends, span_recvs, refs = *refs[7:10], refs[10:]
    bits = [1 << b for b in range(fsdp.bit_length() - 2)]
    turns = len(bits)
    chip_came, side_scratch = refs[: turns * turns], refs[turns * turns :]
    sides_at = (side_refs, side_outs, side_scratch)
    me, rank = lax.axis_index("fsdp"), lax.axis_index("tensor")
    core, chip = lax.rem(me, 2), lax.div(me, 2)
    place, span = lax.rem(rank, parts), lax.div(rank, parts)
    depth = x_ref.shape[1] // fsdp
    tile_cols = grad_ref.shape[1]
    own_cols = tile_cols // spans
    shares = column_shares(tile_cols, turns)
    step = pl.program_id(0)

    def load(which):
        for i in range(fsdp // 2):
            first = pl.multiple_of((2 * i + which) * depth, depth)
            x_half[:, i * depth : (i + 1) * depth] = x_ref[:, pl.ds(first, depth)]

    def core_copy(tile):
        slot = lax.rem(tile, 2)
        return remote(
            sent.at[slot], held.at[tile], send_sems.at[slot], recv_sems.at[tile], fsdp=flip(me, 1)
        )

    def turned(mask):
        which = chip
        for bit in bits:
            if mask & bit:
                which = flip(which, bit)
        return pl.ds(pl.multiple_of(which * depth, depth), depth)

    def swaps(share, turn):
        order = [bits[(share + i) % turns] for i in range(turns)]
        stay = [0]
        for bit in order[turn + 1 :]:
            stay += [mask | bit for mask in stay]
        return order[turn], [(mask | order[turn], mask, i) for i, mask in enumerate(stay)]

    def chip_copies(tile, turn):
        made, number = [], 0
        for share, (start, size) in enumerate(shares):
            for earlier in range(turns):
                bit, moves = swaps(share, earlier)
                for goes, _, slot in moves:
                    if earlier == turn:
                        made.append(
                            remote(
                                held.at[tile, turned(goes), pl.ds(start, size)],
                                chip_came[share * turns + turn].at[tile, slot],
                                chip_sends.at[tile, number],
                                chip_recvs.at[tile, number],
                                fsdp=flip(me, 2 * bit),
                            )
                        )
                    number += 1
        return made

    def span_copies(tile):
        return [
            remote(
                held.at[tile, turned(0), pl.ds(s * own_cols, own_cols)],
                span_came.at[tile, s - 1],
                span_sends.at[tile, s - 1],
                span_recvs.at[tile, s - 1],
                tensor=lax.rem(span + spans - s, spans) * parts + place,
            )
            for s in range(1, spans)
        ]

    @pl.when(step == 0)
    def _():
        load(1 - core)
        partners = [{"fsdp": flip(me, 1)}] + [{"fsdp": flip(me, 2 * bit)} for bit in bits]
        partners += [
            {"tensor": lax.rem(span + s, spans) * parts + place} for s in range(1, spans)
        ]
        side_partners = sides.partners()
        greet(partners + side_partners)

    sides.start_over(step, 2 * tiles, *sides_at)

    @pl.when(step == tiles)
    def _():
        load(core)

    @pl.when(step < tiles)
    def _():
        @pl.when(step >= 2)
        def _():
            core_copy(step - 2).wait_send()

        sent[lax.rem(step, 2)] = tn(x_half[...], grad_ref[...]).astype(LOW)
        core_copy(step).start()

    @pl.when(jnp.logical_and(step >= tiles, step < 2 * tiles))
    def _():
        tile = step - tiles
        total = tn(x_half[...], grad_ref[...])
        core_copy(tile).wait_recv()
        held[tile] = (total + held[tile].astype(F32)).astype(LOW)
        for copy in chip_copies(tile, 0):
            copy.start()

    for turn in range(1, turns + 2):
        tile = step - tiles - turn

        @pl.when(jnp.logical_and(tile >= 0, tile < tiles))
        def _(turn=turn, tile=tile):
            if turn <= turns:
                for copy in chip_copies(tile, turn - 1):
                    copy.wait()
                for share, (start, size) in enumerate(shares):
                    _, moves = swaps(share, turn - 1)
                    for _, stays, slot in moves:
                        where = (tile, turned(stays), pl.ds(start, size))
                        came = chip_came[share * turns + turn - 1][tile, slot]
                        held[where] = (held[where].astype(F32) + came.astype(F32)).astype(LOW)
                for copy in chip_copies(tile, turn) if turn < turns else span_copies(tile):
                    copy.start()
            else:
                total = held[tile, turned(0), :own_cols].astype(F32)
                for s, copy in enumerate(span_copies(tile)):
                    copy.wait()
                    total = total + span_came[tile, s].astype(F32)
                out_ref[...] = total

    @pl.when(step == 2 * tiles + turns)
    def _():
        for last in range(max(0, tiles - 2), tiles):
            core_copy(last).wait_send()
        sides.finish(*sides_at)


def grad_scatter(number, fsdp, parts, spans, x, grads, tiles, earlier=(), sides=NO_SIDES):
    count, width = x.shape
    depth = width // fsdp
    tile = grads.shape[1] // tiles
    own = tile // spans
    turns = fsdp.bit_length() - 2
    shares = column_shares(tile, turns)
    hbm = pl.BlockSpec(memory_space=pl.ANY)
    swapped = turns * (2**turns - 1)
    results = call(
        functools.partial(grad_scatter_kernel, fsdp, parts, spans, tiles, sides),
        [x, grads, *sides.operands],
        [
            pl.BlockSpec((count, width), lambda j: (0, 0)),
            pl.BlockSpec(
                (count, tile),
                lambda j: (0, jnp.where(j < tiles, j, jnp.minimum(j - tiles, tiles - 1))),
            ),
            *[hbm] * len(sides.operands),
        ],
        earlier,
        grid=(2 * tiles + turns + 1,),
        out_specs=[
            pl.BlockSpec((depth, own), lambda j: (0, jnp.maximum(j - (tiles + turns + 1), 0))),
            *[hbm] * len(sides.out_shapes),
        ],
        out_shape=[jax.ShapeDtypeStruct((depth, own * tiles), F32), *sides.out_shapes],
        scratch_shapes=[
            pltpu.VMEM((count, width // 2), LOW),
            pltpu.VMEM((2, width // 2, tile), LOW),
            pltpu.VMEM((tiles, width // 2, tile), LOW),
            pltpu.SemaphoreType.DMA((2,)),
            pltpu.SemaphoreType.DMA((tiles,)),
            pltpu.SemaphoreType.DMA((tiles, swapped)),
            pltpu.SemaphoreType.DMA((tiles, swapped)),
            pltpu.VMEM((tiles, spans - 1, depth, own), LOW),
            pltpu.SemaphoreType.DMA((tiles, spans - 1)),
            pltpu.SemaphoreType.DMA((tiles, spans - 1)),
            *[
                pltpu.VMEM((tiles, 2 ** (turns - 1 - turn), depth, size), LOW)
                for _, size in shares
                for turn in range(turns)
            ],
            *sides.scratch,
        ],
        compiler_params=pltpu.CompilerParams(
            collective_id=number, has_side_effects=True, vmem_limit_bytes=56 * MIB
        ),
        cost_estimate=pl.CostEstimate(
            flops=2 * count * width * tile * tiles,
            bytes_accessed=2 * count * width + 4 * count * tile * tiles,
            transcendentals=0,
        ),
        name="grad_scatter",
    )
    return results[0], *sides.results(results[1:])


def project_kernel(tiles, rows_ref, weight_ref, pre_ref, value_ref, query_sq_ref, key_sq_ref):
    step = pl.program_id(0)
    result = nn(rows_ref[...], weight_ref[...])
    squares = jnp.sum(result * result, axis=1, keepdims=True)

    @pl.when(step < 2 * tiles)
    def _():
        pre_ref[...] = result

    for first, ref in ((0, query_sq_ref), (tiles, key_sq_ref)):

        @pl.when(step == first)
        def _(ref=ref):
            ref[...] = squares

        @pl.when(jnp.logical_and(step > first, step < first + tiles))
        def _(ref=ref):
            ref[...] += squares

    @pl.when(step >= 2 * tiles)
    def _():
        value_ref[...] = result.astype(LOW)


def project(inputs, full):
    rows, depth = inputs.shape
    cols = full.shape[1] // 3
    tile = min(512, cols)
    tiles = cols // tile
    column = pl.BlockSpec((rows, 1), lambda j: (0, 0))
    return pl.pallas_call(
        functools.partial(project_kernel, tiles),
        grid=(3 * tiles,),
        in_specs=[
            pl.BlockSpec((rows, depth), lambda j: (0, 0)),
            pl.BlockSpec((depth, tile), lambda j: (0, j)),
        ],
        out_specs=[
            pl.BlockSpec((rows, tile), lambda j: (0, jnp.minimum(j, 2 * tiles - 1))),
            pl.BlockSpec((rows, tile), lambda j: (0, jnp.maximum(j - 2 * tiles, 0))),
            column,
            column,
        ],
        out_shape=[
            jax.ShapeDtypeStruct((rows, 2 * cols), F32),
            jax.ShapeDtypeStruct((rows, cols), LOW),
            jax.ShapeDtypeStruct((rows, 1), F32),
            jax.ShapeDtypeStruct((rows, 1), F32),
        ],
        compiler_params=pltpu.CompilerParams(vmem_limit_bytes=48 * MIB),
        cost_estimate=pl.CostEstimate(
            flops=6 * rows * depth * cols,
            bytes_accessed=6 * depth * cols + 10 * rows * cols + 2 * rows * depth,
            transcendentals=0,
        ),
        name="project",
    )(inputs, full)


def attention_specs(heads):
    return (
        pl.BlockSpec((SEQ_LEN, HEAD_DIM), lambda i: (0, i)),
        pl.BlockSpec((SEQ_LEN, HEAD_DIM), lambda i: (0, i + heads)),
        pl.BlockSpec((SEQ_LEN, HEAD_DIM), lambda i: (0, 0)),
        pl.BlockSpec((SEQ_LEN, 1), lambda i: (0, 0)),
        pl.BlockSpec((1, HEAD_DIM), lambda i: (0, i)),
        pl.BlockSpec((None, SEQ_LEN, 1), lambda i: (i, 0, 0)),
        pl.BlockSpec(memory_space=pl.ANY),
    )


def attend(number, rows, parts, pre, value, invs, gains, tables, sides):
    width = value.shape[1]
    heads = width // HEAD_DIM
    head, later, whole, column, gain, lse, hbm = attention_specs(heads)
    low = jax.ShapeDtypeStruct((SEQ_LEN, width), LOW)
    results = call(
        functools.partial(attend_kernel, rows, parts, 1.0 / math.sqrt(HEAD_DIM), heads, sides),
        [pre, pre, value, *invs, *gains, *tables, *sides.operands],
        [head, later, head, column, column, gain, gain, whole, whole]
        + [hbm] * len(sides.operands),
        grid=(heads,),
        out_specs=[head, head, head, lse, *[hbm] * len(sides.out_shapes)],
        out_shape=[
            low,
            low,
            low,
            jax.ShapeDtypeStruct((heads, SEQ_LEN, 1), F32),
            *sides.out_shapes,
        ],
        scratch_shapes=[
            pltpu.VMEM((SEQ_LEN, HEAD_DIM), LOW),
            pltpu.VMEM((SEQ_LEN, HEAD_DIM), LOW),
            *sides.scratch,
        ],
        compiler_params=pltpu.CompilerParams(
            vmem_limit_bytes=40 * MIB, **sides.options(number)
        ),
        cost_estimate=pl.CostEstimate(
            flops=8 * heads * SEQ_LEN * SEQ_LEN * HEAD_DIM,
            bytes_accessed=16 * SEQ_LEN * width,
            transcendentals=heads * SEQ_LEN * SEQ_LEN,
        ),
        name="attend",
    )
    return *results[:4], *sides.results(results[4:])


def attend_back(
    number, rows, parts, rots, value, grad, lse_all, pre, invs, gains, tables, earlier, sides
):
    width = value.shape[1]
    heads = width // HEAD_DIM
    head, later, whole, column, gain, lse, hbm = attention_specs(heads)
    full = jax.ShapeDtypeStruct((SEQ_LEN, width), F32)
    low = jax.ShapeDtypeStruct((SEQ_LEN, width), LOW)
    gain_out = jax.ShapeDtypeStruct((1, width), F32)
    inner = jax.ShapeDtypeStruct((SEQ_LEN, 1), F32)
    results = call(
        functools.partial(
            attend_back_kernel, rows, parts, 1.0 / math.sqrt(HEAD_DIM), heads, sides
        ),
        [*rots, value, grad, lse_all, pre, pre, *invs, *gains, *tables, *sides.operands],
        [head, head, head, head, lse, head, later, column, column, gain, gain, whole, whole]
        + [hbm] * len(sides.operands),
        earlier,
        grid=(heads,),
        out_specs=[head, head, head, gain, gain, column, column, *[hbm] * len(sides.out_shapes)],
        out_shape=[full, full, low, gain_out, gain_out, inner, inner, *sides.out_shapes],
        scratch_shapes=[
            pltpu.VMEM((SEQ_LEN, HEAD_DIM), LOW),
            pltpu.VMEM((SEQ_LEN, HEAD_DIM), LOW),
            pltpu.VMEM((SEQ_LEN, HEAD_DIM), F32),
            pltpu.VMEM((SEQ_LEN, HEAD_DIM), F32),
            *sides.scratch,
        ],
        compiler_params=pltpu.CompilerParams(
            vmem_limit_bytes=48 * MIB, **sides.options(number)
        ),
        cost_estimate=pl.CostEstimate(
            flops=20 * heads * SEQ_LEN * SEQ_LEN * HEAD_DIM,
            bytes_accessed=32 * SEQ_LEN * width,
            transcendentals=heads * SEQ_LEN * SEQ_LEN,
        ),
        name="attend_back",
    )
    return *results[:7], *sides.results(results[7:])


def norm_back(grad_hat, values_hat, inverse, width):
    inner = jnp.sum(grad_hat * values_hat, axis=1, keepdims=True) / width
    return inverse * (grad_hat - values_hat * inner)


def layer(fsdp, tensor, *arguments):
    layer_input, query_weight, key_weight, value_weight, out_weight = arguments[:5]
    gate_weight, up_weight, down_weight = arguments[5:8]
    query_gain, key_gain, attn_gain, ffn_gain, out_cotangent = arguments[8:]
    rows_here, width = layer_input.shape
    head_cols = query_weight.shape[1]
    parts = SEQ_LEN // rows_here
    spans = tensor // parts
    rank = lax.axis_index("tensor")
    place, span = rank % parts, rank // parts

    def to_part(x, shift):
        pairs = [
            (s * parts + p, s * parts + (p + shift) % parts)
            for s in range(spans)
            for p in range(parts)
        ]
        return lax.ppermute(x, "tensor", pairs)

    def to_span(x, shift):
        pairs = [
            (s * parts + p, (s + shift) % spans * parts + p)
            for s in range(spans)
            for p in range(parts)
        ]
        return lax.ppermute(x, "tensor", pairs)

    def gather_shard(shard):
        return lax.all_gather(shard, "fsdp", axis=0, tiled=True)

    def add_pieces(total, came):
        for piece in came:
            total = total + piece.astype(F32)
        return total

    def sum_parts(x):
        total = x
        for p in range(1, parts):
            total = total + jnp.roll(to_part(x, p), p * rows_here, axis=0)
        return total

    same_core = [list(range(c, fsdp, 2)) for c in range(2)]

    def scatter(total):
        return lax.psum_scatter(
            total, "fsdp", scatter_dimension=0, tiled=True, axis_index_groups=same_core
        )

    def own_columns(s):
        return ((span + spans - s) % spans * parts + place) * head_cols

    def gain_here(gain):
        return jnp.concatenate(
            [lax.dynamic_slice_in_dim(gain, own_columns(s), head_cols) for s in range(spans)]
        )[None, :]

    def gain_whole(part):
        whole = jnp.zeros((width,), F32)
        for s in range(spans):
            whole = lax.dynamic_update_slice_in_dim(
                whole, part[0, s * head_cols : (s + 1) * head_cols], own_columns(s), 0
            )
        return whole

    gate_up_shard = jnp.concatenate([gate_weight, up_weight], axis=1)
    down_shard = down_weight.T
    out_shard = out_weight.T
    cols = gate_weight.shape[1]
    shards, plan = [], []
    for s in range(spans):
        for w, shard in enumerate([query_weight, key_weight, value_weight, out_shard]):
            shards.append(shard)
            plan.append((w // 3, s, w % 3 * spans + s, False))
    (full_qkv, full_out), (down_came,), inputs = exchange(
        0,
        fsdp,
        parts,
        spans,
        shards,
        plan,
        sides=Sides(Rows(parts, gather=layer_input)),
        sends=[down_shard],
    )
    gate_up_first = gather_shard(after(gate_up_shard, inputs))

    local = jnp.arange(SEQ_LEN)
    position = (place + parts - local // rows_here) % parts * rows_here + local % rows_here
    inverse = THETA ** (-jnp.arange(0, HEAD_DIM, 2).astype(F32) / HEAD_DIM)
    angles = position.astype(F32)[:, None] * inverse[None, :]
    cos, sin = jnp.cos(angles), jnp.sin(angles)
    tables = (jnp.concatenate([cos, cos], axis=1), jnp.concatenate([-sin, sin], axis=1))
    gains = (gain_here(query_gain), gain_here(key_gain))

    pre, value_low, query_sq, key_sq = project(inputs, full_qkv)
    squares = sum_parts(jnp.concatenate([query_sq, key_sq], axis=1))
    invs = lax.rsqrt(squares / width + EPSILON)
    invs = (invs[:, :1], invs[:, 1:])
    others_spans = range(1, spans)
    sides = Sides(Spans(parts, spans, [(gate_up_shard, 0, cols, spans - s) for s in others_spans]))
    attended, query_rot, key_rot, lse, gate_came = attend(
        13, rows_here, parts, pre, value_low, invs, gains, tables, sides
    )
    branch, low = product_sum(parts, [(attended, 0, full_out, 0, full_out.shape[1])])
    down_shards = jnp.concatenate([down_shard, *[down_came[s - 1] for s in others_spans]], axis=1)
    gate_up_first, low, down_shards = lax.optimization_barrier((gate_up_first, low, down_shards))
    full_down = gather_shard(down_shards)
    sides = Sides(
        Rows(parts, deliver=low),
        Spans(parts, spans, [(gate_up_shard, 1, cols, spans - s) for s in others_spans]),
    )
    full_gate, _, came, up_came = exchange(
        1, fsdp, parts, spans, gate_came, [(s - 1, s, 0, True) for s in others_spans], sides=sides
    )
    branch = add_pieces(branch, came)
    branch_inv = lax.rsqrt(jnp.mean(branch * branch, axis=1, keepdims=True) + EPSILON)
    branch_hat = branch * branch_inv
    middle = layer_input.astype(F32) + branch_hat * attn_gain
    half = rows_here // 2
    halves = [slice(0, half), slice(half, rows_here)]
    middle_low = [middle[h].astype(LOW) for h in halves]
    grad_out = out_cotangent.astype(F32)
    full_up, _, *mixed = exchange(
        2,
        fsdp,
        parts,
        spans,
        up_came,
        [(s - 1, s, 0, True) for s in others_spans],
        sides=Sides(*[Rows(parts, gather=rows) for rows in middle_low]),
    )
    full_gate_up = [((gate_up_first, 0), (gate_up_first, 1))]
    full_gate_up += [((gate, 0), (up, 0)) for gate, up in zip(full_gate, full_up)]
    gates, uppers, hiddens = [None] * 2, [None] * 2, [None] * 2
    back, outputs, ffn_gain_parts, grad_middles, attn_gain_parts = [None] * 2, [], [], [], []

    def down_pairs(c):
        return [(hiddens[c], s, full_down, s, cols) for s in range(spans)]

    def up_pairs(c):
        return [
            (grad, s, array, run, cols)
            for s in range(spans)
            for grad, (array, run) in zip(back[c], full_gate_up[s])
        ]

    def turn(c, total, came):
        second = add_pieces(total, came)
        second_inv = lax.rsqrt(jnp.mean(second * second, axis=1, keepdims=True) + EPSILON)
        second_hat = second * second_inv
        outputs.append((middle[halves[c]] + second_hat * ffn_gain).astype(LOW))
        grad = grad_out[halves[c]]
        ffn_gain_parts.append(jnp.sum(grad * second_hat, axis=0))
        return norm_back(grad * ffn_gain, second_hat, second_inv, width).astype(LOW)

    part_cols = cols // 2

    def to_spans(array, run, width):
        each = array.shape[1] // spans // width
        return Spans(parts, spans, [(array, s * each + run, width, s) for s in others_spans])

    def back_to_branch(c, total, came):
        grad_middle = grad_out[halves[c]] + add_pieces(total, came)
        hat = branch_hat[halves[c]]
        grad_middles.append(grad_middle)
        attn_gain_parts.append(jnp.sum(grad_middle * hat, axis=0))
        return norm_back(grad_middle * attn_gain, hat, branch_inv[halves[c]], width).astype(LOW)

    gates[0], uppers[0], hiddens[0] = feed_up(mixed[0], full_gate_up, cols)
    second_first, low = product_sum(parts, down_pairs(0))
    gates[1], uppers[1], hiddens[1], came = feed_up(
        mixed[1], full_gate_up, cols, 4, Sides(Rows(parts, deliver=low))
    )
    grad_second = turn(0, second_first, came)
    second_last, low, grad_rows_first = product_sum(
        parts, down_pairs(1), [], 5, Sides(Rows(parts, gather=grad_second))
    )
    *back[0], came = feed_up_back(
        grad_rows_first, full_down, gates[0], uppers[0], [], 6, Sides(Rows(parts, deliver=low))
    )
    grad_second = turn(1, second_last, came)
    mixed_grad_first, low, grad_rows_last = product_sum(
        parts, up_pairs(0), [], 7, Sides(Rows(parts, gather=grad_second))
    )
    grad_rows = [grad_rows_first, grad_rows_last]
    now, came = weight_grad_half(
        8,
        fsdp,
        grad_rows,
        [(hiddens, 0, spans * cols)],
        sides=Sides(Rows(parts, deliver=low)),
    )
    down_terms = scatter(now)
    grad_branch = back_to_branch(0, mixed_grad_first, came)
    back[1] = feed_up_back(grad_rows_last, full_down, gates[1], uppers[1], [now])
    mixed_grad_last, low, branch_first = product_sum(
        parts, up_pairs(1), [], 9, Sides(Rows(parts, gather=grad_branch))
    )
    backs = list(zip(*back))
    gate_up_grad = {}
    for s in reversed(range(spans)):
        entries = [(list(arrays), s * cols, cols) for arrays in backs]
        if s == spans - 1:
            jobs = [Rows(parts, deliver=low)]
        elif s:
            jobs = []
        else:
            jobs = [Rows(parts, gather=grad_branch), to_spans(down_terms, 0, part_cols)]
        now, *results = weight_grad_half(10 + s, fsdp, mixed, entries, [now], Sides(*jobs))
        if s:
            gate_up_grad[s] = scatter(now)
        if s == spans - 1:
            grad_branch = back_to_branch(1, mixed_grad_last, results[0])
    branch_last, down_came_first = results
    output = jnp.concatenate(outputs, axis=0)
    ffn_gain_part, attn_gain_part = sum(ffn_gain_parts), sum(attn_gain_parts)
    grad_middle = jnp.concatenate(grad_middles, axis=0)
    grad_branch_rows = jnp.concatenate(
        [
            piece[p * half : (p + 1) * half]
            for p in range(parts)
            for piece in (branch_first, branch_last)
        ],
        axis=0,
    )
    grad_attended = nn(grad_branch_rows, full_out).astype(LOW)
    out_total, down_came_last = weight_grad_half(
        30,
        fsdp,
        [grad_branch_rows],
        [([attended], 0, attended.shape[1])],
        [grad_attended],
        Sides(to_spans(down_terms, 1, part_cols)),
    )
    *away, out_total = lax.optimization_barrier(
        (*[gate_up_grad[s] for s in others_spans], out_total)
    )
    gate_up_grad.update(zip(others_spans, away))
    out_terms = scatter(out_total)
    (
        query_gained,
        key_gained,
        grad_value,
        query_gain_part,
        key_gain_part,
        query_inner,
        key_inner,
        gate_came,
    ) = attend_back(
        12,
        rows_here,
        parts,
        (query_rot, key_rot),
        value_low,
        grad_attended,
        lse,
        pre,
        invs,
        gains,
        tables,
        [out_total],
        Sides(Spans(parts, spans, [(gate_up_grad[s], 0, cols, s) for s in others_spans])),
    )
    out_terms, now, grad_value = lax.optimization_barrier((out_terms, now, grad_value))
    gate_up_grad[0] = scatter(now)
    down_came = [jnp.concatenate(pair, axis=1) for pair in zip(down_came_first, down_came_last)]
    down_grad = add_pieces(down_terms[:, :cols].astype(F32), down_came)
    inners = sum_parts(jnp.concatenate([query_inner, key_inner], axis=1)) / width
    local_width = value_low.shape[1]
    grad_query = invs[0] * (query_gained - pre[:, :local_width] * invs[0] * inners[:, :1])
    grad_key = invs[1] * (key_gained - pre[:, local_width:] * invs[1] * inners[:, 1:])
    grad_qkv = jnp.concatenate(
        [grad_query.astype(LOW), grad_key.astype(LOW), grad_value], axis=1
    )
    sides = Sides(Spans(parts, spans, [(gate_up_grad[s], 2, part_cols, s) for s in others_spans]))
    total, low, up_came_first = product_sum(
        parts,
        [(grad_qkv, 0, full_qkv, 0, full_qkv.shape[1])],
        [],
        32,
        sides,
        grad_middle,
    )
    gain_parts = [gain_whole(query_gain_part), gain_whole(key_gain_part)]
    sides = Sides(
        SumAll(fsdp, tensor, jnp.stack([*gain_parts, attn_gain_part, ffn_gain_part])),
        Rows(parts, deliver=low),
        Spans(parts, spans, [(out_terms, s, head_cols, s) for s in others_spans]),
        Spans(parts, spans, [(gate_up_grad[s], 3, part_cols, s) for s in others_spans]),
    )
    qkv_grad, gain_grads, came, out_came, up_came_last = grad_scatter(
        31, fsdp, parts, spans, inputs, grad_qkv, 3, [], sides
    )
    input_grad = add_pieces(total, came)
    out_grad = add_pieces(out_terms[:, :head_cols].astype(F32), out_came)
    up_came = [jnp.concatenate(pair, axis=1) for pair in zip(up_came_first, up_came_last)]
    gate_grad = add_pieces(gate_up_grad[0][:, :cols].astype(F32), gate_came)
    up_grad = add_pieces(gate_up_grad[0][:, cols:].astype(F32), up_came)
    query_grad, key_grad, value_grad = jnp.split(qkv_grad, 3, axis=1)
    return (
        output,
        input_grad,
        query_grad,
        key_grad,
        value_grad,
        out_grad.T,
        gate_grad,
        up_grad,
        down_grad.T,
        *gain_grads,
    )


def solution(mesh):
    columns, rows = P("fsdp", "tensor"), P("tensor", "fsdp")
    tokens = P(("fsdp", "tensor"), None)
    weights = (columns, columns, columns, rows, columns, columns, rows)
    return jax.shard_map(
        functools.partial(layer, mesh.shape["fsdp"], mesh.shape["tensor"]),
        mesh=mesh,
        in_specs=(tokens, *weights, P(), P(), P(), P(), tokens),
        out_specs=(tokens, tokens, *weights, P(), P(), P(), P()),
        check_vma=False,
    )
```

```python
import functools
import math

import jax
import jax.numpy as jnp
from jax import lax
from jax.experimental import pallas as pl
from jax.experimental.pallas import tpu as pltpu
from jax.sharding import PartitionSpec as P

HEAD_DIM = 128
SEQ_LEN = 1024
EPSILON = 1e-06
THETA = 500000.0
BLOCK = 256
LOW = jnp.bfloat16
F32 = jnp.float32


def nn(a, b):
    return lax.dot_general(a, b, (((1,), (0,)), ((), ())), preferred_element_type=F32)


def nt(a, b):
    return lax.dot_general(a, b, (((1,), (1,)), ((), ())), preferred_element_type=F32)


def tn(a, b):
    return lax.dot_general(a, b, (((0,), (0,)), ((), ())), preferred_element_type=F32)


def after(x, *earlier):
    return lax.optimization_barrier((x, *earlier))[0]


def block_start(place, block, rows, parts):
    part = block * BLOCK // rows
    return pl.multiple_of(
        lax.rem(place + parts - part, parts) * rows + block * BLOCK % rows, BLOCK
    )


def masked(scores):
    row = lax.broadcasted_iota(jnp.int32, scores.shape, 0)
    col = lax.broadcasted_iota(jnp.int32, scores.shape, 1)
    return jnp.where(row + (scores.shape[1] - scores.shape[0]) >= col, scores, -1e30)


def attend_kernel(rows, parts, scale, heads, sides, *refs):
    query_ref, key_ref, value_ref, query_inv_ref, key_inv_ref = refs[:5]
    query_gain_ref, key_gain_ref, cos_ref, sin_ref = refs[5:9]
    side_refs, refs = refs[9 : 9 + len(sides.operands)], refs[9 + len(sides.operands) :]
    out_ref, query_rot_ref, key_rot_ref, lse_ref = refs[:4]
    side_outs, refs = refs[4 : 4 + len(sides.out_shapes)], refs[4 + len(sides.out_shapes) :]
    key_seq, value_seq = refs[:2]
    sides_at = (side_refs, side_outs, refs[2:])
    place = lax.rem(lax.axis_index("tensor"), parts)

    @pl.when(pl.program_id(0) == 0)
    def _():
        greet(sides.partners())

    sides.start_over(pl.program_id(0), heads, *sides_at)
    half = HEAD_DIM // 2
    for block in range(SEQ_LEN // BLOCK):
        here = pl.ds(block_start(place, block, rows, parts), BLOCK)
        there = pl.ds(block * BLOCK, BLOCK)
        cos, sin = cos_ref[here], sin_ref[here]
        key = key_ref[here] * key_inv_ref[here] * key_gain_ref[...]
        key = (key * cos + pltpu.roll(key, half, 1) * sin).astype(LOW)
        key_rot_ref[here] = key
        key_seq[there] = key
        value_seq[there] = value_ref[here]
        query = query_ref[here] * query_inv_ref[here] * query_gain_ref[...]
        query = (query * cos + pltpu.roll(query, half, 1) * sin).astype(LOW)
        query_rot_ref[here] = query
        span = (block + 1) * BLOCK
        scores = masked(nt(query, key_seq[:span]) * scale)
        top = jnp.max(scores, axis=1, keepdims=True)
        exps = jnp.exp(scores - top)
        total = jnp.sum(exps, axis=1, keepdims=True)
        weights = (exps * (1.0 / total)).astype(LOW)
        out_ref[here] = nn(weights, value_seq[:span]).astype(LOW)
        lse_ref[here] = top + jnp.log(total)

    @pl.when(pl.program_id(0) == heads - 1)
    def _():
        sides.finish(*sides_at)


def attend_back_kernel(rows, parts, scale, heads, sides, *refs):
    query_rot_ref, key_rot_ref, value_ref, grad_ref, lse_ref, query_ref, key_ref = refs[:7]
    query_inv_ref, key_inv_ref, query_gain_ref, key_gain_ref, cos_ref, sin_ref = refs[7:13]
    side_refs, refs = refs[13 : 13 + len(sides.operands)], refs[13 + len(sides.operands) :]
    query_out_ref, key_out_ref, value_out_ref = refs[:3]
    query_gain_out_ref, key_gain_out_ref, query_inner_ref, key_inner_ref = refs[3:7]
    side_outs, refs = refs[7 : 7 + len(sides.out_shapes)], refs[7 + len(sides.out_shapes) :]
    key_seq, value_seq, key_acc, value_acc = refs[:4]
    sides_at = (side_refs, side_outs, refs[4:])
    place = lax.rem(lax.axis_index("tensor"), parts)
    half = HEAD_DIM // 2
    count = SEQ_LEN // BLOCK

    @pl.when(pl.program_id(0) == 0)
    def _():
        if sides.jobs:
            greet(sides.partners())
        query_inner_ref[...] = jnp.zeros_like(query_inner_ref)
        key_inner_ref[...] = jnp.zeros_like(key_inner_ref)

    sides.start_over(pl.program_id(0), heads, *sides_at)

    def finish(grad, here, values_ref, inv_ref, gain_ref, out_ref, inner_ref):
        back = grad * cos_ref[here] - pltpu.roll(grad, half, 1) * sin_ref[here]
        hat = values_ref[here] * inv_ref[here]
        gained = back * gain_ref[...]
        out_ref[here] = gained.astype(LOW)
        inner_ref[here] += jnp.sum(gained * hat, axis=1, keepdims=True)
        return jnp.sum(back * hat, axis=0, keepdims=True)

    query_gain_sum = jnp.zeros((1, HEAD_DIM), F32)
    for block in range(count):
        here = pl.ds(block_start(place, block, rows, parts), BLOCK)
        there = pl.ds(block * BLOCK, BLOCK)
        key_seq[there] = key_rot_ref[here]
        value_seq[there] = value_ref[here]
        query, grad = query_rot_ref[here], grad_ref[here]
        span = (block + 1) * BLOCK
        scores = masked(nt(query, key_seq[:span]) * scale)
        probs = jnp.exp(scores - lse_ref[here])
        weights = probs.astype(LOW)
        grad_probs = nt(grad, value_seq[:span])
        delta = jnp.sum(probs * grad_probs, axis=1, keepdims=True)
        grad_scores = (probs * (grad_probs - delta) * scale).astype(LOW)
        value_part = tn(weights, grad)
        key_part = tn(grad_scores, query)
        past = block * BLOCK
        if block:
            key_acc[:past] += key_part[:past]
            value_acc[:past] += value_part[:past]
        key_acc[past:span] = key_part[past:]
        value_acc[past:span] = value_part[past:]
        query_gain_sum += finish(
            nn(grad_scores, key_seq[:span]),
            here,
            query_ref,
            query_inv_ref,
            query_gain_ref,
            query_out_ref,
            query_inner_ref,
        )
    query_gain_out_ref[...] = query_gain_sum
    key_gain_sum = jnp.zeros((1, HEAD_DIM), F32)
    for block in range(count):
        here = pl.ds(block_start(place, block, rows, parts), BLOCK)
        there = pl.ds(block * BLOCK, BLOCK)
        value_out_ref[here] = value_acc[there].astype(LOW)
        key_gain_sum += finish(
            key_acc[there],
            here,
            key_ref,
            key_inv_ref,
            key_gain_ref,
            key_out_ref,
            key_inner_ref,
        )
    key_gain_out_ref[...] = key_gain_sum

    @pl.when(pl.program_id(0) == heads - 1)
    def _():
        sides.finish(*sides_at)


MESH = pl.DeviceIdType.MESH
MIB = 2**20
CHUNKS = 4


def flip(index, bit):
    return index + bit - 2 * bit * lax.rem(lax.div(index, bit), 2)


def row_shares(rows, count):
    units = rows // 16
    sizes = [16 * (units // count + (i < units % count)) for i in range(count)]
    starts = [sum(sizes[:i]) for i in range(count)]
    return list(zip(starts, sizes))


def call(kernel, operands, in_specs, earlier=(), **options):
    count = len(operands)

    def body(*refs):
        kernel(*refs[:count], *refs[count + len(earlier) :])

    specs = [*in_specs, *[pl.BlockSpec(memory_space=pl.ANY)] * len(earlier)]
    return pl.pallas_call(body, in_specs=specs, **options)(*operands, *earlier)


def greet(partners):
    barrier = pltpu.get_barrier_semaphore()
    for partner in partners:
        pl.semaphore_signal(barrier, inc=1, device_id=partner, device_id_type=MESH)
    pl.semaphore_wait(barrier, len(partners))


def remote(src, dst, send_sem, recv_sem, **device):
    return pltpu.make_async_remote_copy(
        src_ref=src,
        dst_ref=dst,
        send_sem=send_sem,
        recv_sem=recv_sem,
        device_id=device,
        device_id_type=MESH,
    )


class Copies:
    def __init__(self, send_sems, recv_sems):
        self.send_sems, self.recv_sems = send_sems, recv_sems
        self.used = 0
        self.open = []
        self.moves = []

    def send(self, src, dst, **device):
        copy = remote(
            src, dst, self.send_sems.at[self.used], self.recv_sems.at[self.used], **device
        )
        self.used += 1
        copy.start()
        self.open.append(copy.wait_send)
        return copy

    def move(self, src, hold, dst):
        load = pltpu.make_async_copy(src, hold, self.send_sems.at[self.used])
        store = pltpu.make_async_copy(hold, dst, self.recv_sems.at[self.used])
        self.used += 1
        load.start()
        self.moves.append((load, store))

    def finish(self):
        for load, store in self.moves:
            load.wait()
            store.start()
        for wait in self.open:
            wait()
        for _, store in self.moves:
            store.wait()


class Rows:
    def __init__(self, parts, gather=None, deliver=None):
        self.parts, self.gather = parts, gather is not None
        self.operands = [gather if self.gather else deliver]
        rows, width = self.operands[0].shape
        self.rows = rows if self.gather else rows // parts
        self.chunk = self.rows // CHUNKS
        count = parts if self.gather else parts - 1
        self.out_shapes = [jax.ShapeDtypeStruct((count, self.rows, width), LOW)]
        count = CHUNKS * parts
        self.scratch = [pltpu.SemaphoreType.DMA((count,)), pltpu.SemaphoreType.DMA((count,))]
        if self.gather:
            self.scratch.append(pltpu.VMEM((rows, width), LOW))

    def ranks(self):
        rank = lax.axis_index("tensor")
        place = lax.rem(rank, self.parts)
        shifts = range(1, self.parts)
        if not self.gather:
            shifts = [self.parts - p for p in shifts]
        return [rank - place + lax.rem(place + p, self.parts) for p in shifts]

    def partners(self):
        return [{"tensor": rank} for rank in self.ranks()]

    def copies(self, chunks, refs, outs, send_sems, recv_sems, hold=None):
        made = []
        for chunk in chunks:
            for i, rank in enumerate(self.ranks()):
                first = 0 if self.gather else (i + 1) * self.rows
                src = refs[0].at[pl.ds(first + chunk * self.chunk, self.chunk)]
                dst = outs[0].at[i + 1] if self.gather else outs[0].at[i]
                dst = dst.at[pl.ds(chunk * self.chunk, self.chunk)]
                sem = CHUNKS * i + chunk
                made.append(
                    remote(src, dst, send_sems.at[sem], recv_sems.at[sem], tensor=rank)
                )
        return made

    def load(self, refs, outs, send_sems, recv_sems, hold):
        return pltpu.make_async_copy(refs[0], hold, send_sems.at[CHUNKS * self.parts - 1])

    def store(self, refs, outs, send_sems, recv_sems, hold):
        return pltpu.make_async_copy(hold, outs[0].at[0], recv_sems.at[CHUNKS * self.parts - 1])

    def start(self, chunk, *where):
        if self.gather and chunk == 0:
            self.load(*where).start()
        for copy in self.copies([chunk], *where):
            copy.start()

    def finish(self, *where):
        if self.gather:
            self.load(*where).wait()
            self.store(*where).start()
            self.store(*where).wait()
        for copy in self.copies(range(CHUNKS), *where):
            copy.wait()

    def results(self, outs):
        out = outs[0]
        if self.gather:
            return out.reshape(-1, out.shape[2])
        return [out[i] for i in range(self.parts - 1)]


class Spans:
    def __init__(self, parts, spans, terms):
        self.parts, self.spans, self.terms = parts, spans, terms
        self.operands = [array for array, *_ in terms]
        self.out_shapes = [
            jax.ShapeDtypeStruct((array.shape[0], width), LOW) for array, _, width, _ in terms
        ]
        count = CHUNKS * max(1, len(terms))
        self.scratch = [pltpu.SemaphoreType.DMA((count,)), pltpu.SemaphoreType.DMA((count,))]

    def rank(self, back):
        rank = lax.axis_index("tensor")
        place, span = lax.rem(rank, self.parts), lax.div(rank, self.parts)
        return lax.rem(span + self.spans - back, self.spans) * self.parts + place

    def partners(self):
        return [{"tensor": self.rank(s)} for s in range(1, self.spans)]

    def copies(self, chunks, refs, outs, send_sems, recv_sems):
        made = []
        for chunk in chunks:
            for i, (ref, out, (array, run, width, back)) in enumerate(zip(refs, outs, self.terms)):
                size = array.shape[0] // CHUNKS
                rows, sem = pl.ds(chunk * size, size), CHUNKS * i + chunk
                made.append(
                    remote(
                        ref.at[rows, pl.ds(run * width, width)],
                        out.at[rows],
                        send_sems.at[sem],
                        recv_sems.at[sem],
                        tensor=self.rank(back),
                    )
                )
        return made

    def start(self, chunk, *where):
        for copy in self.copies([chunk], *where):
            copy.start()

    def finish(self, *where):
        for copy in self.copies(range(CHUNKS), *where):
            copy.wait()

    def results(self, outs):
        return list(outs)


class SumAll:
    def __init__(self, fsdp, tensor, array):
        self.operands = [array]
        self.out_shapes = [jax.ShapeDtypeStruct(array.shape, F32)]
        self.turns = [
            (axis, 1 << b)
            for axis, size in (("fsdp", fsdp), ("tensor", tensor))
            for b in range(size.bit_length() - 1)
        ]
        count = len(self.turns)
        self.scratch = [
            pltpu.SemaphoreType.DMA((count + 1,)),
            pltpu.SemaphoreType.DMA((count,)),
            pltpu.VMEM(array.shape, F32),
            pltpu.VMEM((count, *array.shape), F32),
        ]

    def partners(self):
        return [{axis: flip(lax.axis_index(axis), bit)} for axis, bit in self.turns]

    def copy(self, turn, refs, outs, send_sems, recv_sems, total, came):
        axis, bit = self.turns[turn]
        device = {axis: flip(lax.axis_index(axis), bit)}
        return remote(total, came.at[turn], send_sems.at[turn], recv_sems.at[turn], **device)

    def take(self, turn, *where):
        self.copy(turn, *where).wait()
        total, came = where[-2:]
        total[...] += came[turn]

    def start(self, chunk, *where):
        refs, _, send_sems, _, total, _ = where
        if chunk == 0:
            load = pltpu.make_async_copy(refs[0], total, send_sems.at[len(self.turns)])
            load.start()
            load.wait()
        elif chunk < len(self.turns):
            self.take(chunk - 1, *where)
        if chunk < len(self.turns):
            self.copy(chunk, *where).start()

    def finish(self, *where):
        _, outs, send_sems, _, total, _ = where
        count = len(self.turns)
        for turn in range(min(CHUNKS, count) - 1, count):
            self.take(turn, *where)
            if turn + 1 < count:
                self.copy(turn + 1, *where).start()
        store = pltpu.make_async_copy(total, outs[0], send_sems.at[count])
        store.start()
        store.wait()

    def results(self, outs):
        return outs[0]


class Sides:
    def __init__(self, *jobs):
        self.jobs = jobs
        self.operands = [x for job in jobs for x in job.operands]
        self.out_shapes = [x for job in jobs for x in job.out_shapes]
        self.scratch = [x for job in jobs for x in job.scratch]

    def partners(self):
        return [partner for job in self.jobs for partner in job.partners()]

    def each(self, refs, outs, scratch):
        for job in self.jobs:
            counts = len(job.operands), len(job.out_shapes), len(job.scratch)
            yield job, (refs[: counts[0]], outs[: counts[1]], *scratch[: counts[2]])
            refs, outs, scratch = refs[counts[0] :], outs[counts[1] :], scratch[counts[2] :]

    def start(self, chunk, *where):
        for job, own in self.each(*where):
            job.start(chunk, *own)

    def start_over(self, step, steps, *where):
        for job, own in self.each(*where):
            stride = steps // CHUNKS
            if stride < 2 and isinstance(job, Spans):
                stride = 0
            elif stride == 0:
                stride = 1
            for chunk in range(CHUNKS):

                @pl.when(step == min(chunk * stride, steps - 1))
                def _(job=job, own=own, chunk=chunk):
                    job.start(chunk, *own)

    def finish(self, *where):
        for job, own in self.each(*where):
            job.finish(*own)

    def results(self, outs):
        return [job.results(own) for job, (_, own, *_) in self.each([], outs, [])]

    def options(self, number):
        return {"collective_id": number, "has_side_effects": True} if self.jobs else {}


NO_SIDES = Sides()


def exchange_kernel(fsdp, parts, spans, plan, counts, *refs):
    sides, shard_count, send_count, full_count = counts
    rows_count = len(sides.operands)
    rows_refs, refs = refs[:rows_count], refs[rows_count:]
    shard_refs, refs = refs[:shard_count], refs[shard_count:]
    span_refs, refs = refs[:send_count], refs[send_count:]
    full_refs, refs = refs[:full_count], refs[full_count:]
    span_outs, refs = refs[:send_count], refs[send_count:]
    side_outs, refs = refs[: len(sides.out_shapes)], refs[len(sides.out_shapes) :]
    hold_refs, refs = refs[: len(plan)], refs[len(plan) :]
    sides_at = (rows_refs, side_outs, refs[:-2])
    copies = Copies(*refs[-2:])
    me, rank = lax.axis_index("fsdp"), lax.axis_index("tensor")
    place, span = lax.rem(rank, parts), lax.div(rank, parts)
    bits = [1 << b for b in range(1, fsdp.bit_length() - 1)]
    span_ranks = [lax.rem(span + s, spans) * parts + place for s in range(1, spans)]
    partners = [{"fsdp": flip(me, bit)} for bit in [1, *bits]] if plan else []
    partners += sides.partners()
    if send_count or any(s and not here for _, s, _, here in plan):
        partners += [{"tensor": r} for r in span_ranks]
    greet(partners)

    def slot(job, mask, share=None):
        group, s, position, _ = plan[job]
        which = me
        for bit in [1, *bits]:
            if mask & bit:
                which = flip(which, bit)
        cols = shard_refs[job].shape[1]
        ref = full_refs[group].at[which, :, pl.ds(position * cols, cols)]
        return ref if share is None else ref.at[pl.ds(*share)]

    depth = shard_refs[0].shape[0] if plan else 16
    shares = row_shares(depth, len(bits))
    jobs = range(len(plan))
    away = [s and not here for _, s, _, here in plan]
    for chunk in range(CHUNKS // 2):
        sides.start(chunk, *sides_at)
    from_span = {
        job: copies.send(shard_refs[job], slot(job, 0), tensor=span_ranks[plan[job][1] - 1])
        for job in jobs
        if away[job]
    }
    for chunk in range(CHUNKS // 2, CHUNKS):
        sides.start(chunk, *sides_at)
    over = []
    for ref, out in zip(span_refs, span_outs):
        for s, r in enumerate(span_ranks):
            over.append(copies.send(ref, out.at[s], tensor=r))
    for job in jobs:
        if not away[job]:
            copies.move(shard_refs[job], hold_refs[job], slot(job, 0))

    arriving = {}
    held = {(job, p): [0] for job in jobs for p in range(len(shares))}

    def source(job, mask, share):
        if mask == 0 and not away[job]:
            return shard_refs[job].at[pl.ds(*share)]
        return slot(job, mask, share)

    def send_step(job, step):
        for p, share in enumerate(shares):
            bit = bits[(p + step) % len(bits)]
            for mask in held[job, p]:
                arriving[job, p, mask | bit] = copies.send(
                    source(job, mask, share), slot(job, mask, share), fsdp=flip(me, bit)
                )

    def take_step(job, step):
        for p in range(len(shares)):
            bit = bits[(p + step) % len(bits)]
            came = [mask | bit for mask in held[job, p]]
            for mask in came:
                arriving[job, p, mask].wait_recv()
            held[job, p] += came

    for step in range(len(bits) + 1):
        for job in jobs:
            if step == 0 and away[job]:
                from_span[job].wait_recv()
            if step:
                take_step(job, step - 1)
            if step < len(bits):
                send_step(job, step)
            else:
                for mask in range(0, fsdp, 2):
                    whole = (0, depth)
                    over.append(
                        copies.send(
                            source(job, mask, whole), slot(job, mask), fsdp=flip(me, 1)
                        )
                    )
    for copy in over:
        copy.wait_recv()
    copies.finish()
    sides.finish(*sides_at)


def exchange(number, fsdp, parts, spans, shards=(), plan=(), sides=NO_SIDES, sends=(), earlier=()):
    bits = fsdp.bit_length() - 2
    per_job = 2 + bits * (2**bits - 1) + 2**bits
    count = len(plan) * per_job + len(sends) * spans + 1
    hbm = pl.BlockSpec(memory_space=pl.ANY)
    full_count = 1 + max([group for group, *_ in plan], default=-1)
    widths = [0] * full_count
    for shard, (group, *_) in zip(shards, plan):
        widths[group] += shard.shape[1]
    depth = shards[0].shape[0] if plan else 0
    outs = [jax.ShapeDtypeStruct((fsdp, depth, width), LOW) for width in widths]
    outs += [jax.ShapeDtypeStruct((spans - 1, *x.shape), LOW) for x in sends]
    inputs = [*shards, *sends]
    scratch = [pltpu.SemaphoreType.DMA((count,)), pltpu.SemaphoreType.DMA((count,))]
    inputs = [*sides.operands, *inputs]
    outs += sides.out_shapes
    scratch = [*sides.scratch, *scratch]
    scratch = [
        *[pltpu.VMEM(x.shape if here or not s else (16, 128), LOW) for x, (_, s, _, here) in zip(shards, plan)],
        *scratch,
    ]
    results = call(
        functools.partial(
            exchange_kernel,
            fsdp,
            parts,
            spans,
            plan,
            (sides, len(shards), len(sends), full_count),
        ),
        inputs,
        [hbm] * len(inputs),
        earlier,
        out_shape=outs,
        out_specs=[hbm] * len(outs),
        scratch_shapes=scratch,
        compiler_params=pltpu.CompilerParams(collective_id=number, has_side_effects=True),
        name="exchange",
    )
    full = [r.reshape(fsdp * depth, -1) for r in results[:full_count]]
    came = results[full_count : full_count + len(sends)]
    return full, came, *sides.results(results[full_count + len(sends) :])


def sum_kernel(pairs, own, has_addend, sides, steps, *refs):
    step = pl.program_id(0)
    first_side = 2 * pairs + has_addend
    count = first_side + len(sides.operands)
    own_ref, low_ref, outs = refs[count], refs[count + 1], refs[count + 2 :]
    outs, scratch = outs[: len(sides.out_shapes)], outs[len(sides.out_shapes) :]
    sides_at = (refs[first_side:count], outs, scratch)
    if sides.jobs:

        @pl.when(step == 0)
        def _():
            greet(sides.partners())

    sides.start_over(step, steps, *sides_at)
    total = None
    for i in range(pairs):
        term = nt(refs[2 * i][...], refs[2 * i + 1][...])
        total = term if total is None else total + term
    own_ref[...] = total[:own] + refs[2 * pairs][...] if has_addend else total[:own]
    low_ref[...] = total.astype(LOW)
    if sides.jobs:

        @pl.when(step == steps - 1)
        def _():
            sides.finish(*sides_at)


def product_sum(parts, pairs, earlier=(), number=None, sides=NO_SIDES, addend=None):
    rows, width = pairs[0][0].shape[0], pairs[0][2].shape[0]
    own = rows // parts
    tile = min(512 if rows * sum(depth for *_, depth in pairs) < 5 * MIB else 256, width)
    specs, operands, flops = [], [], 0
    for a, a_run, b, b_run, depth in pairs:
        specs.append(pl.BlockSpec((rows, depth), lambda j, run=a_run: (0, run)))
        specs.append(pl.BlockSpec((tile, depth), lambda j, run=b_run: (j, run)))
        operands += [a, b]
        flops += 2 * rows * depth * width
    if addend is not None:
        specs.append(pl.BlockSpec((own, tile), lambda j: (0, j)))
        operands.append(addend)
    hbm = pl.BlockSpec(memory_space=pl.ANY)
    steps = width // tile
    results = call(
        functools.partial(sum_kernel, len(pairs), own, addend is not None, sides, steps),
        [*operands, *sides.operands],
        [*specs, *[hbm] * len(sides.operands)],
        earlier,
        grid=(steps,),
        out_specs=[
            pl.BlockSpec((own, tile), lambda j: (0, j)),
            pl.BlockSpec((rows, tile), lambda j: (0, j)),
            *[hbm] * len(sides.out_shapes),
        ],
        out_shape=[
            jax.ShapeDtypeStruct((own, width), F32),
            jax.ShapeDtypeStruct((rows, width), LOW),
            *sides.out_shapes,
        ],
        scratch_shapes=sides.scratch,
        compiler_params=pltpu.CompilerParams(
            vmem_limit_bytes=56 * MIB, **sides.options(number)
        ),
        cost_estimate=pl.CostEstimate(
            flops=flops, bytes_accessed=flops // rows + 4 * rows * width, transcendentals=0
        ),
        name="product_sum",
    )
    return *results[:2], *sides.results(results[2:])


def up_kernel(spans, tiles, sides, *refs):
    mixed_ref, weight_refs = refs[0], refs[1 : 1 + 2 * spans]
    refs = refs[1 + 2 * spans :]
    side_refs, refs = refs[: len(sides.operands)], refs[len(sides.operands) :]
    gate_ref, upper_ref, hidden_ref, outs = *refs[:3], refs[3:]
    outs, scratch = outs[: len(sides.out_shapes)], outs[len(sides.out_shapes) :]
    sides_at = (side_refs, outs, scratch)
    step = pl.program_id(0)
    if sides.jobs:

        @pl.when(step == 0)
        def _():
            greet(sides.partners())

    sides.start_over(step, spans * tiles, *sides_at)
    for s in range(spans):

        @pl.when(jnp.logical_and(step >= s * tiles, step < (s + 1) * tiles))
        def _(s=s):
            gate = nn(mixed_ref[...], weight_refs[2 * s][...])
            upper = nn(mixed_ref[...], weight_refs[2 * s + 1][...])
            gate_ref[...] = gate
            upper_ref[...] = upper
            hidden_ref[...] = (gate * jax.nn.sigmoid(gate) * upper).astype(LOW)

    if sides.jobs:

        @pl.when(step == spans * tiles - 1)
        def _():
            sides.finish(*sides_at)


def feed_up(mixed, gate_ups, cols, number=None, sides=NO_SIDES):
    rows, depth = mixed.shape
    spans = len(gate_ups)
    tile = min(512, cols)
    tiles = cols // tile
    hbm = pl.BlockSpec(memory_space=pl.ANY)
    out = pl.BlockSpec((rows, tile), lambda j: (0, j))
    operands, specs = [mixed], [pl.BlockSpec((rows, depth), lambda j: (0, 0))]
    for s, pair in enumerate(gate_ups):
        for array, run in pair:
            operands.append(array)
            specs.append(
                pl.BlockSpec(
                    (depth, tile),
                    lambda j, s=s, run=run: (0, jnp.clip(j - s * tiles, 0, tiles - 1) + run * tiles),
                )
            )
    whole = (rows, spans * cols)
    results = call(
        functools.partial(up_kernel, spans, tiles, sides),
        [*operands, *sides.operands],
        [*specs, *[hbm] * len(sides.operands)],
        grid=(spans * tiles,),
        out_specs=[out, out, out, *[hbm] * len(sides.out_shapes)],
        out_shape=[
            jax.ShapeDtypeStruct(whole, F32),
            jax.ShapeDtypeStruct(whole, F32),
            jax.ShapeDtypeStruct(whole, LOW),
            *sides.out_shapes,
        ],
        scratch_shapes=sides.scratch,
        compiler_params=pltpu.CompilerParams(
            vmem_limit_bytes=56 * MIB, **sides.options(number)
        ),
        cost_estimate=pl.CostEstimate(
            flops=4 * rows * depth * spans * cols,
            bytes_accessed=4 * depth * spans * cols + 10 * rows * spans * cols,
            transcendentals=rows * spans * cols,
        ),
        name="feed_up",
    )
    return *results[:3], *sides.results(results[3:])


def up_back_kernel(spans, tiles, sides, *refs):
    steps = spans * tiles
    grad_ref, down_refs, refs = refs[0], refs[1 : 1 + spans], refs[1 + spans :]
    gate_ref, upper_ref, refs = refs[0], refs[1], refs[2:]
    side_refs, refs = refs[: len(sides.operands)], refs[len(sides.operands) :]
    gate_out_ref, up_out_ref, outs = refs[0], refs[1], refs[2:]
    outs, scratch = outs[: len(sides.out_shapes)], outs[len(sides.out_shapes) :]
    sides_at = (side_refs, outs, scratch)
    step = pl.program_id(0)
    if sides.jobs:

        @pl.when(step == 0)
        def _():
            greet(sides.partners())

    sides.start_over(step, steps, *sides_at)
    for s, down_ref in enumerate(down_refs):

        @pl.when(jnp.logical_and(step >= s * tiles, step < (s + 1) * tiles))
        def _(down_ref=down_ref):
            grad = nn(grad_ref[...], down_ref[...])
            gate = gate_ref[...]
            sigmoid = jax.nn.sigmoid(gate)
            scaled = grad * sigmoid
            slope = 1.0 + gate * (1.0 - sigmoid)
            up_out_ref[...] = (scaled * gate).astype(LOW)
            gate_out_ref[...] = (scaled * upper_ref[...] * slope).astype(LOW)

    if sides.jobs:

        @pl.when(step == steps - 1)
        def _():
            sides.finish(*sides_at)


def feed_up_back(grad_rows, down, gate, upper, earlier=(), number=None, sides=NO_SIDES):
    rows, depth = grad_rows.shape
    downs, spans = [down], 1
    tile = min(512, downs[0].shape[1])
    tiles = downs[0].shape[1] // tile
    cols = spans * tiles * tile
    hbm = pl.BlockSpec(memory_space=pl.ANY)
    spec = pl.BlockSpec((rows, tile), lambda j: (0, j))
    out = jax.ShapeDtypeStruct((rows, cols), LOW)
    results = call(
        functools.partial(up_back_kernel, spans, tiles, sides),
        [grad_rows, *downs, gate, upper, *sides.operands],
        [
            pl.BlockSpec((rows, depth), lambda j: (0, 0)),
            *[
                pl.BlockSpec(
                    (depth, tile), lambda j, s=s: (0, jnp.clip(j - s * tiles, 0, tiles - 1))
                )
                for s in range(spans)
            ],
            spec,
            spec,
            *[hbm] * len(sides.operands),
        ],
        earlier,
        grid=(cols // tile,),
        out_specs=[spec, spec, *[hbm] * len(sides.out_shapes)],
        out_shape=[out, out, *sides.out_shapes],
        scratch_shapes=sides.scratch,
        compiler_params=pltpu.CompilerParams(
            vmem_limit_bytes=52 * MIB, **sides.options(number)
        ),
        cost_estimate=pl.CostEstimate(
            flops=2 * rows * depth * cols,
            bytes_accessed=2 * depth * cols + 12 * rows * cols,
            transcendentals=rows * cols,
        ),
        name="feed_up_back",
    )
    return *results[:2], *sides.results(results[2:])


def weight_grad_kernel(fsdp, chunks, tiles, sides, *refs):
    x_refs, refs = refs[:chunks], refs[chunks:]
    grad_refs, refs = refs[: chunks * len(tiles)], refs[chunks * len(tiles) :]
    rows = x_refs[0].shape[0]
    count, outs = len(sides.operands), len(sides.out_shapes)
    side_refs, out_ref, refs = refs[:count], refs[count], refs[count + 1 :]
    side_outs, refs = refs[:outs], refs[outs:]
    x_half, sent, came, send_sems, recv_sems = refs[:5]
    sides_at = (side_refs, side_outs, refs[5:])
    me = lax.axis_index("fsdp")
    core = lax.rem(me, 2)
    total_tiles = sum(tiles)
    depth = x_refs[0].shape[1] // fsdp
    step = pl.program_id(0)

    def load(which):
        for c, x_ref in enumerate(x_refs):
            for i in range(fsdp // 2):
                first = pl.multiple_of((2 * i + which) * depth, depth)
                x_half[c * rows : (c + 1) * rows, i * depth : (i + 1) * depth] = x_ref[
                    :, pl.ds(first, depth)
                ]

    def product(entry):
        total = None
        for c, ref in enumerate(grad_refs[entry * chunks : (entry + 1) * chunks]):
            term = tn(x_half[c * rows : (c + 1) * rows], ref[...])
            total = term if total is None else total + term
        return total

    def copy(tile):
        slot = lax.rem(tile, 2)
        return remote(
            sent.at[slot], came.at[tile], send_sems.at[slot], recv_sems.at[tile], fsdp=flip(me, 1)
        )

    @pl.when(step == 0)
    def _():
        load(1 - core)
        greet([{"fsdp": flip(me, 1)}, *sides.partners()])

    sides.start_over(step, 2 * total_tiles, *sides_at)

    @pl.when(step == total_tiles)
    def _():
        load(core)

    @pl.when(jnp.logical_and(step >= 2, step < total_tiles))
    def _():
        copy(step - 2).wait_send()

    tile = lax.rem(step, total_tiles)
    first = 0
    for entry, count in enumerate(tiles):
        here = jnp.logical_and(tile >= first, tile < first + count)

        @pl.when(jnp.logical_and(here, step < total_tiles))
        def _(entry=entry):
            sent[lax.rem(step, 2)] = product(entry).astype(LOW)

        @pl.when(jnp.logical_and(here, step >= total_tiles))
        def _(entry=entry):
            total = product(entry)
            copy(tile).wait_recv()
            out_ref[...] = (total + came[tile].astype(F32)).astype(LOW)

        first += count

    @pl.when(step < total_tiles)
    def _():
        copy(step).start()

    @pl.when(step == 2 * total_tiles - 1)
    def _():
        for last in range(max(0, total_tiles - 2), total_tiles):
            copy(last).wait_send()
        sides.finish(*sides_at)


def weight_grad_half(number, fsdp, xs, grads, earlier=(), sides=NO_SIDES):
    chunks = len(xs)
    count, width = xs[0].shape
    tile = math.gcd(1024, *[cols for _, _, cols in grads])
    tiles = [cols // tile for _, _, cols in grads]
    total_tiles = sum(tiles)
    firsts = [sum(tiles[:i]) for i in range(len(tiles))]
    cols = tile * total_tiles

    def grad_spec(first, runs, base):
        return pl.BlockSpec(
            (count, tile),
            lambda j: (0, base + jnp.clip(lax.rem(j, total_tiles) - first, 0, runs - 1)),
        )

    hbm = pl.BlockSpec(memory_space=pl.ANY)
    operands = [*xs, *[array for arrays, _, _ in grads for array in arrays]]
    specs = [pl.BlockSpec((count, width), lambda j: (0, 0))] * chunks
    for first, runs, (_, start, _) in zip(firsts, tiles, grads):
        specs += [grad_spec(first, runs, start // tile)] * chunks
    outs = [jax.ShapeDtypeStruct((width // 2, cols), LOW)]
    out_specs = [pl.BlockSpec((width // 2, tile), lambda j: (0, jnp.maximum(j - total_tiles, 0)))]
    scratch = [
        pltpu.VMEM((chunks * count, width // 2), LOW),
        pltpu.VMEM((2, width // 2, tile), LOW),
        pltpu.VMEM((total_tiles, width // 2, tile), LOW),
        pltpu.SemaphoreType.DMA((2,)),
        pltpu.SemaphoreType.DMA((total_tiles,)),
    ]
    operands += sides.operands
    specs += [hbm] * len(sides.operands)
    outs += sides.out_shapes
    out_specs += [hbm] * len(sides.out_shapes)
    scratch += sides.scratch
    results = call(
        functools.partial(weight_grad_kernel, fsdp, chunks, tiles, sides),
        operands,
        specs,
        earlier,
        grid=(2 * total_tiles,),
        out_specs=out_specs,
        out_shape=outs,
        scratch_shapes=scratch,
        compiler_params=pltpu.CompilerParams(
            collective_id=number, has_side_effects=True, vmem_limit_bytes=56 * MIB
        ),
        cost_estimate=pl.CostEstimate(
            flops=2 * chunks * count * width * cols,
            bytes_accessed=chunks * (2 * count * width + 4 * count * cols) + width * cols,
            transcendentals=0,
        ),
        name="weight_grad",
    )
    return results[0], *sides.results(results[1:])


def column_shares(cols, count):
    return [(8 * start, 8 * size) for start, size in row_shares(cols // 8, count)]


def grad_scatter_kernel(fsdp, parts, spans, tiles, sides, *refs):
    x_ref, grad_ref, refs = refs[0], refs[1], refs[2:]
    count, outs = len(sides.operands), len(sides.out_shapes)
    side_refs, out_ref, refs = refs[:count], refs[count], refs[count + 1 :]
    side_outs, refs = refs[:outs], refs[outs:]
    x_half, sent, held, send_sems, recv_sems, chip_sends, chip_recvs = refs[:7]
    span_came, span_sends, span_recvs, refs = *refs[7:10], refs[10:]
    bits = [1 << b for b in range(fsdp.bit_length() - 2)]
    turns = len(bits)
    chip_came, side_scratch = refs[: turns * turns], refs[turns * turns :]
    sides_at = (side_refs, side_outs, side_scratch)
    me, rank = lax.axis_index("fsdp"), lax.axis_index("tensor")
    core, chip = lax.rem(me, 2), lax.div(me, 2)
    place, span = lax.rem(rank, parts), lax.div(rank, parts)
    depth = x_ref.shape[1] // fsdp
    tile_cols = grad_ref.shape[1]
    own_cols = tile_cols // spans
    shares = column_shares(tile_cols, turns)
    step = pl.program_id(0)

    def load(which):
        for i in range(fsdp // 2):
            first = pl.multiple_of((2 * i + which) * depth, depth)
            x_half[:, i * depth : (i + 1) * depth] = x_ref[:, pl.ds(first, depth)]

    def core_copy(tile):
        slot = lax.rem(tile, 2)
        return remote(
            sent.at[slot], held.at[tile], send_sems.at[slot], recv_sems.at[tile], fsdp=flip(me, 1)
        )

    def turned(mask):
        which = chip
        for bit in bits:
            if mask & bit:
                which = flip(which, bit)
        return pl.ds(pl.multiple_of(which * depth, depth), depth)

    def swaps(share, turn):
        order = [bits[(share + i) % turns] for i in range(turns)]
        stay = [0]
        for bit in order[turn + 1 :]:
            stay += [mask | bit for mask in stay]
        return order[turn], [(mask | order[turn], mask, i) for i, mask in enumerate(stay)]

    def chip_copies(tile, turn):
        made, number = [], 0
        for share, (start, size) in enumerate(shares):
            for earlier in range(turns):
                bit, moves = swaps(share, earlier)
                for goes, _, slot in moves:
                    if earlier == turn:
                        made.append(
                            remote(
                                held.at[tile, turned(goes), pl.ds(start, size)],
                                chip_came[share * turns + turn].at[tile, slot],
                                chip_sends.at[tile, number],
                                chip_recvs.at[tile, number],
                                fsdp=flip(me, 2 * bit),
                            )
                        )
                    number += 1
        return made

    def span_copies(tile):
        return [
            remote(
                held.at[tile, turned(0), pl.ds(s * own_cols, own_cols)],
                span_came.at[tile, s - 1],
                span_sends.at[tile, s - 1],
                span_recvs.at[tile, s - 1],
                tensor=lax.rem(span + spans - s, spans) * parts + place,
            )
            for s in range(1, spans)
        ]

    @pl.when(step == 0)
    def _():
        load(1 - core)
        partners = [{"fsdp": flip(me, 1)}] + [{"fsdp": flip(me, 2 * bit)} for bit in bits]
        partners += [
            {"tensor": lax.rem(span + s, spans) * parts + place} for s in range(1, spans)
        ]
        side_partners = sides.partners()
        greet(partners + side_partners)

    sides.start_over(step, 2 * tiles, *sides_at)

    @pl.when(step == tiles)
    def _():
        load(core)

    @pl.when(step < tiles)
    def _():
        @pl.when(step >= 2)
        def _():
            core_copy(step - 2).wait_send()

        sent[lax.rem(step, 2)] = tn(x_half[...], grad_ref[...]).astype(LOW)
        core_copy(step).start()

    @pl.when(jnp.logical_and(step >= tiles, step < 2 * tiles))
    def _():
        tile = step - tiles
        total = tn(x_half[...], grad_ref[...])
        core_copy(tile).wait_recv()
        held[tile] = (total + held[tile].astype(F32)).astype(LOW)
        for copy in chip_copies(tile, 0):
            copy.start()

    for turn in range(1, turns + 2):
        tile = step - tiles - turn

        @pl.when(jnp.logical_and(tile >= 0, tile < tiles))
        def _(turn=turn, tile=tile):
            if turn <= turns:
                for copy in chip_copies(tile, turn - 1):
                    copy.wait()
                for share, (start, size) in enumerate(shares):
                    _, moves = swaps(share, turn - 1)
                    for _, stays, slot in moves:
                        where = (tile, turned(stays), pl.ds(start, size))
                        came = chip_came[share * turns + turn - 1][tile, slot]
                        held[where] = (held[where].astype(F32) + came.astype(F32)).astype(LOW)
                for copy in chip_copies(tile, turn) if turn < turns else span_copies(tile):
                    copy.start()
            else:
                total = held[tile, turned(0), :own_cols].astype(F32)
                for s, copy in enumerate(span_copies(tile)):
                    copy.wait()
                    total = total + span_came[tile, s].astype(F32)
                out_ref[...] = total

    @pl.when(step == 2 * tiles + turns)
    def _():
        for last in range(max(0, tiles - 2), tiles):
            core_copy(last).wait_send()
        sides.finish(*sides_at)


def grad_scatter(number, fsdp, parts, spans, x, grads, tiles, earlier=(), sides=NO_SIDES):
    count, width = x.shape
    depth = width // fsdp
    tile = grads.shape[1] // tiles
    own = tile // spans
    turns = fsdp.bit_length() - 2
    shares = column_shares(tile, turns)
    hbm = pl.BlockSpec(memory_space=pl.ANY)
    swapped = turns * (2**turns - 1)
    results = call(
        functools.partial(grad_scatter_kernel, fsdp, parts, spans, tiles, sides),
        [x, grads, *sides.operands],
        [
            pl.BlockSpec((count, width), lambda j: (0, 0)),
            pl.BlockSpec(
                (count, tile),
                lambda j: (0, jnp.where(j < tiles, j, jnp.minimum(j - tiles, tiles - 1))),
            ),
            *[hbm] * len(sides.operands),
        ],
        earlier,
        grid=(2 * tiles + turns + 1,),
        out_specs=[
            pl.BlockSpec((depth, own), lambda j: (0, jnp.maximum(j - (tiles + turns + 1), 0))),
            *[hbm] * len(sides.out_shapes),
        ],
        out_shape=[jax.ShapeDtypeStruct((depth, own * tiles), F32), *sides.out_shapes],
        scratch_shapes=[
            pltpu.VMEM((count, width // 2), LOW),
            pltpu.VMEM((2, width // 2, tile), LOW),
            pltpu.VMEM((tiles, width // 2, tile), LOW),
            pltpu.SemaphoreType.DMA((2,)),
            pltpu.SemaphoreType.DMA((tiles,)),
            pltpu.SemaphoreType.DMA((tiles, swapped)),
            pltpu.SemaphoreType.DMA((tiles, swapped)),
            pltpu.VMEM((tiles, spans - 1, depth, own), LOW),
            pltpu.SemaphoreType.DMA((tiles, spans - 1)),
            pltpu.SemaphoreType.DMA((tiles, spans - 1)),
            *[
                pltpu.VMEM((tiles, 2 ** (turns - 1 - turn), depth, size), LOW)
                for _, size in shares
                for turn in range(turns)
            ],
            *sides.scratch,
        ],
        compiler_params=pltpu.CompilerParams(
            collective_id=number, has_side_effects=True, vmem_limit_bytes=56 * MIB
        ),
        cost_estimate=pl.CostEstimate(
            flops=2 * count * width * tile * tiles,
            bytes_accessed=2 * count * width + 4 * count * tile * tiles,
            transcendentals=0,
        ),
        name="grad_scatter",
    )
    return results[0], *sides.results(results[1:])


def project_kernel(tiles, rows_ref, weight_ref, pre_ref, value_ref, query_sq_ref, key_sq_ref):
    step = pl.program_id(0)
    result = nn(rows_ref[...], weight_ref[...])
    squares = jnp.sum(result * result, axis=1, keepdims=True)

    @pl.when(step < 2 * tiles)
    def _():
        pre_ref[...] = result

    for first, ref in ((0, query_sq_ref), (tiles, key_sq_ref)):

        @pl.when(step == first)
        def _(ref=ref):
            ref[...] = squares

        @pl.when(jnp.logical_and(step > first, step < first + tiles))
        def _(ref=ref):
            ref[...] += squares

    @pl.when(step >= 2 * tiles)
    def _():
        value_ref[...] = result.astype(LOW)


def project(inputs, full):
    rows, depth = inputs.shape
    cols = full.shape[1] // 3
    tile = min(512, cols)
    tiles = cols // tile
    column = pl.BlockSpec((rows, 1), lambda j: (0, 0))
    return pl.pallas_call(
        functools.partial(project_kernel, tiles),
        grid=(3 * tiles,),
        in_specs=[
            pl.BlockSpec((rows, depth), lambda j: (0, 0)),
            pl.BlockSpec((depth, tile), lambda j: (0, j)),
        ],
        out_specs=[
            pl.BlockSpec((rows, tile), lambda j: (0, jnp.minimum(j, 2 * tiles - 1))),
            pl.BlockSpec((rows, tile), lambda j: (0, jnp.maximum(j - 2 * tiles, 0))),
            column,
            column,
        ],
        out_shape=[
            jax.ShapeDtypeStruct((rows, 2 * cols), F32),
            jax.ShapeDtypeStruct((rows, cols), LOW),
            jax.ShapeDtypeStruct((rows, 1), F32),
            jax.ShapeDtypeStruct((rows, 1), F32),
        ],
        compiler_params=pltpu.CompilerParams(vmem_limit_bytes=48 * MIB),
        cost_estimate=pl.CostEstimate(
            flops=6 * rows * depth * cols,
            bytes_accessed=6 * depth * cols + 10 * rows * cols + 2 * rows * depth,
            transcendentals=0,
        ),
        name="project",
    )(inputs, full)


def attention_specs(heads):
    return (
        pl.BlockSpec((SEQ_LEN, HEAD_DIM), lambda i: (0, i)),
        pl.BlockSpec((SEQ_LEN, HEAD_DIM), lambda i: (0, i + heads)),
        pl.BlockSpec((SEQ_LEN, HEAD_DIM), lambda i: (0, 0)),
        pl.BlockSpec((SEQ_LEN, 1), lambda i: (0, 0)),
        pl.BlockSpec((1, HEAD_DIM), lambda i: (0, i)),
        pl.BlockSpec((None, SEQ_LEN, 1), lambda i: (i, 0, 0)),
        pl.BlockSpec(memory_space=pl.ANY),
    )


def attend(number, rows, parts, pre, value, invs, gains, tables, sides):
    width = value.shape[1]
    heads = width // HEAD_DIM
    head, later, whole, column, gain, lse, hbm = attention_specs(heads)
    low = jax.ShapeDtypeStruct((SEQ_LEN, width), LOW)
    results = call(
        functools.partial(attend_kernel, rows, parts, 1.0 / math.sqrt(HEAD_DIM), heads, sides),
        [pre, pre, value, *invs, *gains, *tables, *sides.operands],
        [head, later, head, column, column, gain, gain, whole, whole]
        + [hbm] * len(sides.operands),
        grid=(heads,),
        out_specs=[head, head, head, lse, *[hbm] * len(sides.out_shapes)],
        out_shape=[
            low,
            low,
            low,
            jax.ShapeDtypeStruct((heads, SEQ_LEN, 1), F32),
            *sides.out_shapes,
        ],
        scratch_shapes=[
            pltpu.VMEM((SEQ_LEN, HEAD_DIM), LOW),
            pltpu.VMEM((SEQ_LEN, HEAD_DIM), LOW),
            *sides.scratch,
        ],
        compiler_params=pltpu.CompilerParams(
            vmem_limit_bytes=40 * MIB, **sides.options(number)
        ),
        cost_estimate=pl.CostEstimate(
            flops=8 * heads * SEQ_LEN * SEQ_LEN * HEAD_DIM,
            bytes_accessed=16 * SEQ_LEN * width,
            transcendentals=heads * SEQ_LEN * SEQ_LEN,
        ),
        name="attend",
    )
    return *results[:4], *sides.results(results[4:])


def attend_back(
    number, rows, parts, rots, value, grad, lse_all, pre, invs, gains, tables, earlier, sides
):
    width = value.shape[1]
    heads = width // HEAD_DIM
    head, later, whole, column, gain, lse, hbm = attention_specs(heads)
    low = jax.ShapeDtypeStruct((SEQ_LEN, width), LOW)
    gain_out = jax.ShapeDtypeStruct((1, width), F32)
    inner = jax.ShapeDtypeStruct((SEQ_LEN, 1), F32)
    results = call(
        functools.partial(
            attend_back_kernel, rows, parts, 1.0 / math.sqrt(HEAD_DIM), heads, sides
        ),
        [*rots, value, grad, lse_all, pre, pre, *invs, *gains, *tables, *sides.operands],
        [head, head, head, head, lse, head, later, column, column, gain, gain, whole, whole]
        + [hbm] * len(sides.operands),
        earlier,
        grid=(heads,),
        out_specs=[head, head, head, gain, gain, column, column, *[hbm] * len(sides.out_shapes)],
        out_shape=[low, low, low, gain_out, gain_out, inner, inner, *sides.out_shapes],
        scratch_shapes=[
            pltpu.VMEM((SEQ_LEN, HEAD_DIM), LOW),
            pltpu.VMEM((SEQ_LEN, HEAD_DIM), LOW),
            pltpu.VMEM((SEQ_LEN, HEAD_DIM), F32),
            pltpu.VMEM((SEQ_LEN, HEAD_DIM), F32),
            *sides.scratch,
        ],
        compiler_params=pltpu.CompilerParams(
            vmem_limit_bytes=48 * MIB, **sides.options(number)
        ),
        cost_estimate=pl.CostEstimate(
            flops=20 * heads * SEQ_LEN * SEQ_LEN * HEAD_DIM,
            bytes_accessed=32 * SEQ_LEN * width,
            transcendentals=heads * SEQ_LEN * SEQ_LEN,
        ),
        name="attend_back",
    )
    return *results[:7], *sides.results(results[7:])


def norm_back(grad_hat, values_hat, inverse, width):
    inner = jnp.sum(grad_hat * values_hat, axis=1, keepdims=True) / width
    return inverse * (grad_hat - values_hat * inner)


def layer(fsdp, tensor, *arguments):
    layer_input, query_weight, key_weight, value_weight, out_weight = arguments[:5]
    gate_weight, up_weight, down_weight = arguments[5:8]
    query_gain, key_gain, attn_gain, ffn_gain, out_cotangent = arguments[8:]
    rows_here, width = layer_input.shape
    head_cols = query_weight.shape[1]
    parts = SEQ_LEN // rows_here
    spans = tensor // parts
    rank = lax.axis_index("tensor")
    place, span = rank % parts, rank // parts

    def to_part(x, shift):
        pairs = [
            (s * parts + p, s * parts + (p + shift) % parts)
            for s in range(spans)
            for p in range(parts)
        ]
        return lax.ppermute(x, "tensor", pairs)

    def to_span(x, shift):
        pairs = [
            (s * parts + p, (s + shift) % spans * parts + p)
            for s in range(spans)
            for p in range(parts)
        ]
        return lax.ppermute(x, "tensor", pairs)

    def gather_shard(shard):
        return lax.all_gather(shard, "fsdp", axis=0, tiled=True)

    def add_pieces(total, came):
        for piece in came:
            total = total + piece.astype(F32)
        return total

    def sum_parts(x):
        total = x
        for p in range(1, parts):
            total = total + jnp.roll(to_part(x, p), p * rows_here, axis=0)
        return total

    same_core = [list(range(c, fsdp, 2)) for c in range(2)]

    def scatter(total):
        return lax.psum_scatter(
            total, "fsdp", scatter_dimension=0, tiled=True, axis_index_groups=same_core
        )

    def own_columns(s):
        return ((span + spans - s) % spans * parts + place) * head_cols

    def gain_here(gain):
        return jnp.concatenate(
            [lax.dynamic_slice_in_dim(gain, own_columns(s), head_cols) for s in range(spans)]
        )[None, :]

    def gain_whole(part):
        whole = jnp.zeros((width,), F32)
        for s in range(spans):
            whole = lax.dynamic_update_slice_in_dim(
                whole, part[0, s * head_cols : (s + 1) * head_cols], own_columns(s), 0
            )
        return whole

    gate_up_shard = jnp.concatenate([gate_weight, up_weight], axis=1)
    down_shard = down_weight.T
    out_shard = out_weight.T
    cols = gate_weight.shape[1]
    shards, plan = [], []
    for s in range(spans):
        for w, shard in enumerate([query_weight, key_weight, value_weight, out_shard]):
            shards.append(shard)
            plan.append((w // 3, s, w % 3 * spans + s, False))
    (full_qkv, full_out), (down_came,), inputs = exchange(
        0,
        fsdp,
        parts,
        spans,
        shards,
        plan,
        sides=Sides(Rows(parts, gather=layer_input)),
        sends=[down_shard],
    )
    gate_up_first = gather_shard(after(gate_up_shard, inputs))

    local = jnp.arange(SEQ_LEN)
    position = (place + parts - local // rows_here) % parts * rows_here + local % rows_here
    inverse = THETA ** (-jnp.arange(0, HEAD_DIM, 2).astype(F32) / HEAD_DIM)
    angles = position.astype(F32)[:, None] * inverse[None, :]
    cos, sin = jnp.cos(angles), jnp.sin(angles)
    tables = (jnp.concatenate([cos, cos], axis=1), jnp.concatenate([-sin, sin], axis=1))
    gains = (gain_here(query_gain), gain_here(key_gain))

    pre, value_low, query_sq, key_sq = project(inputs, full_qkv)
    squares = sum_parts(jnp.concatenate([query_sq, key_sq], axis=1))
    invs = lax.rsqrt(squares / width + EPSILON)
    invs = (invs[:, :1], invs[:, 1:])
    others_spans = range(1, spans)
    sides = Sides(Spans(parts, spans, [(gate_up_shard, 0, cols, spans - s) for s in others_spans]))
    attended, query_rot, key_rot, lse, gate_came = attend(
        13, rows_here, parts, pre, value_low, invs, gains, tables, sides
    )
    branch, low = product_sum(parts, [(attended, 0, full_out, 0, full_out.shape[1])])
    down_shards = jnp.concatenate([down_shard, *[down_came[s - 1] for s in others_spans]], axis=1)
    gate_up_first, low, down_shards = lax.optimization_barrier((gate_up_first, low, down_shards))
    full_down = gather_shard(down_shards)
    sides = Sides(
        Rows(parts, deliver=low),
        Spans(parts, spans, [(gate_up_shard, 1, cols, spans - s) for s in others_spans]),
    )
    full_gate, _, came, up_came = exchange(
        1, fsdp, parts, spans, gate_came, [(s - 1, s, 0, True) for s in others_spans], sides=sides
    )
    branch = add_pieces(branch, came)
    branch_inv = lax.rsqrt(jnp.mean(branch * branch, axis=1, keepdims=True) + EPSILON)
    branch_hat = branch * branch_inv
    middle = layer_input.astype(F32) + branch_hat * attn_gain
    half = rows_here // 2
    halves = [slice(0, half), slice(half, rows_here)]
    middle_low = [middle[h].astype(LOW) for h in halves]
    grad_out = out_cotangent.astype(F32)
    full_up, _, *mixed = exchange(
        2,
        fsdp,
        parts,
        spans,
        up_came,
        [(s - 1, s, 0, True) for s in others_spans],
        sides=Sides(*[Rows(parts, gather=rows) for rows in middle_low]),
    )
    full_gate_up = [((gate_up_first, 0), (gate_up_first, 1))]
    full_gate_up += [((gate, 0), (up, 0)) for gate, up in zip(full_gate, full_up)]
    gates, uppers, hiddens = [None] * 2, [None] * 2, [None] * 2
    back, outputs, ffn_gain_parts, grad_middles, attn_gain_parts = [None] * 2, [], [], [], []

    def down_pairs(c):
        return [(hiddens[c], s, full_down, s, cols) for s in range(spans)]

    def up_pairs(c):
        return [
            (grad, s, array, run, cols)
            for s in range(spans)
            for grad, (array, run) in zip(back[c], full_gate_up[s])
        ]

    def turn(c, total, came):
        second = add_pieces(total, came)
        second_inv = lax.rsqrt(jnp.mean(second * second, axis=1, keepdims=True) + EPSILON)
        second_hat = second * second_inv
        outputs.append((middle[halves[c]] + second_hat * ffn_gain).astype(LOW))
        grad = grad_out[halves[c]]
        ffn_gain_parts.append(jnp.sum(grad * second_hat, axis=0))
        return norm_back(grad * ffn_gain, second_hat, second_inv, width).astype(LOW)

    part_cols = cols // 2

    def to_spans(array, run, width):
        each = array.shape[1] // spans // width
        return Spans(parts, spans, [(array, s * each + run, width, s) for s in others_spans])

    def back_to_branch(c, total, came):
        grad_middle = grad_out[halves[c]] + add_pieces(total, came)
        hat = branch_hat[halves[c]]
        grad_middles.append(grad_middle)
        attn_gain_parts.append(jnp.sum(grad_middle * hat, axis=0))
        return norm_back(grad_middle * attn_gain, hat, branch_inv[halves[c]], width).astype(LOW)

    gates[0], uppers[0], hiddens[0] = feed_up(mixed[0], full_gate_up, cols)
    second_first, low = product_sum(parts, down_pairs(0))
    gates[1], uppers[1], hiddens[1], came = feed_up(
        mixed[1], full_gate_up, cols, 4, Sides(Rows(parts, deliver=low))
    )
    grad_second = turn(0, second_first, came)
    second_last, low, grad_rows_first = product_sum(
        parts, down_pairs(1), [], 5, Sides(Rows(parts, gather=grad_second))
    )
    *back[0], came = feed_up_back(
        grad_rows_first, full_down, gates[0], uppers[0], [], 6, Sides(Rows(parts, deliver=low))
    )
    grad_second = turn(1, second_last, came)
    mixed_grad_first, low, grad_rows_last = product_sum(
        parts, up_pairs(0), [], 7, Sides(Rows(parts, gather=grad_second))
    )
    grad_rows = [grad_rows_first, grad_rows_last]
    now, came = weight_grad_half(
        8,
        fsdp,
        grad_rows,
        [(hiddens, 0, spans * cols)],
        sides=Sides(Rows(parts, deliver=low)),
    )
    down_terms = scatter(now)
    grad_branch = back_to_branch(0, mixed_grad_first, came)
    back[1] = feed_up_back(grad_rows_last, full_down, gates[1], uppers[1], [now])
    mixed_grad_last, low, branch_first = product_sum(
        parts, up_pairs(1), [], 9, Sides(Rows(parts, gather=grad_branch))
    )
    backs = list(zip(*back))
    gate_up_grad = {}
    for s in reversed(range(spans)):
        entries = [(list(arrays), s * cols, cols) for arrays in backs]
        if s == spans - 1:
            jobs = [Rows(parts, deliver=low)]
        elif s:
            jobs = []
        else:
            jobs = [Rows(parts, gather=grad_branch), to_spans(down_terms, 0, part_cols)]
        now, *results = weight_grad_half(10 + s, fsdp, mixed, entries, [now], Sides(*jobs))
        if s:
            gate_up_grad[s] = scatter(now)
        if s == spans - 1:
            grad_branch = back_to_branch(1, mixed_grad_last, results[0])
    branch_last, down_came_first = results
    output = jnp.concatenate(outputs, axis=0)
    ffn_gain_part, attn_gain_part = sum(ffn_gain_parts), sum(attn_gain_parts)
    grad_middle = jnp.concatenate(grad_middles, axis=0)
    grad_branch_rows = jnp.concatenate(
        [
            piece[p * half : (p + 1) * half]
            for p in range(parts)
            for piece in (branch_first, branch_last)
        ],
        axis=0,
    )
    grad_attended = nn(grad_branch_rows, full_out).astype(LOW)
    out_total, down_came_last = weight_grad_half(
        30,
        fsdp,
        [grad_branch_rows],
        [([attended], 0, attended.shape[1])],
        [grad_attended],
        Sides(to_spans(down_terms, 1, part_cols)),
    )
    *away, out_total = lax.optimization_barrier(
        (*[gate_up_grad[s] for s in others_spans], out_total)
    )
    gate_up_grad.update(zip(others_spans, away))
    out_terms = scatter(out_total)
    (
        query_gained,
        key_gained,
        grad_value,
        query_gain_part,
        key_gain_part,
        query_inner,
        key_inner,
        gate_came,
    ) = attend_back(
        12,
        rows_here,
        parts,
        (query_rot, key_rot),
        value_low,
        grad_attended,
        lse,
        pre,
        invs,
        gains,
        tables,
        [out_total],
        Sides(Spans(parts, spans, [(gate_up_grad[s], 0, cols, s) for s in others_spans])),
    )
    out_terms, now, grad_value = lax.optimization_barrier((out_terms, now, grad_value))
    gate_up_grad[0] = scatter(now)
    down_came = [jnp.concatenate(pair, axis=1) for pair in zip(down_came_first, down_came_last)]
    down_grad = add_pieces(down_terms[:, :cols].astype(F32), down_came)
    inners = sum_parts(jnp.concatenate([query_inner, key_inner], axis=1)) / width
    local_width = value_low.shape[1]
    grad_query = invs[0] * (query_gained - pre[:, :local_width] * invs[0] * inners[:, :1])
    grad_key = invs[1] * (key_gained - pre[:, local_width:] * invs[1] * inners[:, 1:])
    grad_qkv = jnp.concatenate(
        [grad_query.astype(LOW), grad_key.astype(LOW), grad_value], axis=1
    )
    quarter = cols // 4
    sides = Sides(Spans(parts, spans, [(gate_up_grad[s], 4, quarter, s) for s in others_spans]))
    total, low, up_came_first = product_sum(
        parts,
        [(grad_qkv, 0, full_qkv, 0, full_qkv.shape[1])],
        [],
        32,
        sides,
        grad_middle,
    )
    gain_parts = [gain_whole(query_gain_part), gain_whole(key_gain_part)]
    sides = Sides(
        SumAll(fsdp, tensor, jnp.stack([*gain_parts, attn_gain_part, ffn_gain_part])),
        Rows(parts, deliver=low),
        Spans(parts, spans, [(out_terms, s, head_cols, s) for s in others_spans]),
        Spans(
            parts,
            spans,
            [(gate_up_grad[s], run, quarter, s) for run in range(5, 8) for s in others_spans],
        ),
    )
    qkv_grad, gain_grads, came, out_came, up_came_last = grad_scatter(
        31, fsdp, parts, spans, inputs, grad_qkv, 3, [], sides
    )
    input_grad = add_pieces(total, came)
    out_grad = add_pieces(out_terms[:, :head_cols].astype(F32), out_came)
    up_came = [
        jnp.concatenate([first, *up_came_last[s :: spans - 1]], axis=1)
        for s, first in enumerate(up_came_first)
    ]
    gate_grad = add_pieces(gate_up_grad[0][:, :cols].astype(F32), gate_came)
    up_grad = add_pieces(gate_up_grad[0][:, cols:].astype(F32), up_came)
    query_grad, key_grad, value_grad = jnp.split(qkv_grad, 3, axis=1)
    return (
        output,
        input_grad,
        query_grad,
        key_grad,
        value_grad,
        out_grad.T,
        gate_grad,
        up_grad,
        down_grad.T,
        *gain_grads,
    )


def solution(mesh):
    columns, rows = P("fsdp", "tensor"), P("tensor", "fsdp")
    tokens = P(("fsdp", "tensor"), None)
    weights = (columns, columns, columns, rows, columns, columns, rows)
    return jax.shard_map(
        functools.partial(layer, mesh.shape["fsdp"], mesh.shape["tensor"]),
        mesh=mesh,
        in_specs=(tokens, *weights, P(), P(), P(), P(), tokens),
        out_specs=(tokens, tokens, *weights, P(), P(), P(), P()),
        check_vma=False,
    )
```
